512 devices in a mesh: sec: 2 (over z_hi), gx: 32 (over x, y), gy: 8 (over z_lo, core).
Axes of the slice: x: 4, y: 8, z: 8 (z_hi: 2, z_lo: 4; z = z_hi * 4 + z_lo), core: 2. Of those that a mesh axis runs over, the one named last changes fastest.
Arguments:
- section_state: float32 [2, 8, 512, 2048], P('sec', None, 'gx', 'gy'), may hold values from -6 to 6
- prev_import: float32 [2, 8, 512, 2048], P('sec', None, 'gx', 'gy'), may hold values from -6 to 6
- land_mask: int32 [2, 512, 2048], P('sec', 'gx', 'gy'), may hold values 0 or 1
- state_mix: float32 [2, 8, 8], P('sec'), may hold values from -1.5 to 1.5
- import_mix: float32 [2, 8, 8], P('sec'), may hold values from -1.5 to 1.5
- damping: float32 [2, 8], P('sec'), may hold values from 0.015 to 0.3
- wave_speed: float32 [2, 2], P('sec'), may hold values from 0.95 to 1
- remap_owner: int32 [2, 512, 32, 2], P('sec', 'gx', 'gy'), may hold values from 0 to 31, as said below
- remap_slot: int32 [2, 512, 32, 2], P('sec', 'gx', 'gy'), may hold values from 0 to 63
- remap_weight: bfloat16 [2, 512, 32, 64, 128], P('sec', 'gx', 'gy'), may hold values from 0 to 1, as said below
Outputs:
- final_state: float32 [2, 8, 512, 2048], P('sec', None, 'gx', 'gy')
- final_import: float32 [2, 8, 512, 2048], P('sec', None, 'gx', 'gy')
The draws below stay inside these ranges and needn't reach their ends.
Inputs may be any that keep to these rules, and one draw needn't show every extreme that they name: `remap_owner`: the source tile lies in the same gy column of the other section and within 2 tiles of the destination block's own gx tile index. `remap_weight`: every destination cell has a positive weight on some cell of each of its source blocks.
All inputs are finite; a program needn't handle non-finite values. No bound on the sum of `land_mask` on one device may be relied on, other than what follows from the above.
Results may differ from the reference program's by a relative error of at most 0.0018.
Values may be sent and summed in bfloat16 or wider, within the bound.
No kernel may reach another device: no remote copies, remote signals or barrier semaphores. Data moves between devices by JAX's collectives and lax.ppermute only.
A program may use at most 64 MiB of HBM per device.

```python
import math
import jax
import jax.numpy as jnp
from jax import lax

FIELDS = 8
BLOCK = 64
NNZ = 2
TX = 16
TY = 256
SUBSTEPS = 16
ITERS = 2
NX = 512
NY = 2048


def draw_remap_owner(key, part):
    key = jax.random.fold_in(key, 11)
    shape = (2, NX, NY // BLOCK, NNZ)
    offsets = jax.random.randint(key, shape, -2, 3)
    row_index = jnp.arange(NX, dtype=jnp.int32)[None, :, None, None]
    segment_index = jnp.arange(NY // BLOCK, dtype=jnp.int32)[None, None, :, None]
    slot_index = jnp.arange(NNZ, dtype=jnp.int32)[None, None, None, :]
    leading = (row_index % TX == 0) & (segment_index % (TY // BLOCK) == 0)
    offsets = jnp.where(leading & (slot_index == 0), -2, offsets)
    offsets = jnp.where(leading & (slot_index == 1), 2, offsets)
    owner = jnp.clip(row_index // TX + offsets, 0, NX // TX - 1)
    return owner.astype(jnp.int32)


def draw_remap_weight(key, part):
    key = jax.random.fold_in(key, 23)
    shape = (2, NX, NY // BLOCK, BLOCK, NNZ * BLOCK)
    uniform_part = jax.random.uniform(key, shape, jnp.float32)
    values = jnp.exp(jnp.log(0.05) * (1.0 - uniform_part))
    target = jnp.arange(BLOCK, dtype=jnp.int32)[:, None]
    source = jnp.arange(NNZ * BLOCK, dtype=jnp.int32)[None, :] % BLOCK
    band = (jnp.abs(source - target) <= 4).astype(jnp.float32)
    return (values * band).astype(jnp.bfloat16)


def smooth_part(phase_key, level):
    phases = jax.random.uniform(phase_key, (2, 3, 2), jnp.float32, 0.0, 2.0 * math.pi)
    rows = ((jnp.arange(NX, dtype=jnp.float32) + 0.5) / NX)[None, :, None]
    cols = ((jnp.arange(NY, dtype=jnp.float32) + 0.5) / NY)[None, None, :]
    turn = 2.0 * math.pi
    height = level + 0.8 * jnp.cos(turn * rows + phases[:, 0, 0][:, None, None]) * jnp.cos(turn * cols + phases[:, 0, 1][:, None, None])
    east_flow = jnp.sin(turn * rows + phases[:, 1, 0][:, None, None]) + 0.0 * cols
    north_flow = jnp.sin(turn * cols + phases[:, 2, 1][:, None, None]) + 0.0 * rows
    waves = jnp.stack([height, east_flow, north_flow], axis=1)
    tracers = jnp.zeros((2, FIELDS - 3, NX, NY), jnp.float32)
    return jnp.concatenate([waves, tracers], axis=1)


def draw_section_state(key, part):
    key = jax.random.fold_in(key, 37)
    noise_key, phase_key = jax.random.split(key, 2)
    shape = (2, FIELDS, NX, NY)
    rough = jnp.clip(jax.random.normal(noise_key, shape, jnp.float32), -3.5, 3.5)
    smooth = smooth_part(phase_key, 2.5)
    return jnp.clip(rough + smooth, -6.0, 6.0).astype(jnp.float32)


def draw_damping(key, part):
    key = jax.random.fold_in(key, 41)
    fast_key, slow_key = jax.random.split(key, 2)
    fast = jnp.exp(jnp.log(0.015) + (jnp.log(0.03) - jnp.log(0.015)) * jax.random.uniform(fast_key, (2, 3), jnp.float32))
    slow = jnp.exp(jnp.log(0.02) + (jnp.log(0.3) - jnp.log(0.02)) * jax.random.uniform(slow_key, (2, FIELDS - 3), jnp.float32))
    return jnp.concatenate([fast, slow], axis=1).astype(jnp.float32)


def place_ends(values, own_key, smallest, high):
    place = [jax.random.randint(jax.random.fold_in(own_key, axis), (), 0, length) for axis, length in enumerate(values.shape)]
    widest = values.shape.index(max(values.shape))
    beside = place[:widest] + [(place[widest] + 1) % values.shape[widest]] + place[widest + 1:]
    return values.at[tuple(place)].set(smallest).at[tuple(beside)].set(high)


def levels(key, shape, cuts, low, largest):
    level = 1.0
    for axis_at, blocks in cuts:
        steps = jax.random.uniform(jax.random.fold_in(jax.random.fold_in(key, 6), axis_at), (blocks,), jnp.float32, low / len(cuts), largest / len(cuts))
        level = level * jnp.repeat(jnp.exp(steps), shape[axis_at] // blocks).reshape((-1,) + (1,) * (len(shape) - 1 - axis_at))
    return level


def bell_draw(own_key, shape, spread, bound, cuts=(), held_as=jnp.bfloat16):
    entries = spread * jax.random.normal(own_key, shape, jnp.float32)
    if cuts:
        entries = entries * levels(own_key, shape, cuts, -0.22, 0.18)
    return jnp.clip(entries, -bound, bound).astype(held_as)


def setup_inputs(seed: int = 0) -> dict:
    arg_keys = jax.random.split(jax.random.key(seed), 11)
    return {
        "section_state": draw_section_state(jax.random.fold_in(arg_keys[10], 71), 0),
        "prev_import": bell_draw(arg_keys[1], (2, FIELDS, NX, NY), 1.0, 6.0, ((0, 2), (2, 32), (3, 8)), jnp.float32),
        "land_mask": place_ends((jax.random.randint(arg_keys[2], (2, NX, NY), 0, 4) < 3).astype(jnp.int32), jax.random.fold_in(arg_keys[2], 1), 0, 1),
        "state_mix": bell_draw(arg_keys[3], (2, FIELDS, FIELDS), (2 * FIELDS) ** -0.5, 1.5, ((0, 2),), jnp.float32),
        "import_mix": bell_draw(arg_keys[4], (2, FIELDS, FIELDS), (2 * FIELDS) ** -0.5, 1.5, ((0, 2),), jnp.float32),
        "damping": draw_damping(jax.random.fold_in(arg_keys[10], 71), 0),
        "wave_speed": jnp.clip(0.95 + 0.050000012 * jax.random.uniform(arg_keys[6], (2, 2), jnp.float32) ** levels(arg_keys[6], (2, 2), ((0, 2),), -0.2, 0.2), 0.95, 1.0),
        "remap_owner": draw_remap_owner(jax.random.fold_in(arg_keys[10], 71), 0),
        "remap_slot": place_ends(jax.random.randint(arg_keys[8], (2, NX, NY // BLOCK, NNZ), 0, TX * TY // BLOCK), jax.random.fold_in(arg_keys[8], 1), 0, (TX * TY // BLOCK) - 1).astype(jnp.int32),
        "remap_weight": draw_remap_weight(jax.random.fold_in(arg_keys[10], 71), 0),
    }


DIFFUSION = 0.1
COUPLING = 0.2

def shifted(field, step_x, step_y):
    padded = jnp.pad(field, ((0, 0), (1, 1), (1, 1)))
    size_x = field.shape[1]
    size_y = field.shape[2]
    return padded[:, 1 + step_x:1 + step_x + size_x, 1 + step_y:1 + step_y + size_y]

def substep(fields, forcing, damping_rates, wave_terms):
    height = fields[0:1]
    east_flow = fields[1:2]
    north_flow = fields[2:3]
    tracers = fields[3:]
    diff_u = 0.5 * (shifted(east_flow, 1, 0) - shifted(east_flow, -1, 0))
    diff_v = 0.5 * (shifted(north_flow, 0, 1) - shifted(north_flow, 0, -1))
    new_height = (1.0 - damping_rates[0]) * height - wave_terms[0] * (diff_u + diff_v) + forcing[0:1]
    grad_x = 0.5 * (shifted(new_height, 1, 0) - shifted(new_height, -1, 0))
    grad_y = 0.5 * (shifted(new_height, 0, 1) - shifted(new_height, 0, -1))
    new_east = (1.0 - damping_rates[1]) * east_flow - wave_terms[1] * grad_x + forcing[1:2]
    new_north = (1.0 - damping_rates[2]) * north_flow - wave_terms[1] * grad_y + forcing[2:3]
    laplacian = shifted(tracers, 1, 0) + shifted(tracers, -1, 0) + shifted(tracers, 0, 1) + shifted(tracers, 0, -1) - 4.0 * tracers
    new_tracers = (1.0 - damping_rates[3:, None, None]) * tracers + DIFFUSION * laplacian + forcing[3:]
    return jnp.concatenate([new_height, new_east, new_north, new_tracers], axis=0)

def remap_blocks(source, owner, slot, weight):
    tile_segments = TY // BLOCK
    grid_segments = NY // BLOCK
    blocks = source.reshape(FIELDS, NX, grid_segments, BLOCK)
    segment = jnp.arange(grid_segments, dtype=jnp.int32)[None, :, None]
    source_row = (owner * TX + slot // tile_segments).astype(jnp.int32)
    source_segment = (segment // tile_segments * tile_segments + slot % tile_segments).astype(jnp.int32)
    picked = blocks[:, source_row, source_segment, :]
    picked = picked.reshape(FIELDS, NX, grid_segments, NNZ * BLOCK)
    weighted = jnp.einsum('xgcj,fxgj->fxgc', weight.astype(jnp.float32), picked.astype(jnp.float32))
    weight_total = lax.optimization_barrier(jnp.sum(weight.astype(jnp.float32), axis=-1))
    return (weighted / weight_total[None]).reshape(FIELDS, NX, NY)

def export_fields(fields, received, wet_cells, mix_state, mix_import):
    mixture = jnp.einsum('ck,kxy->cxy', mix_state, fields, precision=lax.Precision.HIGHEST)
    mixture = mixture + jnp.einsum('ck,kxy->cxy', mix_import, received, precision=lax.Precision.HIGHEST)
    wind_speed = jnp.sqrt(1.0 + fields[1] * fields[1] + fields[2] * fields[2])
    return (wet_cells * wind_speed * mixture).astype(jnp.bfloat16)

def reference(section_state, prev_import, land_mask, state_mix, import_mix, damping, wave_speed, remap_owner, remap_slot, remap_weight):
    wet_cells = land_mask.astype(jnp.float32)
    states = [section_state[0], section_state[1]]
    imports = [prev_import[0], prev_import[1]]
    for interval in range(ITERS):
        exports = [export_fields(states[section], imports[section], wet_cells[section], state_mix[section], import_mix[section]) for section in range(2)]
        imports = [remap_blocks(exports[1 - section], remap_owner[section], remap_slot[section], remap_weight[section]) for section in range(2)]
        for section in range(2):
            forcing = COUPLING * wet_cells[section][None] * imports[section]
            rates = damping[section]
            terms = wave_speed[section]

            def advance(counter, current):
                return substep(current, forcing, rates, terms)
            states[section] = lax.fori_loop(0, SUBSTEPS, advance, states[section])
    return (jnp.stack(states, axis=0), jnp.stack(imports, axis=0))
```

```python
import jax
import jax.numpy as jnp
from jax import lax
from jax.experimental import pallas as pl
from jax.experimental.pallas import tpu as pltpu
from jax.sharding import PartitionSpec as P

SUBSTEPS = 16
ITERS = 2
DIFFUSION = 0.1
COUPLING = 0.2

FIELDS = 8
ROWS = 16
COLS = 256
LANES = 128
HALO = 2 * SUBSTEPS
WIDE = 3 * LANES
STEPS_PER_PHASE = 4

TRACER_MAIN = 0
STRIPS = 20
STRIP_PLANES = 5
WAVE_MAIN = 30
PLANES = 42
FAR_FROM = 23

SMEM = pl.BlockSpec(memory_space=pltpu.SMEM)
VMEM = pl.BlockSpec(memory_space=pltpu.VMEM)
PARAMS = pltpu.CompilerParams(vmem_limit_bytes=32 * 1024 * 1024)

f32 = jnp.float32


def write_export(fields, received, wet, smix_ref, imix_ref, turned, out_ref):
    speed = jnp.sqrt(1.0 + fields[1] * fields[1] + fields[2] * fields[2])
    scale = wet * speed
    for c in range(FIELDS):
        total = smix_ref[c, 0] * fields[0]
        for k in range(1, FIELDS):
            total = total + smix_ref[c, k] * fields[k]
        other = imix_ref[c, 0] * received[0]
        for k in range(1, FIELDS):
            other = other + imix_ref[c, k] * received[k]
        value = scale * (total + other)
        for half in range(2):
            turned[half, pl.ds(c, ROWS, stride=FIELDS), :] = value[:, half * LANES : (half + 1) * LANES]
    for half in range(2):
        out_ref[:, half * LANES : (half + 1) * LANES] = turned[half].astype(jnp.bfloat16)


def export_kernel(smix_ref, imix_ref, fields_ref, received_ref, land_ref, out_ref, turned):
    fields = [fields_ref[c] for c in range(FIELDS)]
    received = [received_ref[c] for c in range(FIELDS)]
    write_export(fields, received, land_ref[...].astype(f32), smix_ref, imix_ref, turned, out_ref)


def export(fields, received, land, smix, imix):
    return pl.pallas_call(
        export_kernel,
        out_shape=jax.ShapeDtypeStruct((ROWS * FIELDS, COLS), jnp.bfloat16),
        in_specs=[SMEM, SMEM, VMEM, VMEM, VMEM],
        out_specs=VMEM,
        scratch_shapes=[pltpu.VMEM((2, ROWS * FIELDS, LANES), f32)],
        compiler_params=PARAMS,
        name="export",
    )(smix, imix, fields, received, land)


def packed(planes, lane, first):
    out = jnp.zeros((ROWS, LANES), f32)
    for j, plane in enumerate(planes):
        shift = (32 * j) if first else (32 * j + 32) % LANES
        moved = pltpu.roll(plane, shift, 1) if shift else plane
        out = jnp.where((lane >= 32 * j) & (lane < 32 * j + 32), moved, out)
    return out


def remap_kernel(
    index_ref, near_ref, far_ref, left_ref, right_ref, weight_ref, fields_ref, land_ref,
    payload_ref, low_ref, high_ref, import_ref, table, turned,
):
    windows = [
        (near_ref, 0), (left_ref, 0), (near_ref, ROWS * FIELDS), (right_ref, 0), (far_ref, 0),
    ]
    half_count = 5 * ROWS * 2
    for w, (ref, start) in enumerate(windows):
        for pair in range(ROWS // 2):
            chunk = ref[start + pair * 16 : start + pair * 16 + 16, :].astype(f32)
            for sub in range(2):
                for half in range(2):
                    part = chunk[sub * 8 : sub * 8 + 8, half * LANES : (half + 1) * LANES]
                    at = (w * ROWS + pair * 2 + sub) * 2 + half
                    table[at] = part
                    table[half_count + at] = pltpu.roll(part, 64, 1)
    lane8 = lax.broadcasted_iota(jnp.int32, (8, LANES), 1)
    low_half = lane8 < 64
    ones = jnp.ones((8, LANES), f32)
    for x in range(ROWS):
        pieces = []
        for seg in range(4):
            at = (x * 4 + seg) * 2
            pieces.append(jnp.where(low_half, table[index_ref[at]], table[index_ref[at + 1]]))
        picked = jnp.concatenate(pieces + [ones], axis=0).astype(jnp.bfloat16)
        product = lax.dot_general(
            picked, weight_ref[x], (((1,), (1,)), ((), ())), preferred_element_type=f32
        )
        for half in range(2):
            cols = product[:, half * LANES : (half + 1) * LANES]
            summed = jnp.where(low_half, cols[16 * half : 16 * half + 8], cols[16 * half + 8 : 16 * half + 16])
            turned[half, x * 8 : x * 8 + 8, :] = summed / cols[32:40]
    lane = lax.broadcasted_iota(jnp.int32, (ROWS, LANES), 1)
    wet = land_ref[...].astype(f32)
    state = []
    forcing = []
    for c in range(FIELDS):
        state.append([fields_ref[c, :, h * LANES : (h + 1) * LANES] for h in range(2)])
        parts = []
        for half in range(2):
            value = turned[half, pl.ds(c, ROWS, stride=FIELDS), :]
            import_ref[c, :, half * LANES : (half + 1) * LANES] = value
            parts.append(COUPLING * wet[:, half * LANES : (half + 1) * LANES] * value)
        forcing.append(parts)
    waves = state[:3] + forcing[:3]
    tracers = state[3:] + forcing[3:]
    for i, pair in enumerate(tracers):
        for half in range(2):
            payload_ref[TRACER_MAIN + 2 * i + half] = pair[half]
    for i, pair in enumerate(waves):
        for half in range(2):
            payload_ref[WAVE_MAIN + 2 * i + half] = pair[half]
    for p in range(2 * STRIP_PLANES):
        payload_ref[STRIPS + p] = jnp.zeros((ROWS, LANES), f32)
    groups = [tracers[0:4], tracers[4:8], tracers[8:10], waves[0:4], waves[4:6]]
    for p, group in enumerate(groups):
        low_ref[p] = packed([pair[0] for pair in group], lane, True)
        high_ref[p] = packed([pair[1] for pair in group], lane, False)


def remap(index, near, far, left, right, weight, fields, land):
    return pl.pallas_call(
        remap_kernel,
        out_shape=(
            jax.ShapeDtypeStruct((PLANES, ROWS, LANES), f32),
            jax.ShapeDtypeStruct((STRIP_PLANES, ROWS, LANES), f32),
            jax.ShapeDtypeStruct((STRIP_PLANES, ROWS, LANES), f32),
            jax.ShapeDtypeStruct((FIELDS, ROWS, COLS), f32),
        ),
        in_specs=[SMEM] + [VMEM] * 7,
        out_specs=(VMEM,) * 4,
        scratch_shapes=[
            pltpu.VMEM((2 * 5 * ROWS * 2, FIELDS, LANES), f32),
            pltpu.VMEM((2, ROWS * FIELDS, LANES), f32),
        ],
        compiler_params=PARAMS,
        name="remap",
    )(index, near, far, left, right, weight, fields, land)


def up(value):
    return pltpu.roll(value, value.shape[0] - 1, 0)


def down(value):
    return pltpu.roll(value, 1, 0)


def east(value):
    return pltpu.roll(value, WIDE - 1, 1)


def west(value):
    return pltpu.roll(value, 1, 1)


def substep_kernel(last, place_ref, damping_ref, wave_ref, smix_ref, imix_ref, *refs):
    tiles = refs[:5]
    if last:
        state_ref, *scratch = refs[5:]
    else:
        received_ref, land_ref, state_ref, export_ref, *scratch = refs[5:]
    waves, wave_forcing, tracers, tracer_forcing, coef, turned = scratch
    lane = lax.broadcasted_iota(jnp.int32, (ROWS, LANES), 1)

    def strip(ref, base, group, j):
        left = ref[STRIPS - base + group]
        right = ref[STRIPS - base + STRIP_PLANES + group]
        if j:
            right = pltpu.roll(right, LANES - 32 * j, 1)
        if j != 3:
            left = pltpu.roll(left, 96 - 32 * j, 1)
        return jnp.where(lane < 32, right, jnp.where(lane >= 96, left, 0.0))

    for t, ref in enumerate(tiles):
        base = FAR_FROM if t in (0, 4) else 0
        for i in range(6):
            dest = waves if i < 3 else wave_forcing
            rows = slice(t * ROWS, (t + 1) * ROWS)
            for half in range(2):
                dest[i % 3, rows, half * LANES : (half + 1) * LANES] = ref[WAVE_MAIN - base + 2 * i + half]
            dest[i % 3, rows, 2 * LANES :] = strip(ref, base, 3 + i // 4, i % 4)
        if t in (0, 4):
            continue
        for i in range(10):
            dest = tracers if i < 5 else tracer_forcing
            rows = slice((t - 1) * ROWS, t * ROWS)
            for half in range(2):
                dest[i % 5, rows, half * LANES : (half + 1) * LANES] = ref[TRACER_MAIN + 2 * i + half]
            dest[i % 5, rows, 2 * LANES :] = strip(ref, base, i // 4, i % 4)

    height = 5 * ROWS
    row = lax.broadcasted_iota(jnp.int32, (height, WIDE), 0) + (place_ref[0] * ROWS - HALO)
    col = lax.broadcasted_iota(jnp.int32, (height, WIDE), 1)
    col = jnp.where(col >= WIDE - HALO, col - WIDE, col) + place_ref[1] * COLS
    ok = (row >= 0) & (row < place_ref[2]) & (col >= 0) & (col < place_ref[3])
    inside = jnp.where(ok, 1.0, 0.0)
    coef[0] = inside * (0.5 * wave_ref[0])
    coef[1] = inside * (0.5 * wave_ref[1])
    coef[2] = inside * DIFFUSION

    keep = [1.0 - damping_ref[c] for c in range(FIELDS)]
    for phase in range(SUBSTEPS // STEPS_PER_PHASE):
        reach = (SUBSTEPS - phase * STEPS_PER_PHASE) * 2
        rows = slice(HALO - reach, HALO + ROWS + reach)
        spread = 16 if phase < 2 else 8
        trows = slice(ROWS - spread, 2 * ROWS + spread)
        crows = slice(HALO - spread, HALO + ROWS + spread)

        def one_step(_, carry, rows=rows, trows=trows, crows=crows):
            h = waves[0, rows]
            u = waves[1, rows]
            v = waves[2, rows]
            spread_u = up(u) - down(u)
            spread_v = east(v) - west(v)
            h = keep[0] * h - coef[0, rows] * (spread_u + spread_v) + wave_forcing[0, rows]
            waves[0, rows] = h
            waves[1, rows] = keep[1] * u - coef[1, rows] * (up(h) - down(h)) + wave_forcing[1, rows]
            waves[2, rows] = keep[2] * v - coef[1, rows] * (east(h) - west(h)) + wave_forcing[2, rows]
            for c in range(5):
                a = tracers[c, trows]
                around = (up(a) + down(a)) + (east(a) + west(a))
                tracers[c, trows] = (
                    (keep[3 + c] - 4.0 * DIFFUSION) * a + coef[2, crows] * around + tracer_forcing[c, trows]
                )
            return carry

        lax.fori_loop(0, STEPS_PER_PHASE, one_step, 0)

    final = [waves[c, HALO : HALO + ROWS, :COLS] for c in range(3)]
    final += [tracers[c, ROWS : 2 * ROWS, :COLS] for c in range(5)]
    for c in range(FIELDS):
        state_ref[c] = final[c]
    if not last:
        received = [received_ref[c] for c in range(FIELDS)]
        write_export(final, received, land_ref[...].astype(f32), smix_ref, imix_ref, turned, export_ref)


def substeps(last, place, damping, wave, smix, imix, tiles, received, land):
    state = jax.ShapeDtypeStruct((FIELDS, ROWS, COLS), f32)
    exported = jax.ShapeDtypeStruct((ROWS * FIELDS, COLS), jnp.bfloat16)
    extra = () if last else (received, land)
    return pl.pallas_call(
        lambda *refs: substep_kernel(last, *refs),
        out_shape=state if last else (state, exported),
        in_specs=[SMEM] * 5 + [VMEM] * (5 + len(extra)),
        out_specs=VMEM if last else (VMEM, VMEM),
        scratch_shapes=[
            pltpu.VMEM((3, 5 * ROWS, WIDE), f32),
            pltpu.VMEM((3, 5 * ROWS, WIDE), f32),
            pltpu.VMEM((5, 3 * ROWS, WIDE), f32),
            pltpu.VMEM((5, 3 * ROWS, WIDE), f32),
            pltpu.VMEM((3, 5 * ROWS, WIDE), f32),
            pltpu.VMEM((2, ROWS * FIELDS, LANES), f32),
        ],
        compiler_params=PARAMS,
        name="substeps_last" if last else "substeps",
    )(place, damping, wave, smix, imix, *tiles, *extra)


def ring(block, axis, by):
    count = lax.axis_size(axis)
    return lax.ppermute(block, axis, [(i, (i + by) % count) for i in range(count)])


def line(block, axis, by):
    count = lax.axis_size(axis)
    return lax.ppermute(block, axis, [(i, i + by) for i in range(count) if 0 <= i + by < count])


def crossed(block, by):
    count = lax.axis_size("gx")
    route = [
        (s * count + g, (1 - s) * count + (g + by) % count) for s in range(2) for g in range(count)
    ]
    return lax.ppermute(block, ("sec", "gx"), route)


def local(
    section_state, prev_import, land_mask, state_mix, import_mix, damping, wave_speed,
    remap_owner, remap_slot, remap_weight,
):
    fields = section_state[0]
    land = land_mask[0]
    smix = state_mix[0]
    imix = import_mix[0]
    damping = damping[0]
    wave = wave_speed[0]
    gx = lax.axis_index("gx")
    gy = lax.axis_index("gy")
    place = jnp.stack(
        [gx, gy, lax.axis_size("gx") * ROWS, lax.axis_size("gy") * COLS]
    ).astype(jnp.int32)
    owner = remap_owner[0].reshape(-1)
    slot = remap_slot[0].reshape(-1)
    entry = ((owner - gx + 2) * ROWS + slot // 4) * 2 + (slot % 4) // 2
    second = lax.iota(jnp.int32, owner.shape[0]) % 2
    index = entry + ((slot % 2) ^ second) * (5 * ROWS * 2)
    weight = remap_weight[0].reshape(ROWS, COLS, 128)

    exported = export(fields, prev_import[0], land, smix, imix)
    for interval in range(ITERS):
        last = interval == ITERS - 1
        left = crossed(exported, 1)
        right = crossed(exported, -1)
        near = ring(jnp.concatenate([left, right], axis=0), "gx", 1)
        far = ring(right, "gx", -1)
        payload, low, high, received = remap(index, near, far, left, right, weight, fields, land)
        from_right = line(low, "gy", -1)
        from_left = line(high, "gy", 1)
        payload = lax.dynamic_update_slice(
            payload, jnp.concatenate([from_left, from_right], axis=0), (STRIPS, 0, 0)
        )
        outer = payload[FAR_FROM:]
        tiles = (
            line(outer, "gx", 2),
            line(payload, "gx", 1),
            payload,
            line(payload, "gx", -1),
            line(outer, "gx", -2),
        )
        result = substeps(last, place, damping, wave, smix, imix, tiles, received, land)
        if last:
            fields = result
        else:
            fields, exported = result
    return (fields[None], received[None])


def solution(mesh):
    in_specs = (
        P("sec", None, "gx", "gy"),
        P("sec", None, "gx", "gy"),
        P("sec", "gx", "gy"),
        P("sec", None, None),
        P("sec", None, None),
        P("sec", None),
        P("sec", None),
        P("sec", "gx", "gy", None),
        P("sec", "gx", "gy", None),
        P("sec", "gx", "gy", None, None),
    )
    out_specs = (P("sec", None, "gx", "gy"), P("sec", None, "gx", "gy"))
    return jax.shard_map(local, mesh=mesh, in_specs=in_specs, out_specs=out_specs, check_vma=False)
```

```python
import jax
import jax.numpy as jnp
from jax import lax
from jax.experimental import pallas as pl
from jax.experimental.pallas import tpu as pltpu
from jax.sharding import PartitionSpec as P

SUBSTEPS = 16
ITERS = 2
DIFFUSION = 0.1
COUPLING = 0.2

FIELDS = 8
WAVES = 3
TRACERS = 5
ROWS = 16
COLS = 256
LANES = 128
TURNED = ROWS * FIELDS
STRIP = 32
STEPS_PER_PHASE = 4

F_TRACER = 0
F_STRIP_T = 10
F_STRIP_W = 12
F_WAVE = 14
F_PLANES = 20
F_FAR = 12
X_TRACER = 0
X_TRACER_LOW = 12
X_WAVE = 24
X_WAVE_LOW = 32
X_EXPORT = 40
X_PLANES = 56
X_FAR = 24

PAD = 8
SMEM = pl.BlockSpec(memory_space=pltpu.SMEM)
VMEM = pl.BlockSpec(memory_space=pltpu.VMEM)
HBM = pl.BlockSpec(memory_space=pl.ANY)

f32 = jnp.float32
bf16 = jnp.bfloat16


def params(mib=24):
    return pltpu.CompilerParams(vmem_limit_bytes=mib * 1024 * 1024)


def shaped(shape, dtype=f32):
    return jax.ShapeDtypeStruct(shape, dtype)


def half_of(value, half):
    return value[:, half * LANES : (half + 1) * LANES]


def write_export(fields, received, wet, smix_ref, imix_ref, turned, out_ref):
    scale = wet * jnp.sqrt(1.0 + fields[1] * fields[1] + fields[2] * fields[2])
    for c in range(FIELDS):
        total = smix_ref[c, 0] * fields[0]
        for k in range(1, FIELDS):
            total = total + smix_ref[c, k] * fields[k]
        other = imix_ref[c, 0] * received[0]
        for k in range(1, FIELDS):
            other = other + imix_ref[c, k] * received[k]
        value = scale * (total + other)
        for half in range(2):
            turned[half, pl.ds(c, ROWS, stride=FIELDS), :] = half_of(value, half)
    for half in range(2):
        out_ref[:, half * LANES : (half + 1) * LANES] = turned[half].astype(bf16)


def write_strips(fields, low_ref, high_ref):
    lane = lax.broadcasted_iota(jnp.int32, (ROWS, LANES), 1)
    groups = [fields[3:7], [fields[7]] + fields[0:3]]
    for p, group in enumerate(groups):
        first = group[0][0]
        last = pltpu.roll(group[0][1], STRIP, 1)
        for j in range(1, 4):
            here = lane >= STRIP * j
            first = jnp.where(here, pltpu.roll(group[j][0], STRIP * j, 1), first)
            moved = group[j][1] if j == 3 else pltpu.roll(group[j][1], STRIP * (j + 1), 1)
            last = jnp.where(here, moved, last)
        low_ref[p] = first
        high_ref[p] = last


def export_kernel(
    smix_ref, imix_ref, fields_ref, received_ref, land_ref, out_ref, low_ref, high_ref,
    turned, fields_buf, received_buf, land_buf, sems,
):
    copies = [
        pltpu.make_async_copy(fields_ref, fields_buf, sems.at[0]),
        pltpu.make_async_copy(received_ref, received_buf, sems.at[1]),
        pltpu.make_async_copy(land_ref, land_buf, sems.at[2]),
    ]
    for copy in copies:
        copy.start()
    for copy in copies:
        copy.wait()
    fields = [fields_buf[c] for c in range(FIELDS)]
    received = [received_buf[c] for c in range(FIELDS)]
    write_export(fields, received, land_buf[...].astype(f32), smix_ref, imix_ref, turned, out_ref)
    write_strips([[half_of(v, 0), half_of(v, 1)] for v in fields], low_ref, high_ref)


def export(fields, received, land, smix, imix):
    strips = shaped((2, ROWS, LANES))
    return pl.pallas_call(
        export_kernel,
        out_shape=(shaped((TURNED, COLS), bf16), strips, strips),
        in_specs=[SMEM, SMEM, HBM, HBM, HBM],
        out_specs=(VMEM,) * 3,
        scratch_shapes=[
            pltpu.VMEM((2, TURNED, LANES), f32),
            pltpu.VMEM((FIELDS, ROWS, COLS), f32),
            pltpu.VMEM((FIELDS, ROWS, COLS), f32),
            pltpu.VMEM((ROWS, COLS), jnp.int32),
            pltpu.SemaphoreType.DMA((3,)),
        ],
        compiler_params=params(56),
        name="export",
    )(smix, imix, fields, received, land)


def pack_kernel(opposite_ref, fields_ref, left_ref, right_ref, near_ref, far_ref):
    def put(at, low_at, value):
        high = value.astype(bf16)
        low = (value - high.astype(f32)).astype(bf16)
        for index, part in ((at, high), (low_at, low)):
            near_ref[index] = part
            if index >= X_FAR:
                far_ref[index - X_FAR] = part

    for i in range(TRACERS):
        for half in range(2):
            plane = 2 * i + half
            value = fields_ref[WAVES + i, :, half * LANES : (half + 1) * LANES]
            put(X_TRACER + plane, X_TRACER_LOW + plane, value)
    put(X_TRACER + 10, X_TRACER_LOW + 10, left_ref[0])
    put(X_TRACER + 11, X_TRACER_LOW + 11, right_ref[0])
    put(X_WAVE, X_WAVE_LOW, left_ref[1])
    put(X_WAVE + 1, X_WAVE_LOW + 1, right_ref[1])
    for i in range(WAVES):
        for half in range(2):
            plane = 2 + 2 * i + half
            value = fields_ref[i, :, half * LANES : (half + 1) * LANES]
            put(X_WAVE + plane, X_WAVE_LOW + plane, value)
    for half in range(2):
        for i in range(TURNED // 16):
            part = opposite_ref[16 * i : 16 * i + 16, half * LANES : (half + 1) * LANES]
            near_ref[X_EXPORT + half * 8 + i] = part
            far_ref[X_EXPORT - X_FAR + half * 8 + i] = part


def pack(opposite, fields, left, right):
    return pl.pallas_call(
        pack_kernel,
        out_shape=(shaped((X_PLANES, ROWS, LANES), bf16), shaped((X_PLANES - X_FAR, ROWS, LANES), bf16)),
        in_specs=[VMEM] * 4,
        out_specs=(VMEM,) * 2,
        compiler_params=params(),
        name="pack",
    )(opposite, fields, left, right)


def remap_kernel(
    index_ref, far_before_ref, before_ref, opposite_ref, after_ref, far_after_ref, weight_ref, land_ref,
    payload_ref, low_ref, high_ref, import_ref, table, turned,
):
    half_count = 5 * ROWS * 2
    windows = [far_before_ref, before_ref, opposite_ref, after_ref, far_after_ref]
    for w, ref in enumerate(windows):
        for half in range(2):
            for i in range(TURNED // 16):
                if w == 2:
                    chunk = ref[16 * i : 16 * i + 16, half * LANES : (half + 1) * LANES]
                else:
                    chunk = ref[X_EXPORT - (X_FAR if w in (0, 4) else 0) + half * 8 + i]
                chunk = chunk.astype(f32)
                for sub in range(2):
                    part = chunk[sub * 8 : sub * 8 + 8]
                    at = (w * ROWS + i * 2 + sub) * 2 + half
                    table[at] = part
                    table[half_count + at] = pltpu.roll(part, 64, 1)
    lane8 = lax.broadcasted_iota(jnp.int32, (8, LANES), 1)
    low_half = lane8 < 64
    ones = jnp.ones((8, LANES), f32)
    for x in range(ROWS):
        pieces = []
        for seg in range(4):
            at = (x * 4 + seg) * 2
            pieces.append(jnp.where(low_half, table[index_ref[at]], table[index_ref[at + 1]]))
        picked = jnp.concatenate(pieces + [ones], axis=0).astype(bf16)
        product = lax.dot_general(
            picked, weight_ref[x], (((1,), (1,)), ((), ())), preferred_element_type=f32
        )
        for half in range(2):
            cols = half_of(product, half)
            summed = jnp.where(low_half, cols[16 * half : 16 * half + 8], cols[16 * half + 8 : 16 * half + 16])
            turned[half, x * 8 : x * 8 + 8, :] = summed / cols[32:40]
    wet = land_ref[...].astype(f32)
    forcing = []
    for c in range(FIELDS):
        parts = []
        for half in range(2):
            value = turned[half, pl.ds(c, ROWS, stride=FIELDS), :]
            import_ref[c, :, half * LANES : (half + 1) * LANES] = value
            part = COUPLING * half_of(wet, half) * value
            parts.append(part)
            if c < WAVES:
                payload_ref[F_WAVE + 2 * c + half] = part
            else:
                payload_ref[F_TRACER + 2 * (c - WAVES) + half] = part
        forcing.append(parts)
    for p in range(F_STRIP_T, F_WAVE):
        payload_ref[p] = jnp.zeros((ROWS, LANES), f32)
    write_strips(forcing, low_ref, high_ref)


def remap(index, windows, weight, land):
    strips = shaped((2, ROWS, LANES))
    return pl.pallas_call(
        remap_kernel,
        out_shape=(shaped((F_PLANES, ROWS, LANES)), strips, strips, shaped((FIELDS, ROWS, COLS))),
        in_specs=[SMEM] + [VMEM] * 7,
        out_specs=(VMEM,) * 4,
        scratch_shapes=[
            pltpu.VMEM((2 * 5 * ROWS * 2, FIELDS, LANES), f32),
            pltpu.VMEM((2, TURNED, LANES), f32),
        ],
        compiler_params=params(),
        name="remap",
    )(index, *windows, weight, land)


def sides(left, right, j):
    lane = lax.broadcasted_iota(jnp.int32, (ROWS, LANES), 1)
    if j:
        right = pltpu.roll(right, LANES - STRIP * j, 1)
    if j != 3:
        left = pltpu.roll(left, 96 - STRIP * j, 1)
    return jnp.where(lane < STRIP, right, jnp.where(lane >= 96, left, 0.0))


def place_field(dest, rows, parts):
    for j, part in enumerate(parts):
        dest[j, rows, :] = part


def joined(ref, at, low_at):
    return ref[at].astype(f32) + ref[low_at].astype(f32)


def inside_tile(place_ref, first_row, count, j):
    shape = (count, LANES)
    row = lax.broadcasted_iota(jnp.int32, shape, 0) + (place_ref[0] * ROWS + first_row)
    col = lax.broadcasted_iota(jnp.int32, shape, 1) + j * LANES
    if j == 2:
        col = jnp.where(col >= 3 * LANES - STRIP, col - 3 * LANES, col)
    col = col + place_ref[1] * COLS
    ok = (row >= 0) & (row < place_ref[2]) & (col >= 0) & (col < place_ref[3])
    return jnp.where(ok, 1.0, 0.0)


def westward(parts, lane):
    moved = [pltpu.roll(part, 1, 1) for part in parts]
    return [jnp.where(lane == 0, moved[j - 1], moved[j]) for j in range(3)]


def eastward(parts, lane):
    moved = [pltpu.roll(part, LANES - 1, 1) for part in parts]
    return [jnp.where(lane == LANES - 1, moved[(j + 1) % 3], moved[j]) for j in range(3)]


def tracer_kernel(
    place_ref, damping_ref, forcing_before_ref, forcing_ref, forcing_after_ref, state_before_ref,
    fields_ref, left_ref, right_ref, state_after_ref, out_ref, state, forcing, coef,
):
    for t, ref in enumerate((forcing_before_ref, forcing_ref, forcing_after_ref)):
        rows = slice(t * ROWS, (t + 1) * ROWS)
        for i in range(TRACERS):
            strip = F_STRIP_T if i < 4 else F_STRIP_W
            beside = sides(ref[strip], ref[strip + 1], i % 4)
            place_field(forcing.at[i], rows, [ref[F_TRACER + 2 * i], ref[F_TRACER + 2 * i + 1], beside])
    for t, ref in enumerate((state_before_ref, None, state_after_ref)):
        rows = slice(PAD + t * ROWS, PAD + (t + 1) * ROWS)
        for i in range(TRACERS):
            if ref is None:
                p = 0 if i < 4 else 1
                parts = [half_of(fields_ref[WAVES + i], 0), half_of(fields_ref[WAVES + i], 1)]
                parts.append(sides(left_ref[p], right_ref[p], i % 4))
            else:
                at, low = X_TRACER + 2 * i, X_TRACER_LOW + 2 * i
                parts = [joined(ref, at, low), joined(ref, at + 1, low + 1)]
                at, low = (X_TRACER + 10, X_TRACER_LOW + 10) if i < 4 else (X_WAVE, X_WAVE_LOW)
                parts.append(sides(joined(ref, at, low), joined(ref, at + 1, low + 1), i % 4))
            place_field(state.at[0, i], rows, parts)
    height = 3 * ROWS
    for k in range(2):
        for i in range(TRACERS):
            for j in range(3):
                state[k, i, j, 0:PAD, :] = jnp.zeros((PAD, LANES), f32)
                state[k, i, j, PAD + height : height + 2 * PAD, :] = jnp.zeros((PAD, LANES), f32)
    for j in range(3):
        coef[j] = inside_tile(place_ref, -ROWS, height, j) * DIFFUSION

    lane = lax.broadcasted_iota(jnp.int32, (8, LANES), 1)
    keep = [(1.0 - damping_ref[WAVES + c]) - 4.0 * DIFFUSION for c in range(TRACERS)]

    def step(source, dest, first, count):
        for t in range(first, first + count):
            at = PAD + 8 * t
            here = slice(8 * t, 8 * t + 8)
            for c in range(TRACERS):
                mid = [state[source, c, j, at : at + 8, :] for j in range(3)]
                west = westward(mid, lane)
                east = eastward(mid, lane)
                for j in range(3):
                    above = state[source, c, j, at + 1 : at + 9, :]
                    below = state[source, c, j, at - 1 : at + 7, :]
                    around = (above + below) + (east[j] + west[j])
                    state[dest, c, j, at : at + 8, :] = (
                        keep[c] * mid[j] + forcing[c, j, here, :]
                    ) + coef[j, here, :] * around

    def pair_of_steps(first, count):
        def run(_, carry):
            step(0, 1, first, count)
            step(1, 0, first, count)
            return carry
        return run

    lax.fori_loop(0, SUBSTEPS // 4, pair_of_steps(0, 6), 0)
    lax.fori_loop(0, SUBSTEPS // 4, pair_of_steps(1, 4), 0)
    for i in range(TRACERS):
        for half in range(2):
            out_ref[i, :, half * LANES : (half + 1) * LANES] = state[0, i, half, PAD + ROWS : PAD + 2 * ROWS, :]


def tracer_steps(place, damping, forcings, before, fields, left, right, after):
    return pl.pallas_call(
        tracer_kernel,
        out_shape=shaped((TRACERS, ROWS, COLS)),
        in_specs=[SMEM] * 2 + [VMEM] * 8,
        out_specs=VMEM,
        scratch_shapes=[
            pltpu.VMEM((2, TRACERS, 3, 3 * ROWS + 2 * PAD, LANES), f32),
            pltpu.VMEM((TRACERS, 3, 3 * ROWS, LANES), f32),
            pltpu.VMEM((3, 3 * ROWS, LANES), f32),
        ],
        compiler_params=params(),
        cost_estimate=pl.CostEstimate(flops=10_000_000, bytes_accessed=4_000_000, transcendentals=0),
        name="tracer_steps",
    )(place, damping, *forcings, before, fields, left, right, after)


def wave_kernel(last, place_ref, damping_ref, wave_ref, smix_ref, imix_ref, *refs):
    forcing_refs = refs[:5]
    state_refs = list(refs[5:7]) + [None] + list(refs[7:9])
    fields_ref, left_ref, right_ref, tracers_ref = refs[9:13]
    if last:
        out_ref, state, forcing, coef, turned = refs[13:]
    else:
        received_ref, land_ref, out_ref, export_ref, low_ref, high_ref, state, forcing, coef, turned = refs[13:]
    height = 5 * ROWS
    for t, ref in enumerate(forcing_refs):
        rows = slice(t * ROWS, (t + 1) * ROWS)
        base = F_FAR if t in (0, 4) else 0
        left, right = ref[F_STRIP_W - base], ref[F_STRIP_W - base + 1]
        for i in range(WAVES):
            at = F_WAVE - base + 2 * i
            place_field(forcing.at[i], rows, [ref[at], ref[at + 1], sides(left, right, i + 1)])
    for t, ref in enumerate(state_refs):
        rows = slice(PAD + t * ROWS, PAD + (t + 1) * ROWS)
        base = X_FAR if t in (0, 4) else 0
        if ref is None:
            left, right = left_ref[1], right_ref[1]
        else:
            at, low = X_WAVE - base, X_WAVE_LOW - base
            left, right = joined(ref, at, low), joined(ref, at + 1, low + 1)
        for i in range(WAVES):
            if ref is None:
                parts = [half_of(fields_ref[i], 0), half_of(fields_ref[i], 1)]
            else:
                shift = 2 + 2 * i
                parts = [joined(ref, at + shift, low + shift), joined(ref, at + shift + 1, low + shift + 1)]
            place_field(state.at[i], rows, parts + [sides(left, right, i + 1)])
    for i in range(WAVES):
        for j in range(3):
            state[i, j, 0:PAD, :] = jnp.zeros((PAD, LANES), f32)
            state[i, j, PAD + height : height + 2 * PAD, :] = jnp.zeros((PAD, LANES), f32)
    for j in range(3):
        inside = inside_tile(place_ref, -2 * ROWS, height, j)
        coef[0, j] = inside * (0.5 * wave_ref[0])
        coef[1, j] = inside * (0.5 * wave_ref[1])

    lane = lax.broadcasted_iota(jnp.int32, (8, LANES), 1)
    keep = [1.0 - damping_ref[c] for c in range(WAVES)]

    def step(first, end):
        for t in range(first, end):
            at = PAD + 8 * t
            here = slice(8 * t, 8 * t + 8)
            v = [state[2, j, at : at + 8, :] for j in range(3)]
            west = westward(v, lane)
            east = eastward(v, lane)
            for j in range(3):
                spread = (state[1, j, at + 1 : at + 9, :] - state[1, j, at - 1 : at + 7, :]) + (east[j] - west[j])
                state[0, j, at : at + 8, :] = (
                    keep[0] * state[0, j, at : at + 8, :] + forcing[0, j, here, :]
                ) - coef[0, j, here, :] * spread
        for t in range(first, end):
            at = PAD + 8 * t
            here = slice(8 * t, 8 * t + 8)
            h = [state[0, j, at : at + 8, :] for j in range(3)]
            west = westward(h, lane)
            east = eastward(h, lane)
            for j in range(3):
                slope = state[0, j, at + 1 : at + 9, :] - state[0, j, at - 1 : at + 7, :]
                factor = coef[1, j, here, :]
                state[1, j, at : at + 8, :] = (
                    keep[1] * state[1, j, at : at + 8, :] + forcing[1, j, here, :]
                ) - factor * slope
                state[2, j, at : at + 8, :] = (
                    keep[2] * state[2, j, at : at + 8, :] + forcing[2, j, here, :]
                ) - factor * (east[j] - west[j])

    def steps(first, end):
        def run(_, carry):
            step(first, end)
            return carry
        return run

    for phase in range(SUBSTEPS // STEPS_PER_PHASE):
        lax.fori_loop(0, STEPS_PER_PHASE, steps(phase, 10 - phase), 0)

    own = slice(PAD + 2 * ROWS, PAD + 3 * ROWS)
    halves = [[state[i, half, own, :] for half in range(2)] for i in range(WAVES)]
    for i in range(TRACERS):
        halves.append([half_of(tracers_ref[i], half) for half in range(2)])
    for i in range(FIELDS):
        for half in range(2):
            out_ref[i, :, half * LANES : (half + 1) * LANES] = halves[i][half]
    if not last:
        fields = [jnp.concatenate(pair, axis=1) for pair in halves]
        received = [received_ref[c] for c in range(FIELDS)]
        write_export(fields, received, land_ref[...].astype(f32), smix_ref, imix_ref, turned, export_ref)
        write_strips(halves, low_ref, high_ref)


def wave_steps(last, place, damping, wave, smix, imix, operands):
    state = shaped((FIELDS, ROWS, COLS))
    strips = shaped((2, ROWS, LANES))
    return pl.pallas_call(
        lambda *refs: wave_kernel(last, *refs),
        out_shape=state if last else (state, shaped((TURNED, COLS), bf16), strips, strips),
        in_specs=[SMEM] * 5 + [VMEM] * len(operands),
        out_specs=VMEM if last else (VMEM,) * 4,
        scratch_shapes=[
            pltpu.VMEM((WAVES, 3, 5 * ROWS + 2 * PAD, LANES), f32),
            pltpu.VMEM((WAVES, 3, 5 * ROWS, LANES), f32),
            pltpu.VMEM((2, 3, 5 * ROWS, LANES), f32),
            pltpu.VMEM((2, TURNED, LANES), f32),
        ],
        compiler_params=params(),
        name="wave_steps_last" if last else "wave_steps",
    )(place, damping, wave, smix, imix, *operands)


def line(block, axis, by):
    count = lax.axis_size(axis)
    return lax.ppermute(block, axis, [(i, i + by) for i in range(count) if 0 <= i + by < count])


def local(
    section_state, prev_import, land_mask, state_mix, import_mix, damping, wave_speed,
    remap_owner, remap_slot, remap_weight,
):
    fields = section_state[0]
    land = land_mask[0]
    smix = state_mix[0]
    imix = import_mix[0]
    damping = damping[0]
    wave = wave_speed[0]
    gx = lax.axis_index("gx")
    gy = lax.axis_index("gy")
    place = jnp.stack(
        [gx, gy, lax.axis_size("gx") * ROWS, lax.axis_size("gy") * COLS]
    ).astype(jnp.int32)
    owner = remap_owner[0].reshape(-1)
    slot = remap_slot[0].reshape(-1)
    entry = ((owner - gx + 2) * ROWS + slot // 4) * 2 + (slot % 4) // 2
    second = lax.iota(jnp.int32, owner.shape[0]) % 2
    index = entry + ((slot % 2) ^ second) * (5 * ROWS * 2)
    weight = remap_weight[0].reshape(ROWS, COLS, 128)

    exported, low, high = export(fields, prev_import[0], land, smix, imix)
    for interval in range(ITERS):
        last = interval == ITERS - 1
        opposite = lax.ppermute(exported, "sec", [(0, 1), (1, 0)])
        left = line(high, "gy", 1)
        right = line(low, "gy", -1)
        near, far = pack(opposite, fields, left, right)
        before = line(near, "gx", 1)
        after = line(near, "gx", -1)
        far_before = line(far, "gx", 2)
        far_after = line(far, "gx", -2)
        forcing, low, high, received = remap(
            index, (far_before, before, opposite, after, far_after), weight, land
        )
        from_left = line(high, "gy", 1)
        from_right = line(low, "gy", -1)
        strips = jnp.stack([from_left, from_right], axis=1).reshape(4, ROWS, LANES)
        forcing = lax.dynamic_update_slice(forcing, strips, (F_STRIP_T, 0, 0))
        outer = forcing[F_FAR:]
        forcing_before = line(forcing, "gx", 1)
        forcing_after = line(forcing, "gx", -1)
        forcing_far_before = line(outer, "gx", 2)
        forcing_far_after = line(outer, "gx", -2)
        tracers = tracer_steps(
            place, damping, (forcing_before, forcing, forcing_after), before, fields, left, right, after
        )
        operands = (forcing_far_before, forcing_before, forcing, forcing_after, forcing_far_after)
        operands += (far_before, before, after, far_after, fields, left, right, tracers)
        if last:
            fields = wave_steps(last, place, damping, wave, smix, imix, operands)
        else:
            operands += (received, land)
            fields, exported, low, high = wave_steps(last, place, damping, wave, smix, imix, operands)
    return (fields[None], received[None])


def solution(mesh):
    in_specs = (
        P("sec", None, "gx", "gy"),
        P("sec", None, "gx", "gy"),
        P("sec", "gx", "gy"),
        P("sec", None, None),
        P("sec", None, None),
        P("sec", None),
        P("sec", None),
        P("sec", "gx", "gy", None),
        P("sec", "gx", "gy", None),
        P("sec", "gx", "gy", None, None),
    )
    out_specs = (P("sec", None, "gx", "gy"), P("sec", None, "gx", "gy"))
    return jax.shard_map(local, mesh=mesh, in_specs=in_specs, out_specs=out_specs, check_vma=False)
```

```python
import jax
import jax.numpy as jnp
from jax import lax
from jax.experimental import pallas as pl
from jax.experimental.pallas import tpu as pltpu
from jax.sharding import PartitionSpec as P

SUBSTEPS = 16
ITERS = 2
DIFFUSION = 0.1
COUPLING = 0.2

FIELDS = 8
WAVES = 3
TRACERS = 5
ROWS = 16
COLS = 256
LANES = 128
TURNED = ROWS * FIELDS
STRIP = 32
STEPS_PER_PHASE = 4

T_PLANES = 12
W_PLANES = 8
A_WAVE = T_PLANES
A_EXPORT = A_WAVE + 2 * W_PLANES
A_PLANES = A_EXPORT + 16
B_WAVE = T_PLANES
B_BEHIND = B_WAVE + 2 * W_PLANES
B_PLANES = B_BEHIND + 2 * W_PLANES

PAD = 8
WAVE_SPEED = 8
ROW0, COL0, ROW_END, COL_END = 10, 11, 12, 13
SMEM = pl.BlockSpec(memory_space=pltpu.SMEM)
VMEM = pl.BlockSpec(memory_space=pltpu.VMEM)
HBM = pl.BlockSpec(memory_space=pl.ANY)

f32 = jnp.float32
bf16 = jnp.bfloat16


def params(mib=24):
    return pltpu.CompilerParams(vmem_limit_bytes=mib * 1024 * 1024)


def shaped(shape, dtype=f32):
    return jax.ShapeDtypeStruct(shape, dtype)


def half_of(value, half):
    return value[:, half * LANES : (half + 1) * LANES]


def write_export(fields, received, wet, smix_ref, imix_ref, turned, out_ref):
    scale = wet * jnp.sqrt(1.0 + fields[1] * fields[1] + fields[2] * fields[2])
    for c in range(FIELDS):
        total = smix_ref[c, 0] * fields[0]
        for k in range(1, FIELDS):
            total = total + smix_ref[c, k] * fields[k]
        other = imix_ref[c, 0] * received[0]
        for k in range(1, FIELDS):
            other = other + imix_ref[c, k] * received[k]
        value = scale * (total + other)
        for half in range(2):
            turned[half, pl.ds(c, ROWS, stride=FIELDS), :] = half_of(value, half)
    for half in range(2):
        out_ref[:, half * LANES : (half + 1) * LANES] = turned[half].astype(bf16)


def write_strips(fields, low_ref, high_ref):
    lane = lax.broadcasted_iota(jnp.int32, (ROWS, LANES), 1)
    groups = [fields[3:7], [fields[7]] + fields[0:3]]
    for p, group in enumerate(groups):
        first = group[0][0]
        last = pltpu.roll(group[0][1], STRIP, 1)
        for j in range(1, 4):
            here = lane >= STRIP * j
            first = jnp.where(here, pltpu.roll(group[j][0], STRIP * j, 1), first)
            moved = group[j][1] if j == 3 else pltpu.roll(group[j][1], STRIP * (j + 1), 1)
            last = jnp.where(here, moved, last)
        low_ref[p] = first
        high_ref[p] = last


def export_kernel(
    smix_ref, imix_ref, fields_ref, received_ref, land_ref,
    out_ref, low_ref, high_ref, fields_out, land_out, turned, received_buf, sems,
):
    copies = [
        pltpu.make_async_copy(fields_ref, fields_out, sems.at[0]),
        pltpu.make_async_copy(received_ref, received_buf, sems.at[1]),
        pltpu.make_async_copy(land_ref, land_out, sems.at[2]),
    ]
    for copy in copies:
        copy.start()
    for copy in copies:
        copy.wait()
    fields = [fields_out[c] for c in range(FIELDS)]
    received = [received_buf[c] for c in range(FIELDS)]
    write_export(fields, received, land_out[...].astype(f32), smix_ref, imix_ref, turned, out_ref)
    write_strips([[half_of(v, 0), half_of(v, 1)] for v in fields], low_ref, high_ref)


def export(fields, received, land, smix, imix):
    strips = shaped((2, ROWS, LANES))
    return pl.pallas_call(
        export_kernel,
        out_shape=(
            shaped((TURNED, COLS), bf16), strips, strips, shaped((FIELDS, ROWS, COLS)), shaped((ROWS, COLS), jnp.int32),
        ),
        in_specs=[SMEM, SMEM, HBM, HBM, HBM],
        out_specs=(VMEM,) * 5,
        scratch_shapes=[
            pltpu.VMEM((2, TURNED, LANES), f32),
            pltpu.VMEM((FIELDS, ROWS, COLS), f32),
            pltpu.SemaphoreType.DMA((3,)),
        ],
        compiler_params=params(56),
        name="export",
    )(smix, imix, fields, received, land)


def stage_kernel(weight_ref, out_ref, sem):
    copy = pltpu.make_async_copy(weight_ref, out_ref, sem)
    copy.start()
    copy.wait()


def stage(weight):
    return pl.pallas_call(
        stage_kernel,
        out_shape=shaped(weight.shape, weight.dtype),
        in_specs=[HBM],
        out_specs=VMEM,
        scratch_shapes=[pltpu.SemaphoreType.DMA],
        compiler_params=params(56),
        cost_estimate=pl.CostEstimate(flops=0, bytes_accessed=4_000_000, transcendentals=0),
        name="stage_weights",
    )(weight)


def split_to(ref, at, low_at, value):
    high = value.astype(bf16)
    ref[at] = high
    ref[low_at] = (value - high.astype(f32)).astype(bf16)


def write_halo(ref, base, fields, left, right):
    for i in range(TRACERS):
        for half in range(2):
            ref[2 * i + half] = fields(WAVES + i, half).astype(bf16)
    ref[10] = left[0].astype(bf16)
    ref[11] = right[0].astype(bf16)
    split_to(ref, base, base + W_PLANES, left[1])
    split_to(ref, base + 1, base + 1 + W_PLANES, right[1])
    for i in range(WAVES):
        for half in range(2):
            at = base + 2 + 2 * i + half
            split_to(ref, at, at + W_PLANES, fields(i, half))


def pack_kernel(opposite_ref, fields_ref, left_ref, right_ref, index_ref, config_ref, weight_ref, near_ref, far_ref):
    del index_ref, config_ref, weight_ref
    write_halo(
        near_ref, A_WAVE, lambda i, half: fields_ref[i, :, half * LANES : (half + 1) * LANES], left_ref, right_ref
    )
    for half in range(2):
        for i in range(TURNED // 16):
            part = opposite_ref[16 * i : 16 * i + 16, half * LANES : (half + 1) * LANES]
            near_ref[A_EXPORT + half * 8 + i] = part
            far_ref[half * 8 + i] = part


def pack(opposite, fields, left, right, index, config, weight):
    return pl.pallas_call(
        pack_kernel,
        out_shape=(shaped((A_PLANES, ROWS, LANES), bf16), shaped((16, ROWS, LANES), bf16)),
        in_specs=[VMEM] * 4 + [HBM] * 3,
        out_specs=(VMEM,) * 2,
        compiler_params=params(),
        name="pack",
    )(opposite, fields, left, right, index, config, weight)


def pack_forcing_kernel(
    forcing_ref, left_ref, right_ref, before_ref, after_ref, forward_ref, backward_ref, far_ref,
):
    for ref, behind in ((forward_ref, before_ref), (backward_ref, after_ref)):
        write_halo(
            ref, B_WAVE, lambda i, half: forcing_ref[i, :, half * LANES : (half + 1) * LANES], left_ref, right_ref
        )
        for p in range(2 * W_PLANES):
            ref[B_BEHIND + p] = behind[A_WAVE + p]
    for p in range(2 * W_PLANES):
        far_ref[p] = forward_ref[B_WAVE + p]


def pack_forcing(forcing, left, right, before, after):
    payload = shaped((B_PLANES, ROWS, LANES), bf16)
    return pl.pallas_call(
        pack_forcing_kernel,
        out_shape=(payload, payload, shaped((2 * W_PLANES, ROWS, LANES), bf16)),
        in_specs=[VMEM] * 5,
        out_specs=(VMEM,) * 3,
        compiler_params=params(),
        name="pack_forcing",
    )(forcing, left, right, before, after)


def remap_kernel(
    index_ref, far_before_ref, before_ref, opposite_ref, after_ref, far_after_ref, weight_ref, land_ref,
    forcing_ref, low_ref, high_ref, import_ref, table, turned,
):
    half_count = 5 * ROWS * 2
    windows = [far_before_ref, before_ref, opposite_ref, after_ref, far_after_ref]
    for w, ref in enumerate(windows):
        for half in range(2):
            for i in range(TURNED // 16):
                if w == 2:
                    chunk = ref[16 * i : 16 * i + 16, half * LANES : (half + 1) * LANES]
                else:
                    chunk = ref[(0 if w in (0, 4) else A_EXPORT) + half * 8 + i]
                chunk = chunk.astype(f32)
                for sub in range(2):
                    part = chunk[sub * 8 : sub * 8 + 8]
                    at = (w * ROWS + i * 2 + sub) * 2 + half
                    table[at] = part
                    table[half_count + at] = pltpu.roll(part, 64, 1)
    lane8 = lax.broadcasted_iota(jnp.int32, (8, LANES), 1)
    low_half = lane8 < 64
    ones = jnp.ones((8, LANES), f32)
    for x in range(ROWS):
        pieces = []
        for seg in range(4):
            at = (x * 4 + seg) * 2
            pieces.append(jnp.where(low_half, table[index_ref[at]], table[index_ref[at + 1]]))
        picked = jnp.concatenate(pieces + [ones], axis=0).astype(bf16)
        product = lax.dot_general(
            picked, weight_ref[x], (((1,), (1,)), ((), ())), preferred_element_type=f32
        )
        for half in range(2):
            cols = half_of(product, half)
            summed = jnp.where(low_half, cols[16 * half : 16 * half + 8], cols[16 * half + 8 : 16 * half + 16])
            turned[half, x * 8 : x * 8 + 8, :] = summed / cols[32:40]
    wet = land_ref[...].astype(f32)
    forcing = []
    for c in range(FIELDS):
        parts = []
        for half in range(2):
            value = turned[half, pl.ds(c, ROWS, stride=FIELDS), :]
            import_ref[c, :, half * LANES : (half + 1) * LANES] = value
            part = COUPLING * half_of(wet, half) * value
            forcing_ref[c, :, half * LANES : (half + 1) * LANES] = part
            parts.append(part)
        forcing.append(parts)
    write_strips(forcing, low_ref, high_ref)


def remap(index, windows, weight, land):
    strips = shaped((2, ROWS, LANES))
    return pl.pallas_call(
        remap_kernel,
        out_shape=(shaped((FIELDS, ROWS, COLS)), strips, strips, shaped((FIELDS, ROWS, COLS))),
        in_specs=[SMEM] + [VMEM] * 7,
        out_specs=(VMEM,) * 4,
        scratch_shapes=[
            pltpu.VMEM((2 * 5 * ROWS * 2, FIELDS, LANES), f32),
            pltpu.VMEM((2, TURNED, LANES), f32),
        ],
        compiler_params=params(),
        name="remap",
    )(index, *windows, weight, land)


def sides(left, right, j):
    lane = lax.broadcasted_iota(jnp.int32, (ROWS, LANES), 1)
    if j:
        right = pltpu.roll(right, LANES - STRIP * j, 1)
    if j != 3:
        left = pltpu.roll(left, 96 - STRIP * j, 1)
    return jnp.where(lane < STRIP, right, jnp.where(lane >= 96, left, 0.0))


def place_field(dest, rows, parts):
    for j, part in enumerate(parts):
        dest[j, rows, :] = part


def joined(ref, at, low_at):
    return ref[at].astype(f32) + ref[low_at].astype(f32)


def inside_tile(config_ref, first_row, count, j, shift=0):
    shape = (count, LANES)
    row = lax.broadcasted_iota(jnp.int32, shape, 0).astype(f32) + (config_ref[ROW0] + first_row)
    col = lax.broadcasted_iota(jnp.int32, shape, 1) + j * LANES
    if j == 2:
        col = jnp.where(col >= 3 * LANES - STRIP, col - 3 * LANES, col)
    col = (col + shift).astype(f32) + config_ref[COL0]
    ok = (row >= 0.0) & (row < config_ref[ROW_END]) & (col >= 0.0) & (col < config_ref[COL_END])
    return jnp.where(ok, 1.0, 0.0)


def westward(parts, lane, by=1):
    moved = [pltpu.roll(part, by, 1) for part in parts]
    return [jnp.where(lane < by, moved[j - 1], moved[j]) for j in range(3)]


def eastward(parts, lane, by=1):
    moved = [pltpu.roll(part, LANES - by, 1) for part in parts]
    return [jnp.where(lane >= LANES - by, moved[(j + 1) % 3], moved[j]) for j in range(3)]


def own_parts(fields_ref, left_ref, right_ref, i):
    p, j = (0, i - WAVES) if WAVES <= i < FIELDS - 1 else (1, (i + 1) % FIELDS)
    return [
        fields_ref[i, :, :LANES], fields_ref[i, :, LANES:], sides(left_ref[p], right_ref[p], j),
    ]


def tracer_parts(ref, wave_base, i):
    parts = [ref[2 * i].astype(f32), ref[2 * i + 1].astype(f32)]
    at = 10 if i < 4 else wave_base
    return parts + [sides(ref[at].astype(f32), ref[at + 1].astype(f32), i % 4)]


def wave_parts(ref, base, i):
    planes = [base + 2 + 2 * i, base + 3 + 2 * i, base, base + 1]
    first, second, left, right = [joined(ref, p, p + W_PLANES) for p in planes]
    return [first, second, sides(left, right, i + 1)]


def tracer_kernel(
    config_ref, forcing_before_ref, forcing_ref, forcing_left_ref, forcing_right_ref, forcing_after_ref,
    state_before_ref, fields_ref, left_ref, right_ref, state_after_ref, out_ref, state, forcing, coef,
):
    own_forcing = (forcing_ref, forcing_left_ref, forcing_right_ref)
    own_state = (fields_ref, left_ref, right_ref)
    for t, ref in enumerate((forcing_before_ref, None, forcing_after_ref)):
        rows = slice(t * ROWS, (t + 1) * ROWS)
        for i in range(TRACERS):
            parts = own_parts(*own_forcing, WAVES + i) if ref is None else tracer_parts(ref, B_WAVE, i)
            place_field(forcing.at[i], rows, parts)
    for t, ref in enumerate((state_before_ref, None, state_after_ref)):
        rows = slice(PAD + t * ROWS, PAD + (t + 1) * ROWS)
        for i in range(TRACERS):
            parts = own_parts(*own_state, WAVES + i) if ref is None else tracer_parts(ref, A_WAVE, i)
            place_field(state.at[0, i], rows, parts)
    height = 3 * ROWS
    for k in range(2):
        for i in range(TRACERS):
            for j in range(3):
                state[k, i, j, 0:PAD, :] = jnp.zeros((PAD, LANES), f32)
                state[k, i, j, PAD + height : height + 2 * PAD, :] = jnp.zeros((PAD, LANES), f32)
    for j in range(3):
        coef[j] = inside_tile(config_ref, -ROWS, height, j) * DIFFUSION

    lane = lax.broadcasted_iota(jnp.int32, (8, LANES), 1)
    keep = [(1.0 - config_ref[WAVES + c]) - 4.0 * DIFFUSION for c in range(TRACERS)]

    def step(source, dest, first, count):
        for t in range(first, first + count):
            at = PAD + 8 * t
            here = slice(8 * t, 8 * t + 8)
            for c in range(TRACERS):
                mid = [state[source, c, j, at : at + 8, :] for j in range(3)]
                west = westward(mid, lane)
                east = eastward(mid, lane)
                for j in range(3):
                    above = state[source, c, j, at + 1 : at + 9, :]
                    below = state[source, c, j, at - 1 : at + 7, :]
                    around = (above + below) + (east[j] + west[j])
                    state[dest, c, j, at : at + 8, :] = (
                        keep[c] * mid[j] + forcing[c, j, here, :]
                    ) + coef[j, here, :] * around

    def pair_of_steps(first, count):
        def run(_, carry):
            step(0, 1, first, count)
            step(1, 0, first, count)
            return carry
        return run

    lax.fori_loop(0, SUBSTEPS // 4, pair_of_steps(0, 6), 0)
    lax.fori_loop(0, SUBSTEPS // 4, pair_of_steps(1, 4), 0)
    for i in range(TRACERS):
        for half in range(2):
            out_ref[i, :, half * LANES : (half + 1) * LANES] = state[0, i, half, PAD + ROWS : PAD + 2 * ROWS, :]


def tracer_steps(config, operands):
    return pl.pallas_call(
        tracer_kernel,
        out_shape=shaped((TRACERS, ROWS, COLS)),
        in_specs=[SMEM] + [VMEM] * len(operands),
        out_specs=VMEM,
        scratch_shapes=[
            pltpu.VMEM((2, TRACERS, 3, 3 * ROWS + 2 * PAD, LANES), f32),
            pltpu.VMEM((TRACERS, 3, 3 * ROWS, LANES), f32),
            pltpu.VMEM((3, 3 * ROWS, LANES), f32),
        ],
        compiler_params=params(),
        cost_estimate=pl.CostEstimate(flops=10_000_000, bytes_accessed=4_000_000, transcendentals=0),
        name="tracer_steps",
    )(config, *operands)


def wave_kernel(last, config_ref, *refs):
    if not last:
        smix_ref, imix_ref, *refs = refs
    (far_before, near_before, forcing_ref, forcing_left_ref, forcing_right_ref, near_after, far_after,
     state_before, fields_ref, left_ref, right_ref, state_after, tracers_ref, *refs) = refs
    if last:
        out_ref, state, forcing, coef = refs
    else:
        received_ref, land_ref, out_ref, export_ref, low_ref, high_ref, state, forcing, coef, turned = refs
    height = 5 * ROWS
    tiles = height // 8

    for i in range(WAVES):
        forcing_tiles = [
            wave_parts(far_before, 0, i), wave_parts(near_before, B_WAVE, i),
            own_parts(forcing_ref, forcing_left_ref, forcing_right_ref, i),
            wave_parts(near_after, B_WAVE, i), wave_parts(far_after, 0, i),
        ]
        state_tiles = [
            wave_parts(near_before, B_BEHIND, i), wave_parts(state_before, A_WAVE, i),
            own_parts(fields_ref, left_ref, right_ref, i),
            wave_parts(state_after, A_WAVE, i), wave_parts(near_after, B_BEHIND, i),
        ]
        for t in range(5):
            rows = slice(PAD + t * ROWS, PAD + (t + 1) * ROWS)
            place_field(forcing.at[i], rows, forcing_tiles[t])
            place_field(state.at[i], rows, state_tiles[t])
        for j in range(3):
            for ref in (state, forcing):
                ref[i, j, 0:PAD, :] = jnp.zeros((PAD, LANES), f32)
                ref[i, j, PAD + height : height + 2 * PAD, :] = jnp.zeros((PAD, LANES), f32)
    half_a = 0.5 * config_ref[WAVE_SPEED]
    half_b = 0.5 * config_ref[WAVE_SPEED + 1]
    first_row = -2.0 * ROWS
    for j in range(3):
        coef[0, j] = inside_tile(config_ref, first_row, height, j) * half_a
        coef[1, j] = inside_tile(config_ref, first_row + 1.0, height, j) * half_b
        coef[2, j] = inside_tile(config_ref, first_row - 1.0, height, j) * half_b
        coef[3, j] = inside_tile(config_ref, first_row, height, j, 1) * half_b
        coef[4, j] = inside_tile(config_ref, first_row, height, j, -1) * half_b

    lane = lax.broadcasted_iota(jnp.int32, (8, LANES), 1)
    keep = [1.0 - config_ref[c] for c in range(WAVES)]

    def load(ref, i, t, by=0):
        at = PAD + 8 * t + by
        return [ref[i, j, at : at + 8, :] for j in range(3)]

    def along(ref, i, t):
        ahead, behind = load(ref, i, t, 1), load(ref, i, t, -1)
        return [ahead[j] - behind[j] for j in range(3)]

    def across(parts):
        ahead, behind = eastward(parts, lane), westward(parts, lane)
        return [ahead[j] - behind[j] for j in range(3)]

    h = [load(state, 0, t) for t in range(tiles)]
    du = [along(state, 1, t) for t in range(tiles)]
    dv = [across(load(state, 2, t)) for t in range(tiles)]
    for t in range(tiles):
        at = PAD + 8 * t
        push_u, push_v = along(forcing, 1, t), across(load(forcing, 2, t))
        for j in range(3):
            coef[5, j, 8 * t : 8 * t + 8, :] = push_u[j]
            coef[6, j, 8 * t : 8 * t + 8, :] = push_v[j]
    own = (4, 5)
    sum_u = {t: [jnp.zeros((8, LANES), f32)] * 2 for t in (3, 4, 5, 6)}
    sum_v = {t: [jnp.zeros((8, LANES), f32)] * 3 for t in own}
    for step in range(SUBSTEPS):
        first = step // STEPS_PER_PHASE
        final = step == SUBSTEPS - 1
        span = range(first, tiles - first)
        for t in span:
            here = slice(8 * t, 8 * t + 8)
            push = load(forcing, 0, t)
            for j in range(3):
                h[t][j] = (keep[0] * h[t][j] + push[j]) - coef[0, j, here, :] * (du[t][j] + dv[t][j])
                if not final:
                    state[0, j, PAD + 8 * t : PAD + 8 * t + 8, :] = h[t][j]
        for t in sum_u:
            sum_u[t] = [keep[1] * sum_u[t][j] + h[t][j] for j in range(2)]
        for t in own:
            sum_v[t] = [keep[2] * sum_v[t][j] + h[t][j] for j in range(3)]
        if final:
            break
        for t in span:
            here = slice(8 * t, 8 * t + 8)
            east, west = eastward(h[t], lane, 2), westward(h[t], lane, 2)
            up, down = load(state, 0, t, 2), load(state, 0, t, -2)
            for j in range(3):
                mid = h[t][j]
                du[t][j] = (keep[1] * du[t][j] + coef[5, j, here, :]) - (
                    coef[1, j, here, :] * (up[j] - mid) - coef[2, j, here, :] * (mid - down[j])
                )
                dv[t][j] = (keep[2] * dv[t][j] + coef[6, j, here, :]) - (
                    coef[3, j, here, :] * (east[j] - mid) - coef[4, j, here, :] * (mid - west[j])
                )

    def decays(c):
        power, total = c, 1.0 + 0.0 * c
        for _ in range(SUBSTEPS - 1):
            total = total + power
            power = power * c
        return power, total

    for t in sum_u:
        for j in range(2):
            state[0, j, PAD + 8 * t : PAD + 8 * t + 8, :] = sum_u[t][j]
    power_u, total_u = decays(keep[1])
    power_v, total_v = decays(keep[2])
    for j in range(2):
        inside = inside_tile(config_ref, 0.0, ROWS, j) * half_b
        for t in own:
            at = PAD + 8 * t
            rows = slice(8 * (t - 4), 8 * (t - 4) + 8)
            factor = inside[rows]
            slope_u = state[0, j, at + 1 : at + 9, :] - state[0, j, at - 1 : at + 7, :]
            slope_v = across(sum_v[t])[j]
            new_u = power_u * state[1, j, at : at + 8, :] + total_u * forcing[1, j, at : at + 8, :] - factor * slope_u
            new_v = power_v * state[2, j, at : at + 8, :] + total_v * forcing[2, j, at : at + 8, :] - factor * slope_v
            cols = slice(j * LANES, (j + 1) * LANES)
            out_ref[0, rows, cols] = h[t][j]
            out_ref[1, rows, cols] = new_u
            out_ref[2, rows, cols] = new_v
    for i in range(TRACERS):
        out_ref[WAVES + i] = tracers_ref[i]
    if not last:
        fields = [out_ref[c] for c in range(FIELDS)]
        received = [received_ref[c] for c in range(FIELDS)]
        write_export(fields, received, land_ref[...].astype(f32), smix_ref, imix_ref, turned, export_ref)
        write_strips([[half_of(v, 0), half_of(v, 1)] for v in fields], low_ref, high_ref)


def wave_steps(last, config, mixes, operands):
    state = shaped((FIELDS, ROWS, COLS))
    strips = shaped((2, ROWS, LANES))
    scratch = [
        pltpu.VMEM((WAVES, 3, 5 * ROWS + 2 * PAD, LANES), f32),
        pltpu.VMEM((WAVES, 3, 5 * ROWS + 2 * PAD, LANES), f32),
        pltpu.VMEM((7, 3, 5 * ROWS, LANES), f32),
    ]
    if not last:
        scratch.append(pltpu.VMEM((2, TURNED, LANES), f32))
    return pl.pallas_call(
        lambda *refs: wave_kernel(last, *refs),
        out_shape=state if last else (state, shaped((TURNED, COLS), bf16), strips, strips),
        in_specs=[SMEM] * (1 + len(mixes)) + [VMEM] * len(operands),
        out_specs=VMEM if last else (VMEM,) * 4,
        scratch_shapes=scratch,
        compiler_params=params(),
        name="wave_steps_last" if last else "wave_steps",
    )(config, *mixes, *operands)


def line(block, axis, by):
    count = lax.axis_size(axis)
    return lax.ppermute(block, axis, [(i, i + by) for i in range(count) if 0 <= i + by < count])


def local(
    section_state, prev_import, land_mask, state_mix, import_mix, damping, wave_speed,
    remap_owner, remap_slot, remap_weight,
):
    smix = state_mix[0]
    imix = import_mix[0]
    gx = lax.axis_index("gx")
    gy = lax.axis_index("gy")
    place = jnp.stack([gx * ROWS, gy * COLS, lax.axis_size("gx") * ROWS, lax.axis_size("gy") * COLS])
    config = jnp.concatenate([damping[0], wave_speed[0], place.astype(f32)])
    owner = remap_owner[0].reshape(-1)
    slot = remap_slot[0].reshape(-1)
    entry = ((owner - gx + 2) * ROWS + slot // 4) * 2 + (slot % 4) // 2
    second = lax.iota(jnp.int32, owner.shape[0]) % 2
    index = entry + ((slot % 2) ^ second) * (5 * ROWS * 2)

    exported, low, high, fields, land = export(section_state[0], prev_import[0], land_mask[0], smix, imix)
    weight = stage(remap_weight[0].reshape(ROWS, COLS, 128))
    for interval in range(ITERS):
        last = interval == ITERS - 1
        opposite = lax.ppermute(exported, "sec", [(0, 1), (1, 0)])
        left = line(high, "gy", 1)
        right = line(low, "gy", -1)
        near, far = pack(opposite, fields, left, right, index, config, weight)
        before = line(near, "gx", 1)
        after = line(near, "gx", -1)
        far_before = line(far, "gx", 2)
        far_after = line(far, "gx", -2)
        forcing, low, high, received = remap(
            index, (far_before, before, opposite, after, far_after), weight, land
        )
        forcing_left = line(high, "gy", 1)
        forcing_right = line(low, "gy", -1)
        forward, backward, outer = pack_forcing(forcing, forcing_left, forcing_right, before, after)
        near_before = line(forward, "gx", 1)
        near_after = line(backward, "gx", -1)
        outer_before = line(outer, "gx", 2)
        outer_after = line(outer, "gx", -2)
        own = (forcing, forcing_left, forcing_right)
        state = (before, fields, left, right, after)
        tracers = tracer_steps(config, (near_before, *own, near_after, *state))
        operands = (outer_before, near_before, *own, near_after, outer_after, *state, tracers)
        if last:
            fields = wave_steps(last, config, (), operands)
        else:
            operands += (received, land)
            fields, exported, low, high = wave_steps(last, config, (smix, imix), operands)
    return (fields[None], received[None])


def solution(mesh):
    in_specs = (
        P("sec", None, "gx", "gy"),
        P("sec", None, "gx", "gy"),
        P("sec", "gx", "gy"),
        P("sec", None, None),
        P("sec", None, None),
        P("sec", None),
        P("sec", None),
        P("sec", "gx", "gy", None),
        P("sec", "gx", "gy", None),
        P("sec", "gx", "gy", None, None),
    )
    out_specs = (P("sec", None, "gx", "gy"), P("sec", None, "gx", "gy"))
    return jax.shard_map(local, mesh=mesh, in_specs=in_specs, out_specs=out_specs, check_vma=False)
```

```python
import jax
import jax.numpy as jnp
from jax import lax
from jax.experimental import pallas as pl
from jax.experimental.pallas import tpu as pltpu
from jax.sharding import PartitionSpec as P

SUBSTEPS = 16
ITERS = 2
DIFFUSION = 0.1
COUPLING = 0.2

FIELDS = 8
WAVES = 3
TRACERS = 5
ROWS = 16
COLS = 256
LANES = 128
TURNED = ROWS * FIELDS
STRIP = 32
STEPS_PER_PHASE = 4

A_WAVE = 10
A_EXPORT = 22
A_PLANES = 38
B_WAVE = 12
B_STRIP_T = 28
B_STRIP_W = 30
B_BEHIND = 34
B_PLANES = 46
C_STRIP_W = 16
C_PLANES = 20

PAD = 8
WAVE_SPEED = 8
ROW0, COL0, ROW_END, COL_END = 10, 11, 12, 13
SMEM = pl.BlockSpec(memory_space=pltpu.SMEM)
VMEM = pl.BlockSpec(memory_space=pltpu.VMEM)
HBM = pl.BlockSpec(memory_space=pl.ANY)

f32 = jnp.float32
bf16 = jnp.bfloat16


def params(mib=24):
    return pltpu.CompilerParams(vmem_limit_bytes=mib * 1024 * 1024)


def shaped(shape, dtype=f32):
    return jax.ShapeDtypeStruct(shape, dtype)


def half_of(value, half):
    return value[:, half * LANES : (half + 1) * LANES]


def write_export(fields, received, wet, smix_ref, imix_ref, turned, out_ref):
    scale = wet * jnp.sqrt(1.0 + fields[1] * fields[1] + fields[2] * fields[2])
    for c in range(FIELDS):
        total = smix_ref[c, 0] * fields[0]
        for k in range(1, FIELDS):
            total = total + smix_ref[c, k] * fields[k]
        other = imix_ref[c, 0] * received[0]
        for k in range(1, FIELDS):
            other = other + imix_ref[c, k] * received[k]
        value = scale * (total + other)
        for half in range(2):
            turned[half, pl.ds(c, ROWS, stride=FIELDS), :] = half_of(value, half)
    for half in range(2):
        out_ref[:, half * LANES : (half + 1) * LANES] = turned[half].astype(bf16)


def write_strips(fields, at, low_ref, high_ref):
    lane = lax.broadcasted_iota(jnp.int32, (ROWS, LANES), 1)
    groups = [fields[3:7], [fields[7]] + fields[0:3]]
    for p, group in enumerate(groups):
        first = group[0][0]
        last = pltpu.roll(group[0][1], STRIP, 1)
        for j in range(1, 4):
            here = lane >= STRIP * j
            first = jnp.where(here, pltpu.roll(group[j][0], STRIP * j, 1), first)
            moved = group[j][1] if j == 3 else pltpu.roll(group[j][1], STRIP * (j + 1), 1)
            last = jnp.where(here, moved, last)
        low_ref[at + p] = first
        high_ref[at + p] = last


def export_kernel(
    smix_ref, imix_ref, fields_ref, received_ref, land_ref,
    out_ref, fields_out, land_out, turned, received_buf, sems,
):
    copies = [
        pltpu.make_async_copy(fields_ref, fields_out, sems.at[0]),
        pltpu.make_async_copy(received_ref, received_buf, sems.at[1]),
        pltpu.make_async_copy(land_ref, land_out, sems.at[2]),
    ]
    for copy in copies:
        copy.start()
    for copy in copies:
        copy.wait()
    fields = [fields_out[c] for c in range(FIELDS)]
    received = [received_buf[c] for c in range(FIELDS)]
    write_export(fields, received, land_out[...].astype(f32), smix_ref, imix_ref, turned, out_ref)


def export(fields, received, land, smix, imix):
    return pl.pallas_call(
        export_kernel,
        out_shape=(
            shaped((TURNED, COLS), bf16), shaped((FIELDS, ROWS, COLS)), shaped((ROWS, COLS), jnp.int32),
        ),
        in_specs=[SMEM, SMEM, HBM, HBM, HBM],
        out_specs=(VMEM,) * 3,
        scratch_shapes=[
            pltpu.VMEM((2, TURNED, LANES), f32),
            pltpu.VMEM((FIELDS, ROWS, COLS), f32),
            pltpu.SemaphoreType.DMA((3,)),
        ],
        compiler_params=params(56),
        name="export",
    )(smix, imix, fields, received, land)


def split_to(ref, at, low_at, value):
    high = value.astype(bf16)
    ref[at] = high
    ref[low_at] = (value - high.astype(f32)).astype(bf16)


def write_main(ref, tracer_at, wave_at, wave_low_at, fields_ref):
    for half in range(2):
        cols = slice(half * LANES, (half + 1) * LANES)
        for i in range(TRACERS):
            ref[tracer_at + 2 * i + half] = fields_ref[WAVES + i, :, cols].astype(bf16)
        for i in range(WAVES):
            split_to(ref, wave_at + 2 * i + half, wave_low_at + 2 * i + half, fields_ref[i, :, cols])


def pack_kernel(opposite_ref, fields_ref, index_ref, config_ref, near_ref):
    del index_ref, config_ref
    write_main(near_ref, 0, A_WAVE, A_WAVE + 6, fields_ref)
    for half in range(2):
        for i in range(TURNED // 16):
            near_ref[A_EXPORT + half * 8 + i] = opposite_ref[16 * i : 16 * i + 16, half * LANES : (half + 1) * LANES]


def pack(opposite, fields, index, config):
    return pl.pallas_call(
        pack_kernel,
        out_shape=shaped((A_PLANES, ROWS, LANES), bf16),
        in_specs=[VMEM] * 2 + [HBM] * 2,
        out_specs=VMEM,
        compiler_params=params(),
        name="pack",
    )(opposite, fields, index, config)


def pack_forcing_kernel(
    forcing_ref, left_ref, right_ref, before_ref, after_ref, forward_ref, backward_ref, far_ref,
):
    for ref, behind in ((forward_ref, before_ref), (backward_ref, after_ref)):
        write_main(ref, 0, B_WAVE + 2, B_WAVE + 10, forcing_ref)
        for k, strips in enumerate((left_ref, right_ref)):
            ref[10 + k] = strips[0].astype(bf16)
            split_to(ref, B_WAVE + k, B_WAVE + 8 + k, strips[1])
            ref[B_STRIP_T + k] = strips[2].astype(bf16)
            split_to(ref, B_STRIP_W + k, B_STRIP_W + 2 + k, strips[3])
        for p in range(12):
            ref[B_BEHIND + p] = behind[A_WAVE + p]
    for p in range(16):
        far_ref[p] = forward_ref[B_WAVE + p]
    for p in range(4):
        far_ref[C_STRIP_W + p] = forward_ref[B_STRIP_W + p]


def pack_forcing(forcing, left, right, before, after):
    payload = shaped((B_PLANES, ROWS, LANES), bf16)
    return pl.pallas_call(
        pack_forcing_kernel,
        out_shape=(payload, payload, shaped((C_PLANES, ROWS, LANES), bf16)),
        in_specs=[VMEM] * 5,
        out_specs=(VMEM,) * 3,
        compiler_params=params(),
        name="pack_forcing",
    )(forcing, left, right, before, after)


def remap_kernel(
    index_ref, far_before_ref, before_ref, opposite_ref, after_ref, far_after_ref, weight_hbm, land_ref, fields_ref,
    forcing_ref, low_ref, high_ref, import_ref, table, turned, weight_ref, sem,
):
    copy = pltpu.make_async_copy(weight_hbm, weight_ref, sem)
    copy.start()
    half_count = 5 * ROWS * 2
    windows = [far_before_ref, before_ref, opposite_ref, after_ref, far_after_ref]
    for w, ref in enumerate(windows):
        for half in range(2):
            for i in range(TURNED // 16):
                if w in (1, 3):
                    chunk = ref[A_EXPORT + half * 8 + i]
                else:
                    chunk = ref[16 * i : 16 * i + 16, half * LANES : (half + 1) * LANES]
                chunk = chunk.astype(f32)
                for sub in range(2):
                    part = chunk[sub * 8 : sub * 8 + 8]
                    at = (w * ROWS + i * 2 + sub) * 2 + half
                    table[at] = part
                    table[half_count + at] = pltpu.roll(part, 64, 1)
    lane8 = lax.broadcasted_iota(jnp.int32, (8, LANES), 1)
    low_half = lane8 < 64
    ones = jnp.ones((8, LANES), f32)
    copy.wait()
    for x in range(ROWS):
        pieces = []
        for seg in range(4):
            at = (x * 4 + seg) * 2
            pieces.append(jnp.where(low_half, table[index_ref[at]], table[index_ref[at + 1]]))
        picked = jnp.concatenate(pieces + [ones], axis=0).astype(bf16)
        product = lax.dot_general(
            picked, weight_ref[x], (((1,), (1,)), ((), ())), preferred_element_type=f32
        )
        for half in range(2):
            cols = half_of(product, half)
            summed = jnp.where(low_half, cols[16 * half : 16 * half + 8], cols[16 * half + 8 : 16 * half + 16])
            turned[half, x * 8 : x * 8 + 8, :] = summed / cols[32:40]
    wet = land_ref[...].astype(f32)
    forcing = []
    for c in range(FIELDS):
        parts = []
        for half in range(2):
            value = turned[half, pl.ds(c, ROWS, stride=FIELDS), :]
            import_ref[c, :, half * LANES : (half + 1) * LANES] = value
            part = COUPLING * half_of(wet, half) * value
            forcing_ref[c, :, half * LANES : (half + 1) * LANES] = part
            parts.append(part)
        forcing.append(parts)
    state = [[half_of(fields_ref[c], half) for half in range(2)] for c in range(FIELDS)]
    write_strips(forcing, 0, low_ref, high_ref)
    write_strips(state, 2, low_ref, high_ref)


def remap(index, windows, weight, land, fields):
    strips = shaped((4, ROWS, LANES))
    return pl.pallas_call(
        remap_kernel,
        out_shape=(shaped((FIELDS, ROWS, COLS)), strips, strips, shaped((FIELDS, ROWS, COLS))),
        in_specs=[SMEM] + [VMEM] * 5 + [HBM] + [VMEM] * 2,
        out_specs=(VMEM,) * 4,
        scratch_shapes=[
            pltpu.VMEM((2 * 5 * ROWS * 2, FIELDS, LANES), f32),
            pltpu.VMEM((2, TURNED, LANES), f32),
            pltpu.VMEM((ROWS, COLS, 128), bf16),
            pltpu.SemaphoreType.DMA,
        ],
        compiler_params=params(52),
        name="remap",
    )(index, *windows, weight, land, fields)


def sides(left, right, j):
    lane = lax.broadcasted_iota(jnp.int32, (ROWS, LANES), 1)
    if j:
        right = pltpu.roll(right, LANES - STRIP * j, 1)
    if j != 3:
        left = pltpu.roll(left, 96 - STRIP * j, 1)
    return jnp.where(lane < STRIP, right, jnp.where(lane >= 96, left, 0.0))


def place_field(dest, rows, parts):
    for j, part in enumerate(parts):
        dest[j, rows, :] = part


def joined(ref, at, low_at):
    return ref[at].astype(f32) + ref[low_at].astype(f32)


def inside_tile(config_ref, first_row, count, j, shift=0):
    shape = (count, LANES)
    row = lax.broadcasted_iota(jnp.int32, shape, 0).astype(f32) + (config_ref[ROW0] + first_row)
    col = lax.broadcasted_iota(jnp.int32, shape, 1) + j * LANES
    if j == 2:
        col = jnp.where(col >= 3 * LANES - STRIP, col - 3 * LANES, col)
    col = (col + shift).astype(f32) + config_ref[COL0]
    ok = (row >= 0.0) & (row < config_ref[ROW_END]) & (col >= 0.0) & (col < config_ref[COL_END])
    return jnp.where(ok, 1.0, 0.0)


def westward(parts, lane, by=1):
    moved = [pltpu.roll(part, by, 1) for part in parts]
    return [jnp.where(lane < by, moved[j - 1], moved[j]) for j in range(3)]


def eastward(parts, lane, by=1):
    moved = [pltpu.roll(part, LANES - by, 1) for part in parts]
    return [jnp.where(lane >= LANES - by, moved[(j + 1) % 3], moved[j]) for j in range(3)]


def own_parts(fields_ref, left_ref, right_ref, at, i):
    p, j = (0, i - WAVES) if WAVES <= i < FIELDS - 1 else (1, (i + 1) % FIELDS)
    return [
        fields_ref[i, :, :LANES], fields_ref[i, :, LANES:], sides(left_ref[at + p], right_ref[at + p], j),
    ]


def tracer_parts(ref, strip_ref, strip_at, wave_strip_at, i):
    at = strip_at if i < 4 else wave_strip_at
    beside = sides(strip_ref[at].astype(f32), strip_ref[at + 1].astype(f32), i % 4)
    return [ref[2 * i].astype(f32), ref[2 * i + 1].astype(f32), beside]


def wave_parts(ref, at, low_at, strip_ref, strip_at, strip_low_at, i):
    first, second = [joined(ref, at + 2 * i + half, low_at + 2 * i + half) for half in range(2)]
    left, right = [joined(strip_ref, strip_at + k, strip_low_at + k) for k in range(2)]
    return [first, second, sides(left, right, i + 1)]


def tracer_kernel(
    config_ref, near_before_ref, forcing_ref, left_ref, right_ref, near_after_ref,
    state_before_ref, fields_ref, state_after_ref, out_ref, state, forcing, coef,
):
    for t, (near, main) in enumerate(
        ((near_before_ref, state_before_ref), (None, None), (near_after_ref, state_after_ref))
    ):
        for i in range(TRACERS):
            if near is None:
                pushed = own_parts(forcing_ref, left_ref, right_ref, 0, WAVES + i)
                parts = own_parts(fields_ref, left_ref, right_ref, 2, WAVES + i)
            else:
                pushed = tracer_parts(near, near, 10, B_WAVE, i)
                parts = tracer_parts(main, near, B_STRIP_T, B_STRIP_W, i)
            place_field(forcing.at[i], slice(t * ROWS, (t + 1) * ROWS), pushed)
            place_field(state.at[0, i], slice(PAD + t * ROWS, PAD + (t + 1) * ROWS), parts)
    height = 3 * ROWS
    for k in range(2):
        for i in range(TRACERS):
            for j in range(3):
                state[k, i, j, 0:PAD, :] = jnp.zeros((PAD, LANES), f32)
                state[k, i, j, PAD + height : height + 2 * PAD, :] = jnp.zeros((PAD, LANES), f32)
    for j in range(3):
        coef[j] = inside_tile(config_ref, -ROWS, height, j) * DIFFUSION

    lane = lax.broadcasted_iota(jnp.int32, (8, LANES), 1)
    keep = [(1.0 - config_ref[WAVES + c]) - 4.0 * DIFFUSION for c in range(TRACERS)]

    def step(source, dest, first, count):
        for t in range(first, first + count):
            at = PAD + 8 * t
            here = slice(8 * t, 8 * t + 8)
            for c in range(TRACERS):
                mid = [state[source, c, j, at : at + 8, :] for j in range(3)]
                west = westward(mid, lane)
                east = eastward(mid, lane)
                for j in range(3):
                    above = state[source, c, j, at + 1 : at + 9, :]
                    below = state[source, c, j, at - 1 : at + 7, :]
                    around = (above + below) + (east[j] + west[j])
                    state[dest, c, j, at : at + 8, :] = (
                        keep[c] * mid[j] + forcing[c, j, here, :]
                    ) + coef[j, here, :] * around

    def pair_of_steps(first, count):
        def run(_, carry):
            step(0, 1, first, count)
            step(1, 0, first, count)
            return carry
        return run

    lax.fori_loop(0, SUBSTEPS // 4, pair_of_steps(0, 6), 0)
    lax.fori_loop(0, SUBSTEPS // 4, pair_of_steps(1, 4), 0)
    for i in range(TRACERS):
        for half in range(2):
            out_ref[i, :, half * LANES : (half + 1) * LANES] = state[0, i, half, PAD + ROWS : PAD + 2 * ROWS, :]


def tracer_steps(config, operands):
    return pl.pallas_call(
        tracer_kernel,
        out_shape=shaped((TRACERS, ROWS, COLS)),
        in_specs=[SMEM] + [VMEM] * len(operands),
        out_specs=VMEM,
        scratch_shapes=[
            pltpu.VMEM((2, TRACERS, 3, 3 * ROWS + 2 * PAD, LANES), f32),
            pltpu.VMEM((TRACERS, 3, 3 * ROWS, LANES), f32),
            pltpu.VMEM((3, 3 * ROWS, LANES), f32),
        ],
        compiler_params=params(),
        cost_estimate=pl.CostEstimate(flops=10_000_000, bytes_accessed=4_000_000, transcendentals=0),
        name="tracer_steps",
    )(config, *operands)


def wave_kernel(last, config_ref, *refs):
    if not last:
        smix_ref, imix_ref, *refs = refs
    (far_before, near_before, forcing_ref, left_ref, right_ref, near_after, far_after,
     state_before, fields_ref, state_after, tracers_ref, *refs) = refs
    if last:
        out_ref, state, forcing, coef = refs
    else:
        received_ref, land_ref, out_ref, export_ref, state, forcing, coef, turned = refs
    height = 5 * ROWS
    tiles = height // 8

    for i in range(WAVES):
        forcing_tiles = [
            wave_parts(far_before, 2, 10, far_before, 0, 8, i),
            wave_parts(near_before, B_WAVE + 2, B_WAVE + 10, near_before, B_WAVE, B_WAVE + 8, i),
            own_parts(forcing_ref, left_ref, right_ref, 0, i),
            wave_parts(near_after, B_WAVE + 2, B_WAVE + 10, near_after, B_WAVE, B_WAVE + 8, i),
            wave_parts(far_after, 2, 10, far_after, 0, 8, i),
        ]
        state_tiles = [
            wave_parts(near_before, B_BEHIND, B_BEHIND + 6, far_before, C_STRIP_W, C_STRIP_W + 2, i),
            wave_parts(state_before, A_WAVE, A_WAVE + 6, near_before, B_STRIP_W, B_STRIP_W + 2, i),
            own_parts(fields_ref, left_ref, right_ref, 2, i),
            wave_parts(state_after, A_WAVE, A_WAVE + 6, near_after, B_STRIP_W, B_STRIP_W + 2, i),
            wave_parts(near_after, B_BEHIND, B_BEHIND + 6, far_after, C_STRIP_W, C_STRIP_W + 2, i),
        ]
        for t in range(5):
            rows = slice(PAD + t * ROWS, PAD + (t + 1) * ROWS)
            place_field(forcing.at[i], rows, forcing_tiles[t])
            place_field(state.at[i], rows, state_tiles[t])
        for j in range(3):
            for ref in (state, forcing):
                ref[i, j, 0:PAD, :] = jnp.zeros((PAD, LANES), f32)
                ref[i, j, PAD + height : height + 2 * PAD, :] = jnp.zeros((PAD, LANES), f32)
    half_a = 0.5 * config_ref[WAVE_SPEED]
    half_b = 0.5 * config_ref[WAVE_SPEED + 1]
    first_row = -2.0 * ROWS
    for j in range(3):
        coef[0, j] = inside_tile(config_ref, first_row, height, j) * half_a
        coef[1, j] = inside_tile(config_ref, first_row + 1.0, height, j) * half_b
        coef[2, j] = inside_tile(config_ref, first_row - 1.0, height, j) * half_b
        coef[3, j] = inside_tile(config_ref, first_row, height, j, 1) * half_b
        coef[4, j] = inside_tile(config_ref, first_row, height, j, -1) * half_b

    lane = lax.broadcasted_iota(jnp.int32, (8, LANES), 1)
    keep = [1.0 - config_ref[c] for c in range(WAVES)]

    def load(ref, i, t, by=0):
        at = PAD + 8 * t + by
        return [ref[i, j, at : at + 8, :] for j in range(3)]

    def along(ref, i, t):
        ahead, behind = load(ref, i, t, 1), load(ref, i, t, -1)
        return [ahead[j] - behind[j] for j in range(3)]

    def across(parts):
        ahead, behind = eastward(parts, lane), westward(parts, lane)
        return [ahead[j] - behind[j] for j in range(3)]

    h = [load(state, 0, t) for t in range(tiles)]
    du = [along(state, 1, t) for t in range(tiles)]
    dv = [across(load(state, 2, t)) for t in range(tiles)]
    for t in range(tiles):
        at = PAD + 8 * t
        push_u, push_v = along(forcing, 1, t), across(load(forcing, 2, t))
        for j in range(3):
            coef[5, j, 8 * t : 8 * t + 8, :] = push_u[j]
            coef[6, j, 8 * t : 8 * t + 8, :] = push_v[j]
    own = (4, 5)
    sum_u = {t: [jnp.zeros((8, LANES), f32)] * 2 for t in (3, 4, 5, 6)}
    sum_v = {t: [jnp.zeros((8, LANES), f32)] * 3 for t in own}
    for step in range(SUBSTEPS):
        first = step // STEPS_PER_PHASE
        final = step == SUBSTEPS - 1
        span = range(first, tiles - first)
        for t in span:
            here = slice(8 * t, 8 * t + 8)
            push = load(forcing, 0, t)
            for j in range(3):
                h[t][j] = (keep[0] * h[t][j] + push[j]) - coef[0, j, here, :] * (du[t][j] + dv[t][j])
                if not final:
                    state[0, j, PAD + 8 * t : PAD + 8 * t + 8, :] = h[t][j]
        for t in sum_u:
            sum_u[t] = [keep[1] * sum_u[t][j] + h[t][j] for j in range(2)]
        for t in own:
            sum_v[t] = [keep[2] * sum_v[t][j] + h[t][j] for j in range(3)]
        if final:
            break
        for t in span:
            here = slice(8 * t, 8 * t + 8)
            east, west = eastward(h[t], lane, 2), westward(h[t], lane, 2)
            up, down = load(state, 0, t, 2), load(state, 0, t, -2)
            for j in range(3):
                mid = h[t][j]
                du[t][j] = (keep[1] * du[t][j] + coef[5, j, here, :]) - (
                    coef[1, j, here, :] * (up[j] - mid) - coef[2, j, here, :] * (mid - down[j])
                )
                dv[t][j] = (keep[2] * dv[t][j] + coef[6, j, here, :]) - (
                    coef[3, j, here, :] * (east[j] - mid) - coef[4, j, here, :] * (mid - west[j])
                )

    def decays(c):
        power, total = c, 1.0 + 0.0 * c
        for _ in range(SUBSTEPS - 1):
            total = total + power
            power = power * c
        return power, total

    for t in sum_u:
        for j in range(2):
            state[0, j, PAD + 8 * t : PAD + 8 * t + 8, :] = sum_u[t][j]
    power_u, total_u = decays(keep[1])
    power_v, total_v = decays(keep[2])
    for j in range(2):
        inside = inside_tile(config_ref, 0.0, ROWS, j) * half_b
        for t in own:
            at = PAD + 8 * t
            rows = slice(8 * (t - 4), 8 * (t - 4) + 8)
            factor = inside[rows]
            slope_u = state[0, j, at + 1 : at + 9, :] - state[0, j, at - 1 : at + 7, :]
            slope_v = across(sum_v[t])[j]
            new_u = power_u * state[1, j, at : at + 8, :] + total_u * forcing[1, j, at : at + 8, :] - factor * slope_u
            new_v = power_v * state[2, j, at : at + 8, :] + total_v * forcing[2, j, at : at + 8, :] - factor * slope_v
            cols = slice(j * LANES, (j + 1) * LANES)
            out_ref[0, rows, cols] = h[t][j]
            out_ref[1, rows, cols] = new_u
            out_ref[2, rows, cols] = new_v
    for i in range(TRACERS):
        out_ref[WAVES + i] = tracers_ref[i]
    if not last:
        fields = [out_ref[c] for c in range(FIELDS)]
        received = [received_ref[c] for c in range(FIELDS)]
        write_export(fields, received, land_ref[...].astype(f32), smix_ref, imix_ref, turned, export_ref)


def wave_steps(last, config, mixes, operands):
    state = shaped((FIELDS, ROWS, COLS))
    scratch = [
        pltpu.VMEM((WAVES, 3, 5 * ROWS + 2 * PAD, LANES), f32),
        pltpu.VMEM((WAVES, 3, 5 * ROWS + 2 * PAD, LANES), f32),
        pltpu.VMEM((7, 3, 5 * ROWS, LANES), f32),
    ]
    if not last:
        scratch.append(pltpu.VMEM((2, TURNED, LANES), f32))
    return pl.pallas_call(
        lambda *refs: wave_kernel(last, *refs),
        out_shape=state if last else (state, shaped((TURNED, COLS), bf16)),
        in_specs=[SMEM] * (1 + len(mixes)) + [VMEM] * len(operands),
        out_specs=VMEM if last else (VMEM,) * 2,
        scratch_shapes=scratch,
        compiler_params=params(),
        name="wave_steps_last" if last else "wave_steps",
    )(config, *mixes, *operands)


def line(block, axis, by):
    count = lax.axis_size(axis)
    return lax.ppermute(block, axis, [(i, i + by) for i in range(count) if 0 <= i + by < count])


def local(
    section_state, prev_import, land_mask, state_mix, import_mix, damping, wave_speed,
    remap_owner, remap_slot, remap_weight,
):
    smix = state_mix[0]
    imix = import_mix[0]
    gx = lax.axis_index("gx")
    gy = lax.axis_index("gy")
    place = jnp.stack([gx * ROWS, gy * COLS, lax.axis_size("gx") * ROWS, lax.axis_size("gy") * COLS])
    config = jnp.concatenate([damping[0], wave_speed[0], place.astype(f32)])
    owner = remap_owner[0].reshape(-1)
    slot = remap_slot[0].reshape(-1)
    entry = ((owner - gx + 2) * ROWS + slot // 4) * 2 + (slot % 4) // 2
    second = lax.iota(jnp.int32, owner.shape[0]) % 2
    index = entry + ((slot % 2) ^ second) * (5 * ROWS * 2)

    weight = remap_weight[0].reshape(ROWS, COLS, 128)

    exported, fields, land = export(section_state[0], prev_import[0], land_mask[0], smix, imix)
    for interval in range(ITERS):
        last = interval == ITERS - 1
        opposite = lax.ppermute(exported, "sec", [(0, 1), (1, 0)])
        near = pack(opposite, fields, index, config)
        far_before = line(opposite, "gx", 2)
        far_after = line(opposite, "gx", -2)
        before = line(near, "gx", 1)
        after = line(near, "gx", -1)
        forcing, low, high, received = remap(
            index, (far_before, before, opposite, after, far_after), weight, land, fields
        )
        left = line(high, "gy", 1)
        right = line(low, "gy", -1)
        forward, backward, outer = pack_forcing(forcing, left, right, before, after)
        near_before = line(forward, "gx", 1)
        near_after = line(backward, "gx", -1)
        outer_before = line(outer, "gx", 2)
        outer_after = line(outer, "gx", -2)
        own = (forcing, left, right)
        state = (before, fields, after)
        tracers = tracer_steps(config, (near_before, *own, near_after, *state))
        operands = (outer_before, near_before, *own, near_after, outer_after, *state, tracers)
        if last:
            fields = wave_steps(last, config, (), operands)
        else:
            operands += (received, land)
            fields, exported = wave_steps(last, config, (smix, imix), operands)
    return (fields[None], received[None])


def solution(mesh):
    in_specs = (
        P("sec", None, "gx", "gy"),
        P("sec", None, "gx", "gy"),
        P("sec", "gx", "gy"),
        P("sec", None, None),
        P("sec", None, None),
        P("sec", None),
        P("sec", None),
        P("sec", "gx", "gy", None),
        P("sec", "gx", "gy", None),
        P("sec", "gx", "gy", None, None),
    )
    out_specs = (P("sec", None, "gx", "gy"), P("sec", None, "gx", "gy"))
    return jax.shard_map(local, mesh=mesh, in_specs=in_specs, out_specs=out_specs, check_vma=False)
```

```python
import jax
import jax.numpy as jnp
from jax import lax
from jax.experimental import pallas as pl
from jax.experimental.pallas import tpu as pltpu
from jax.sharding import PartitionSpec as P

SUBSTEPS = 16
ITERS = 2
DIFFUSION = 0.1
COUPLING = 0.2

FIELDS = 8
WAVES = 3
TRACERS = 5
ROWS = 16
COLS = 256
LANES = 128
TURNED = ROWS * FIELDS
STRIP = 32
STEPS_PER_PHASE = 4

A_WAVE = 10
A_EXPORT = 22
A_PLANES = 38
B_WAVE = 12
B_STRIP_T = 28
B_STRIP_W = 30
B_BEHIND = 34
B_PLANES = 46
C_STRIP_W = 16
C_PLANES = 20

PAD = 8
WEIGHT_CHUNKS = 8
WAVE_SPEED = 8
ROW0, COL0, ROW_END, COL_END, NEAR_C, NEAR_I, FAR_C, FAR_I = range(8)
SMEM = pl.BlockSpec(memory_space=pltpu.SMEM)
VMEM = pl.BlockSpec(memory_space=pltpu.VMEM)
HBM = pl.BlockSpec(memory_space=pl.ANY)

f32 = jnp.float32
bf16 = jnp.bfloat16


def params(mib=24):
    return pltpu.CompilerParams(vmem_limit_bytes=mib * 1024 * 1024)


def shaped(shape, dtype=f32):
    return jax.ShapeDtypeStruct(shape, dtype)


def half_of(value, half):
    return value[:, half * LANES : (half + 1) * LANES]


def write_export(fields, received, wet, smix_ref, imix_ref, turned, out_ref):
    scale = wet * jnp.sqrt(1.0 + fields[1] * fields[1] + fields[2] * fields[2])
    for c in range(FIELDS):
        total = smix_ref[c, 0] * fields[0]
        for k in range(1, FIELDS):
            total = total + smix_ref[c, k] * fields[k]
        other = imix_ref[c, 0] * received[0]
        for k in range(1, FIELDS):
            other = other + imix_ref[c, k] * received[k]
        value = scale * (total + other)
        for half in range(2):
            turned[half, pl.ds(c, ROWS, stride=FIELDS), :] = half_of(value, half)
    for half in range(2):
        out_ref[:, half * LANES : (half + 1) * LANES] = turned[half].astype(bf16)


def write_strips(fields, at, low_ref, high_ref):
    lane = lax.broadcasted_iota(jnp.int32, (ROWS, LANES), 1)
    groups = [fields[3:7], [fields[7]] + fields[0:3]]
    for p, group in enumerate(groups):
        first = group[0][0]
        last = pltpu.roll(group[0][1], STRIP, 1)
        for j in range(1, 4):
            here = lane >= STRIP * j
            first = jnp.where(here, pltpu.roll(group[j][0], STRIP * j, 1), first)
            moved = group[j][1] if j == 3 else pltpu.roll(group[j][1], STRIP * (j + 1), 1)
            last = jnp.where(here, moved, last)
        low_ref[at + p] = first
        high_ref[at + p] = last


def export_kernel(
    smix_ref, imix_ref, fields_ref, received_ref, land_ref,
    out_ref, fields_out, land_out, turned, received_buf, sems,
):
    copies = [
        pltpu.make_async_copy(fields_ref, fields_out, sems.at[0]),
        pltpu.make_async_copy(received_ref, received_buf, sems.at[1]),
        pltpu.make_async_copy(land_ref, land_out, sems.at[2]),
    ]
    for copy in copies:
        copy.start()
    for copy in copies:
        copy.wait()
    fields = [fields_out[c] for c in range(FIELDS)]
    received = [received_buf[c] for c in range(FIELDS)]
    write_export(fields, received, land_out[...].astype(f32), smix_ref, imix_ref, turned, out_ref)


def export(fields, received, land, smix, imix):
    return pl.pallas_call(
        export_kernel,
        out_shape=(
            shaped((TURNED, COLS), bf16), shaped((FIELDS, ROWS, COLS)), shaped((ROWS, COLS), jnp.int32),
        ),
        in_specs=[SMEM, SMEM, HBM, HBM, HBM],
        out_specs=(VMEM,) * 3,
        scratch_shapes=[
            pltpu.VMEM((2, TURNED, LANES), f32),
            pltpu.VMEM((FIELDS, ROWS, COLS), f32),
            pltpu.SemaphoreType.DMA((3,)),
        ],
        compiler_params=params(56),
        name="export",
    )(smix, imix, fields, received, land)


def split_to(ref, at, low_at, value):
    high = value.astype(bf16)
    ref[at] = high
    ref[low_at] = (value - high.astype(f32)).astype(bf16)


def write_main(ref, tracer_at, wave_at, wave_low_at, fields_ref):
    for half in range(2):
        cols = slice(half * LANES, (half + 1) * LANES)
        for i in range(TRACERS):
            ref[tracer_at + 2 * i + half] = fields_ref[WAVES + i, :, cols].astype(bf16)
        for i in range(WAVES):
            split_to(ref, wave_at + 2 * i + half, wave_low_at + 2 * i + half, fields_ref[i, :, cols])


def pack_kernel(opposite_ref, fields_ref, index_ref, place_ref, config_ref, near_ref):
    del index_ref, place_ref, config_ref
    write_main(near_ref, 0, A_WAVE, A_WAVE + 6, fields_ref)
    for half in range(2):
        for i in range(TURNED // 16):
            near_ref[A_EXPORT + half * 8 + i] = opposite_ref[16 * i : 16 * i + 16, half * LANES : (half + 1) * LANES]


def pack(opposite, fields, index, place, config):
    return pl.pallas_call(
        pack_kernel,
        out_shape=shaped((A_PLANES, ROWS, LANES), bf16),
        in_specs=[VMEM] * 2 + [HBM] * 3,
        out_specs=VMEM,
        compiler_params=params(),
        name="pack",
    )(opposite, fields, index, place, config)


def pack_forcing_kernel(
    forcing_ref, left_ref, right_ref, state_c_ref, state_i_ref, out_c_ref, out_i_ref, far_ref,
):
    for ref, behind in ((out_c_ref, state_i_ref), (out_i_ref, state_c_ref)):
        write_main(ref, 0, B_WAVE + 2, B_WAVE + 10, forcing_ref)
        for k, strips in enumerate((left_ref, right_ref)):
            ref[10 + k] = strips[0].astype(bf16)
            split_to(ref, B_WAVE + k, B_WAVE + 8 + k, strips[1])
            ref[B_STRIP_T + k] = strips[2].astype(bf16)
            split_to(ref, B_STRIP_W + k, B_STRIP_W + 2 + k, strips[3])
        for p in range(12):
            ref[B_BEHIND + p] = behind[A_WAVE + p]
    for p in range(16):
        far_ref[p] = out_c_ref[B_WAVE + p]
    for p in range(4):
        far_ref[C_STRIP_W + p] = out_c_ref[B_STRIP_W + p]


def pack_forcing(forcing, left, right, state_c, state_i):
    payload = shaped((B_PLANES, ROWS, LANES), bf16)
    return pl.pallas_call(
        pack_forcing_kernel,
        out_shape=(payload, payload, shaped((C_PLANES, ROWS, LANES), bf16)),
        in_specs=[VMEM] * 5,
        out_specs=(VMEM,) * 3,
        compiler_params=params(),
        name="pack_forcing",
    )(forcing, left, right, state_c, state_i)


def remap_kernel(
    index_ref, far_i_ref, near_i_ref, opposite_ref, near_c_ref, far_c_ref, weight_hbm, land_ref, fields_ref,
    forcing_ref, low_ref, high_ref, import_ref, table, turned, weight_ref, sems,
):
    chunk_rows = ROWS // WEIGHT_CHUNKS
    copies = []
    for k in range(WEIGHT_CHUNKS):
        rows = pl.ds(k * chunk_rows, chunk_rows)
        copies.append(pltpu.make_async_copy(weight_hbm.at[rows], weight_ref.at[rows], sems.at[k]))
        copies[k].start()
    half_count = 5 * ROWS * 2
    windows = [far_c_ref, near_c_ref, opposite_ref, near_i_ref, far_i_ref]
    for w, ref in enumerate(windows):
        for half in range(2):
            for i in range(TURNED // 16):
                if w in (1, 3):
                    chunk = ref[A_EXPORT + half * 8 + i]
                else:
                    chunk = ref[16 * i : 16 * i + 16, half * LANES : (half + 1) * LANES]
                chunk = chunk.astype(f32)
                for sub in range(2):
                    part = chunk[sub * 8 : sub * 8 + 8]
                    at = (w * ROWS + i * 2 + sub) * 2 + half
                    table[at] = part
                    table[half_count + at] = pltpu.roll(part, 64, 1)
    lane8 = lax.broadcasted_iota(jnp.int32, (8, LANES), 1)
    low_half = lane8 < 64
    ones = jnp.ones((8, LANES), f32)
    for x in range(ROWS):
        if x % chunk_rows == 0:
            copies[x // chunk_rows].wait()
        pieces = []
        for seg in range(4):
            at = (x * 4 + seg) * 2
            pieces.append(jnp.where(low_half, table[index_ref[at]], table[index_ref[at + 1]]))
        picked = jnp.concatenate(pieces + [ones], axis=0).astype(bf16)
        product = lax.dot_general(
            picked, weight_ref[x], (((1,), (1,)), ((), ())), preferred_element_type=f32
        )
        for half in range(2):
            cols = half_of(product, half)
            summed = jnp.where(low_half, cols[16 * half : 16 * half + 8], cols[16 * half + 8 : 16 * half + 16])
            turned[half, x * 8 : x * 8 + 8, :] = summed / cols[32:40]
    wet = land_ref[...].astype(f32)
    forcing = []
    for c in range(FIELDS):
        parts = []
        for half in range(2):
            value = turned[half, pl.ds(c, ROWS, stride=FIELDS), :]
            import_ref[c, :, half * LANES : (half + 1) * LANES] = value
            part = COUPLING * half_of(wet, half) * value
            forcing_ref[c, :, half * LANES : (half + 1) * LANES] = part
            parts.append(part)
        forcing.append(parts)
    state = [[half_of(fields_ref[c], half) for half in range(2)] for c in range(FIELDS)]
    write_strips(forcing, 0, low_ref, high_ref)
    write_strips(state, 2, low_ref, high_ref)


def remap(index, windows, weight, land, fields):
    strips = shaped((4, ROWS, LANES))
    return pl.pallas_call(
        remap_kernel,
        out_shape=(shaped((FIELDS, ROWS, COLS)), strips, strips, shaped((FIELDS, ROWS, COLS))),
        in_specs=[SMEM] + [VMEM] * 5 + [HBM] + [VMEM] * 2,
        out_specs=(VMEM,) * 4,
        scratch_shapes=[
            pltpu.VMEM((2 * 5 * ROWS * 2, FIELDS, LANES), f32),
            pltpu.VMEM((2, TURNED, LANES), f32),
            pltpu.VMEM((ROWS, COLS, 128), bf16),
            pltpu.SemaphoreType.DMA((WEIGHT_CHUNKS,)),
        ],
        compiler_params=params(52),
        name="remap",
    )(index, *windows, weight, land, fields)


def sides(left, right, j):
    lane = lax.broadcasted_iota(jnp.int32, (ROWS, LANES), 1)
    if j:
        right = pltpu.roll(right, LANES - STRIP * j, 1)
    if j != 3:
        left = pltpu.roll(left, 96 - STRIP * j, 1)
    return jnp.where(lane < STRIP, right, jnp.where(lane >= 96, left, 0.0))


def place_field(dest, start, parts, strip_start=None):
    for j, part in enumerate(parts):
        at = strip_start if j == 2 and strip_start is not None else start
        at = at if isinstance(at, int) else pl.multiple_of(at, 8)
        dest[j, pl.ds(at, ROWS), :] = part


def joined(ref, at, low_at):
    return ref[at].astype(f32) + ref[low_at].astype(f32)


def inside_tile(place_ref, first_row, count, j, shift=0):
    shape = (count, LANES)
    row = lax.broadcasted_iota(jnp.int32, shape, 0) + (place_ref[ROW0] + first_row)
    col = lax.broadcasted_iota(jnp.int32, shape, 1) + j * LANES
    if j == 2:
        col = jnp.where(col >= 3 * LANES - STRIP, col - 3 * LANES, col)
    col = col + (place_ref[COL0] + shift)
    ok = (row >= 0) & (row < place_ref[ROW_END]) & (col >= 0) & (col < place_ref[COL_END])
    return jnp.where(ok, 1.0, 0.0)


def westward(parts, lane, by=1):
    moved = [pltpu.roll(part, by, 1) for part in parts]
    return [jnp.where(lane < by, moved[j - 1], moved[j]) for j in range(3)]


def eastward(parts, lane, by=1):
    moved = [pltpu.roll(part, LANES - by, 1) for part in parts]
    return [jnp.where(lane >= LANES - by, moved[(j + 1) % 3], moved[j]) for j in range(3)]


def own_parts(fields_ref, left_ref, right_ref, at, i):
    p, j = (0, i - WAVES) if WAVES <= i < FIELDS - 1 else (1, (i + 1) % FIELDS)
    return [
        fields_ref[i, :, :LANES], fields_ref[i, :, LANES:], sides(left_ref[at + p], right_ref[at + p], j),
    ]


def tracer_parts(ref, strip_ref, strip_at, wave_strip_at, i):
    at = strip_at if i < 4 else wave_strip_at
    beside = sides(strip_ref[at].astype(f32), strip_ref[at + 1].astype(f32), i % 4)
    return [ref[2 * i].astype(f32), ref[2 * i + 1].astype(f32), beside]


def wave_parts(ref, at, low_at, strip_ref, strip_at, strip_low_at, i):
    first, second = [joined(ref, at + 2 * i + half, low_at + 2 * i + half) for half in range(2)]
    left, right = [joined(strip_ref, strip_at + k, strip_low_at + k) for k in range(2)]
    return [first, second, sides(left, right, i + 1)]


def tracer_kernel(
    place_ref, config_ref, near_c_ref, forcing_ref, left_ref, right_ref, near_i_ref,
    state_c_ref, fields_ref, state_i_ref, out_ref, state, forcing, coef,
):
    pairs = (
        ((place_ref[NEAR_C] - 1) * ROWS, near_c_ref, state_c_ref),
        ((place_ref[NEAR_I] - 1) * ROWS, near_i_ref, state_i_ref),
        (ROWS, None, None),
    )
    for start, near, main in pairs:
        for i in range(TRACERS):
            if near is None:
                pushed = own_parts(forcing_ref, left_ref, right_ref, 0, WAVES + i)
                parts = own_parts(fields_ref, left_ref, right_ref, 2, WAVES + i)
            else:
                pushed = tracer_parts(near, near, 10, B_WAVE, i)
                parts = tracer_parts(main, near, B_STRIP_T, B_STRIP_W, i)
            place_field(forcing.at[i], start, pushed)
            place_field(state.at[0, i], start + PAD, parts)
    height = 3 * ROWS
    for k in range(2):
        for i in range(TRACERS):
            for j in range(3):
                state[k, i, j, 0:PAD, :] = jnp.zeros((PAD, LANES), f32)
                state[k, i, j, PAD + height : height + 2 * PAD, :] = jnp.zeros((PAD, LANES), f32)
    for j in range(3):
        coef[j] = inside_tile(place_ref, -ROWS, height, j) * DIFFUSION

    lane = lax.broadcasted_iota(jnp.int32, (8, LANES), 1)
    keep = [(1.0 - config_ref[WAVES + c]) - 4.0 * DIFFUSION for c in range(TRACERS)]

    def step(source, dest, first, count):
        for t in range(first, first + count):
            at = PAD + 8 * t
            here = slice(8 * t, 8 * t + 8)
            for c in range(TRACERS):
                mid = [state[source, c, j, at : at + 8, :] for j in range(3)]
                west = westward(mid, lane)
                east = eastward(mid, lane)
                for j in range(3):
                    above = state[source, c, j, at + 1 : at + 9, :]
                    below = state[source, c, j, at - 1 : at + 7, :]
                    around = (above + below) + (east[j] + west[j])
                    state[dest, c, j, at : at + 8, :] = (
                        keep[c] * mid[j] + forcing[c, j, here, :]
                    ) + coef[j, here, :] * around

    def pair_of_steps(first, count):
        def run(_, carry):
            step(0, 1, first, count)
            step(1, 0, first, count)
            return carry
        return run

    lax.fori_loop(0, SUBSTEPS // 4, pair_of_steps(0, 6), 0)
    lax.fori_loop(0, SUBSTEPS // 4, pair_of_steps(1, 4), 0)
    for i in range(TRACERS):
        for half in range(2):
            out_ref[i, :, half * LANES : (half + 1) * LANES] = state[0, i, half, PAD + ROWS : PAD + 2 * ROWS, :]


def tracer_steps(place, config, operands):
    return pl.pallas_call(
        tracer_kernel,
        out_shape=shaped((TRACERS, ROWS, COLS)),
        in_specs=[SMEM] * 2 + [VMEM] * len(operands),
        out_specs=VMEM,
        scratch_shapes=[
            pltpu.VMEM((2, TRACERS, 3, 3 * ROWS + 2 * PAD, LANES), f32),
            pltpu.VMEM((TRACERS, 3, 3 * ROWS, LANES), f32),
            pltpu.VMEM((3, 3 * ROWS, LANES), f32),
        ],
        compiler_params=params(),
        cost_estimate=pl.CostEstimate(flops=10_000_000, bytes_accessed=4_000_000, transcendentals=0),
        name="tracer_steps",
    )(place, config, *operands)


def wave_kernel(last, place_ref, config_ref, *refs):
    if not last:
        smix_ref, imix_ref, *refs = refs
    (far_i, near_c, forcing_ref, left_ref, right_ref, near_i, far_c,
     state_c, fields_ref, state_i, tracers_ref, *refs) = refs
    if last:
        out_ref, state, forcing, coef = refs
    else:
        received_ref, land_ref, out_ref, export_ref, state, forcing, coef, turned = refs
    height = 5 * ROWS
    tiles = height // 8

    row_of = {k: PAD + place_ref[k] * ROWS for k in (NEAR_C, NEAR_I, FAR_C, FAR_I)}
    for i in range(WAVES):
        place_field(forcing.at[i], PAD + 2 * ROWS, own_parts(forcing_ref, left_ref, right_ref, 0, i))
        place_field(state.at[i], PAD + 2 * ROWS, own_parts(fields_ref, left_ref, right_ref, 2, i))
        for near, main, at in ((near_c, state_c, row_of[NEAR_C]), (near_i, state_i, row_of[NEAR_I])):
            pushed = wave_parts(near, B_WAVE + 2, B_WAVE + 10, near, B_WAVE, B_WAVE + 8, i)
            place_field(forcing.at[i], at, pushed)
            place_field(state.at[i], at, wave_parts(main, A_WAVE, A_WAVE + 6, near, B_STRIP_W, B_STRIP_W + 2, i))
        for far, near, at, main_at in (
            (far_c, near_c, row_of[FAR_C], 2 * row_of[NEAR_C] - (PAD + 2 * ROWS)),
            (far_i, near_i, row_of[FAR_I], 2 * row_of[NEAR_I] - (PAD + 2 * ROWS)),
        ):
            place_field(forcing.at[i], at, wave_parts(far, 2, 10, far, 0, 8, i))
            parts = wave_parts(near, B_BEHIND, B_BEHIND + 6, far, C_STRIP_W, C_STRIP_W + 2, i)
            place_field(state.at[i], main_at, parts, at)
        for j in range(3):
            for ref in (state, forcing):
                ref[i, j, 0:PAD, :] = jnp.zeros((PAD, LANES), f32)
                ref[i, j, PAD + height : height + 2 * PAD, :] = jnp.zeros((PAD, LANES), f32)
    half_a = 0.5 * config_ref[WAVE_SPEED]
    half_b = 0.5 * config_ref[WAVE_SPEED + 1]
    first_row = -2 * ROWS
    for j in range(3):
        coef[0, j] = inside_tile(place_ref, first_row, height, j) * half_a
        coef[1, j] = inside_tile(place_ref, first_row + 1, height, j) * half_b
        coef[2, j] = inside_tile(place_ref, first_row - 1, height, j) * half_b
        coef[3, j] = inside_tile(place_ref, first_row, height, j, 1) * half_b
        coef[4, j] = inside_tile(place_ref, first_row, height, j, -1) * half_b

    lane = lax.broadcasted_iota(jnp.int32, (8, LANES), 1)
    keep = [1.0 - config_ref[c] for c in range(WAVES)]

    def load(ref, i, t, by=0):
        at = PAD + 8 * t + by
        return [ref[i, j, at : at + 8, :] for j in range(3)]

    def along(ref, i, t):
        ahead, behind = load(ref, i, t, 1), load(ref, i, t, -1)
        return [ahead[j] - behind[j] for j in range(3)]

    def across(parts):
        ahead, behind = eastward(parts, lane), westward(parts, lane)
        return [ahead[j] - behind[j] for j in range(3)]

    h = [load(state, 0, t) for t in range(tiles)]
    du = [along(state, 1, t) for t in range(tiles)]
    dv = [across(load(state, 2, t)) for t in range(tiles)]
    for t in range(tiles):
        at = PAD + 8 * t
        push_u, push_v = along(forcing, 1, t), across(load(forcing, 2, t))
        for j in range(3):
            coef[5, j, 8 * t : 8 * t + 8, :] = push_u[j]
            coef[6, j, 8 * t : 8 * t + 8, :] = push_v[j]
    own = (4, 5)
    sum_u = {t: [jnp.zeros((8, LANES), f32)] * 2 for t in (3, 4, 5, 6)}
    sum_v = {t: [jnp.zeros((8, LANES), f32)] * 3 for t in own}
    for step in range(SUBSTEPS):
        first = step // STEPS_PER_PHASE
        final = step == SUBSTEPS - 1
        span = range(first, tiles - first)
        for t in span:
            here = slice(8 * t, 8 * t + 8)
            push = load(forcing, 0, t)
            for j in range(3):
                h[t][j] = (keep[0] * h[t][j] + push[j]) - coef[0, j, here, :] * (du[t][j] + dv[t][j])
                if not final:
                    state[0, j, PAD + 8 * t : PAD + 8 * t + 8, :] = h[t][j]
        for t in sum_u:
            sum_u[t] = [keep[1] * sum_u[t][j] + h[t][j] for j in range(2)]
        for t in own:
            sum_v[t] = [keep[2] * sum_v[t][j] + h[t][j] for j in range(3)]
        if final:
            break
        for t in span:
            here = slice(8 * t, 8 * t + 8)
            east, west = eastward(h[t], lane, 2), westward(h[t], lane, 2)
            up, down = load(state, 0, t, 2), load(state, 0, t, -2)
            for j in range(3):
                mid = h[t][j]
                du[t][j] = (keep[1] * du[t][j] + coef[5, j, here, :]) - (
                    coef[1, j, here, :] * (up[j] - mid) - coef[2, j, here, :] * (mid - down[j])
                )
                dv[t][j] = (keep[2] * dv[t][j] + coef[6, j, here, :]) - (
                    coef[3, j, here, :] * (east[j] - mid) - coef[4, j, here, :] * (mid - west[j])
                )

    def decays(c):
        power, total = c, 1.0 + 0.0 * c
        for _ in range(SUBSTEPS - 1):
            total = total + power
            power = power * c
        return power, total

    for t in sum_u:
        for j in range(2):
            state[0, j, PAD + 8 * t : PAD + 8 * t + 8, :] = sum_u[t][j]
    power_u, total_u = decays(keep[1])
    power_v, total_v = decays(keep[2])
    for j in range(2):
        inside = inside_tile(place_ref, 0, ROWS, j) * half_b
        for t in own:
            at = PAD + 8 * t
            rows = slice(8 * (t - 4), 8 * (t - 4) + 8)
            factor = inside[rows]
            slope_u = state[0, j, at + 1 : at + 9, :] - state[0, j, at - 1 : at + 7, :]
            slope_v = across(sum_v[t])[j]
            new_u = power_u * state[1, j, at : at + 8, :] + total_u * forcing[1, j, at : at + 8, :] - factor * slope_u
            new_v = power_v * state[2, j, at : at + 8, :] + total_v * forcing[2, j, at : at + 8, :] - factor * slope_v
            cols = slice(j * LANES, (j + 1) * LANES)
            out_ref[0, rows, cols] = h[t][j]
            out_ref[1, rows, cols] = new_u
            out_ref[2, rows, cols] = new_v
    for i in range(TRACERS):
        out_ref[WAVES + i] = tracers_ref[i]
    if not last:
        fields = [out_ref[c] for c in range(FIELDS)]
        received = [received_ref[c] for c in range(FIELDS)]
        write_export(fields, received, land_ref[...].astype(f32), smix_ref, imix_ref, turned, export_ref)


def wave_steps(last, place, config, mixes, operands):
    state = shaped((FIELDS, ROWS, COLS))
    scratch = [
        pltpu.VMEM((WAVES, 3, 5 * ROWS + 2 * PAD, LANES), f32),
        pltpu.VMEM((WAVES, 3, 5 * ROWS + 2 * PAD, LANES), f32),
        pltpu.VMEM((7, 3, 5 * ROWS, LANES), f32),
    ]
    if not last:
        scratch.append(pltpu.VMEM((2, TURNED, LANES), f32))
    return pl.pallas_call(
        lambda *refs: wave_kernel(last, *refs),
        out_shape=state if last else (state, shaped((TURNED, COLS), bf16)),
        in_specs=[SMEM] * (2 + len(mixes)) + [VMEM] * len(operands),
        out_specs=VMEM if last else (VMEM,) * 2,
        scratch_shapes=scratch,
        compiler_params=params(),
        name="wave_steps_last" if last else "wave_steps",
    )(place, config, *mixes, *operands)


def line(block, axis, by):
    count = lax.axis_size(axis)
    return lax.ppermute(block, axis, [(i, i + by) for i in range(count) if 0 <= i + by < count])


def exchanged(block, distance, phase):
    count = lax.axis_size("gx")
    route = []
    for low in range(count - distance):
        if (low // distance) % 2 == phase:
            route += [(low, low + distance), (low + distance, low)]
    return lax.ppermute(block, "gx", route)


def local(
    section_state, prev_import, land_mask, state_mix, import_mix, damping, wave_speed,
    remap_owner, remap_slot, remap_weight,
):
    smix = state_mix[0]
    imix = import_mix[0]
    gx = lax.axis_index("gx")
    gy = lax.axis_index("gy")
    side_near = 1 - 2 * (gx % 2)
    side_far = 1 - 2 * ((gx // 2) % 2)
    place = jnp.stack([
        gx * ROWS, gy * COLS, lax.axis_size("gx") * ROWS, lax.axis_size("gy") * COLS,
        2 - side_near, 2 + side_near, 2 - 2 * side_far, 2 + 2 * side_far,
    ]).astype(jnp.int32)
    config = jnp.concatenate([damping[0], wave_speed[0]])
    owner = remap_owner[0].reshape(-1)
    slot = remap_slot[0].reshape(-1)
    away = owner - gx
    window = 2 + away * jnp.where(away % 2 == 1, side_near, side_far)
    entry = (window * ROWS + slot // 4) * 2 + (slot % 4) // 2
    second = lax.iota(jnp.int32, owner.shape[0]) % 2
    index = entry + ((slot % 2) ^ second) * (5 * ROWS * 2)
    weight = remap_weight[0].reshape(ROWS, COLS, 128)

    exported, fields, land = export(section_state[0], prev_import[0], land_mask[0], smix, imix)
    for interval in range(ITERS):
        last = interval == ITERS - 1
        opposite = lax.ppermute(exported, "sec", [(0, 1), (1, 0)])
        near = pack(opposite, fields, index, place, config)
        state_c = exchanged(near, 1, 1)
        state_i = exchanged(near, 1, 0)
        export_c = exchanged(opposite, 2, 1)
        export_i = exchanged(opposite, 2, 0)
        forcing, low, high, received = remap(
            index, (export_i, state_i, opposite, state_c, export_c), weight, land, fields
        )
        left = line(high, "gy", 1)
        right = line(low, "gy", -1)
        out_c, out_i, outer = pack_forcing(forcing, left, right, state_c, state_i)
        near_c = exchanged(out_c, 1, 1)
        near_i = exchanged(out_i, 1, 0)
        far_c = exchanged(outer, 2, 1)
        far_i = exchanged(outer, 2, 0)
        own = (forcing, left, right)
        state = (state_c, fields, state_i)
        tracers = tracer_steps(place, config, (near_c, *own, near_i, *state))
        operands = (far_i, near_c, *own, near_i, far_c, *state, tracers)
        if last:
            fields = wave_steps(last, place, config, (), operands)
        else:
            operands += (received, land)
            fields, exported = wave_steps(last, place, config, (smix, imix), operands)
    return (fields[None], received[None])


def solution(mesh):
    in_specs = (
        P("sec", None, "gx", "gy"),
        P("sec", None, "gx", "gy"),
        P("sec", "gx", "gy"),
        P("sec", None, None),
        P("sec", None, None),
        P("sec", None),
        P("sec", None),
        P("sec", "gx", "gy", None),
        P("sec", "gx", "gy", None),
        P("sec", "gx", "gy", None, None),
    )
    out_specs = (P("sec", None, "gx", "gy"), P("sec", None, "gx", "gy"))
    return jax.shard_map(local, mesh=mesh, in_specs=in_specs, out_specs=out_specs, check_vma=False)
```

```python
import jax
import jax.numpy as jnp
from jax import lax
from jax.experimental import pallas as pl
from jax.experimental.pallas import tpu as pltpu
from jax.sharding import PartitionSpec as P

SUBSTEPS = 16
ITERS = 2
DIFFUSION = 0.1
COUPLING = 0.2

FIELDS = 8
WAVES = 3
TRACERS = 5
ROWS = 16
COLS = 256
LANES = 128
TURNED = ROWS * FIELDS
STRIP = 32
STEPS_PER_PHASE = 4

A_WAVE = 10
A_EXPORT = 22
A_PLANES = 38
B_WAVE = 12
B_STRIP_T = 28
B_STRIP_W = 30
B_BEHIND = 34
B_PLANES = 46
C_STRIP_W = 16
C_PLANES = 20

PAD = 8
WAVE_SPEED = 8
ROW0, COL0, ROW_END, COL_END, NEAR_C, NEAR_I, FAR_C, FAR_I, GY_ODD = range(9)
SMEM = pl.BlockSpec(memory_space=pltpu.SMEM)
VMEM = pl.BlockSpec(memory_space=pltpu.VMEM)
HBM = pl.BlockSpec(memory_space=pl.ANY)

f32 = jnp.float32
bf16 = jnp.bfloat16


def params(mib=24):
    return pltpu.CompilerParams(vmem_limit_bytes=mib * 1024 * 1024)


def shaped(shape, dtype=f32):
    return jax.ShapeDtypeStruct(shape, dtype)


def half_of(value, half):
    return value[:, half * LANES : (half + 1) * LANES]


def write_export(fields, received, wet, smix_ref, imix_ref, turned, out_ref):
    scale = wet * jnp.sqrt(1.0 + fields[1] * fields[1] + fields[2] * fields[2])
    for c in range(FIELDS):
        total = smix_ref[c, 0] * fields[0]
        for k in range(1, FIELDS):
            total = total + smix_ref[c, k] * fields[k]
        other = imix_ref[c, 0] * received[0]
        for k in range(1, FIELDS):
            other = other + imix_ref[c, k] * received[k]
        value = scale * (total + other)
        for half in range(2):
            turned[half, pl.ds(c, ROWS, stride=FIELDS), :] = half_of(value, half)
    for half in range(2):
        out_ref[:, half * LANES : (half + 1) * LANES] = turned[half].astype(bf16)


def write_strips(fields, at, odd, chip_ref, outer_ref):
    lane = lax.broadcasted_iota(jnp.int32, (ROWS, LANES), 1)
    groups = [fields[3:7], [fields[7]] + fields[0:3]]
    for p, group in enumerate(groups):
        first = group[0][0]
        last = pltpu.roll(group[0][1], STRIP, 1)
        for j in range(1, 4):
            here = lane >= STRIP * j
            first = jnp.where(here, pltpu.roll(group[j][0], STRIP * j, 1), first)
            moved = group[j][1] if j == 3 else pltpu.roll(group[j][1], STRIP * (j + 1), 1)
            last = jnp.where(here, moved, last)
        chip_ref[at + p] = jnp.where(odd, first, last)
        outer_ref[at + p] = jnp.where(odd, last, first)


def export_kernel(
    smix_ref, imix_ref, fields_ref, received_ref, land_ref,
    out_ref, fields_out, land_out, turned, received_buf, sems,
):
    copies = [
        pltpu.make_async_copy(fields_ref, fields_out, sems.at[0]),
        pltpu.make_async_copy(received_ref, received_buf, sems.at[1]),
        pltpu.make_async_copy(land_ref, land_out, sems.at[2]),
    ]
    for copy in copies:
        copy.start()
    for copy in copies:
        copy.wait()
    fields = [fields_out[c] for c in range(FIELDS)]
    received = [received_buf[c] for c in range(FIELDS)]
    write_export(fields, received, land_out[...].astype(f32), smix_ref, imix_ref, turned, out_ref)


def export(fields, received, land, smix, imix):
    return pl.pallas_call(
        export_kernel,
        out_shape=(
            shaped((TURNED, COLS), bf16), shaped((FIELDS, ROWS, COLS)), shaped((ROWS, COLS), jnp.int32),
        ),
        in_specs=[SMEM, SMEM, HBM, HBM, HBM],
        out_specs=(VMEM,) * 3,
        scratch_shapes=[
            pltpu.VMEM((2, TURNED, LANES), f32),
            pltpu.VMEM((FIELDS, ROWS, COLS), f32),
            pltpu.SemaphoreType.DMA((3,)),
        ],
        compiler_params=params(56),
        name="export",
    )(smix, imix, fields, received, land)


def split_to(ref, at, low_at, value):
    high = value.astype(bf16)
    ref[at] = high
    ref[low_at] = (value - high.astype(f32)).astype(bf16)


def write_main(ref, tracer_at, wave_at, wave_low_at, fields_ref):
    for half in range(2):
        cols = slice(half * LANES, (half + 1) * LANES)
        for i in range(TRACERS):
            ref[tracer_at + 2 * i + half] = fields_ref[WAVES + i, :, cols].astype(bf16)
        for i in range(WAVES):
            split_to(ref, wave_at + 2 * i + half, wave_low_at + 2 * i + half, fields_ref[i, :, cols])


def pack_kernel(opposite_ref, fields_ref, index_ref, place_ref, config_ref, near_ref):
    del index_ref, place_ref, config_ref
    write_main(near_ref, 0, A_WAVE, A_WAVE + 6, fields_ref)
    for half in range(2):
        for i in range(TURNED // 16):
            near_ref[A_EXPORT + half * 8 + i] = opposite_ref[16 * i : 16 * i + 16, half * LANES : (half + 1) * LANES]


def pack(opposite, fields, index, place, config):
    return pl.pallas_call(
        pack_kernel,
        out_shape=shaped((A_PLANES, ROWS, LANES), bf16),
        in_specs=[VMEM] * 2 + [HBM] * 3,
        out_specs=VMEM,
        compiler_params=params(),
        name="pack",
    )(opposite, fields, index, place, config)


def pack_forcing_kernel(
    place_ref, forcing_ref, outer_ref, chip_ref, state_c_ref, state_i_ref,
    out_c_ref, out_i_ref, far_ref, left_ref, right_ref,
):
    odd = place_ref[GY_ODD] == 1
    left_ref[...] = jnp.where(odd, chip_ref[...], outer_ref[...])
    right_ref[...] = jnp.where(odd, outer_ref[...], chip_ref[...])
    for ref, behind in ((out_c_ref, state_i_ref), (out_i_ref, state_c_ref)):
        write_main(ref, 0, B_WAVE + 2, B_WAVE + 10, forcing_ref)
        for k, strips in enumerate((left_ref, right_ref)):
            ref[10 + k] = strips[0].astype(bf16)
            split_to(ref, B_WAVE + k, B_WAVE + 8 + k, strips[1])
            ref[B_STRIP_T + k] = strips[2].astype(bf16)
            split_to(ref, B_STRIP_W + k, B_STRIP_W + 2 + k, strips[3])
        for p in range(12):
            ref[B_BEHIND + p] = behind[A_WAVE + p]
    for p in range(16):
        far_ref[p] = out_c_ref[B_WAVE + p]
    for p in range(4):
        far_ref[C_STRIP_W + p] = out_c_ref[B_STRIP_W + p]


def pack_forcing(place, forcing, outer, chip, state_c, state_i):
    payload, strips = shaped((B_PLANES, ROWS, LANES), bf16), shaped((4, ROWS, LANES))
    return pl.pallas_call(
        pack_forcing_kernel,
        out_shape=(payload, payload, shaped((C_PLANES, ROWS, LANES), bf16), strips, strips),
        in_specs=[SMEM] + [VMEM] * 5,
        out_specs=(VMEM,) * 5,
        compiler_params=params(),
        name="pack_forcing",
    )(place, forcing, outer, chip, state_c, state_i)


def stage_kernel(weight_ref, near_c_ref, near_i_ref, out_ref):
    del near_c_ref, near_i_ref
    out_ref[...] = weight_ref[...]


def stage(weight, near_c, near_i):
    return pl.pallas_call(
        stage_kernel,
        out_shape=shaped(weight.shape, weight.dtype),
        in_specs=[VMEM, HBM, HBM],
        out_specs=VMEM,
        compiler_params=params(),
        name="stage_weights",
    )(weight, near_c, near_i)


def remap_kernel(
    index_ref, far_i_ref, near_i_ref, opposite_ref, near_c_ref, far_c_ref, weight_ref, land_ref, fields_ref,
    forcing_ref, chip_ref, outer_ref, import_ref, table, turned,
):
    half_count = 5 * ROWS * 2
    windows = [far_c_ref, near_c_ref, opposite_ref, near_i_ref, far_i_ref]
    for w, ref in enumerate(windows):
        for half in range(2):
            for i in range(TURNED // 16):
                if w in (1, 3):
                    chunk = ref[A_EXPORT + half * 8 + i]
                else:
                    chunk = ref[16 * i : 16 * i + 16, half * LANES : (half + 1) * LANES]
                chunk = chunk.astype(f32)
                for sub in range(2):
                    part = chunk[sub * 8 : sub * 8 + 8]
                    at = (w * ROWS + i * 2 + sub) * 2 + half
                    table[at] = part
                    table[half_count + at] = pltpu.roll(part, 64, 1)
    lane8 = lax.broadcasted_iota(jnp.int32, (8, LANES), 1)
    low_half = lane8 < 64
    ones = jnp.ones((8, LANES), f32)
    for x in range(ROWS):
        pieces = []
        for seg in range(4):
            at = (x * 4 + seg) * 2
            pieces.append(jnp.where(low_half, table[index_ref[at]], table[index_ref[at + 1]]))
        picked = jnp.concatenate(pieces + [ones], axis=0).astype(bf16)
        product = lax.dot_general(
            picked, weight_ref[x], (((1,), (1,)), ((), ())), preferred_element_type=f32
        )
        for half in range(2):
            cols = half_of(product, half)
            summed = jnp.where(low_half, cols[16 * half : 16 * half + 8], cols[16 * half + 8 : 16 * half + 16])
            turned[half, x * 8 : x * 8 + 8, :] = summed / cols[32:40]
    wet = land_ref[...].astype(f32)
    forcing = []
    for c in range(FIELDS):
        parts = []
        for half in range(2):
            value = turned[half, pl.ds(c, ROWS, stride=FIELDS), :]
            import_ref[c, :, half * LANES : (half + 1) * LANES] = value
            part = COUPLING * half_of(wet, half) * value
            forcing_ref[c, :, half * LANES : (half + 1) * LANES] = part
            parts.append(part)
        forcing.append(parts)
    state = [[half_of(fields_ref[c], half) for half in range(2)] for c in range(FIELDS)]
    odd = index_ref[TURNED] == 1
    write_strips(forcing, 0, odd, chip_ref, outer_ref)
    write_strips(state, 2, odd, chip_ref, outer_ref)


def remap(index, windows, weight, land, fields):
    strips = shaped((4, ROWS, LANES))
    return pl.pallas_call(
        remap_kernel,
        out_shape=(shaped((FIELDS, ROWS, COLS)), strips, strips, shaped((FIELDS, ROWS, COLS))),
        in_specs=[SMEM] + [VMEM] * 8,
        out_specs=(VMEM,) * 4,
        scratch_shapes=[
            pltpu.VMEM((2 * 5 * ROWS * 2, FIELDS, LANES), f32),
            pltpu.VMEM((2, TURNED, LANES), f32),
        ],
        compiler_params=params(),
        name="remap",
    )(index, *windows, weight, land, fields)


def sides(left, right, j):
    lane = lax.broadcasted_iota(jnp.int32, (ROWS, LANES), 1)
    if j:
        right = pltpu.roll(right, LANES - STRIP * j, 1)
    if j != 3:
        left = pltpu.roll(left, 96 - STRIP * j, 1)
    return jnp.where(lane < STRIP, right, jnp.where(lane >= 96, left, 0.0))


def place_field(dest, start, parts, strip_start=None):
    for j, part in enumerate(parts):
        at = strip_start if j == 2 and strip_start is not None else start
        at = at if isinstance(at, int) else pl.multiple_of(at, 8)
        dest[j, pl.ds(at, ROWS), :] = part


def joined(ref, at, low_at):
    return ref[at].astype(f32) + ref[low_at].astype(f32)


def inside_tile(place_ref, first_row, count, j, shift=0):
    shape = (count, LANES)
    row = lax.broadcasted_iota(jnp.int32, shape, 0) + (place_ref[ROW0] + first_row)
    col = lax.broadcasted_iota(jnp.int32, shape, 1) + j * LANES
    if j == 2:
        col = jnp.where(col >= 3 * LANES - STRIP, col - 3 * LANES, col)
    col = col + (place_ref[COL0] + shift)
    ok = (row >= 0) & (row < place_ref[ROW_END]) & (col >= 0) & (col < place_ref[COL_END])
    return jnp.where(ok, 1.0, 0.0)


def westward(parts, lane, by=1):
    moved = [pltpu.roll(part, by, 1) for part in parts]
    return [jnp.where(lane < by, moved[j - 1], moved[j]) for j in range(3)]


def eastward(parts, lane, by=1):
    moved = [pltpu.roll(part, LANES - by, 1) for part in parts]
    return [jnp.where(lane >= LANES - by, moved[(j + 1) % 3], moved[j]) for j in range(3)]


def own_parts(fields_ref, left_ref, right_ref, at, i):
    p, j = (0, i - WAVES) if WAVES <= i < FIELDS - 1 else (1, (i + 1) % FIELDS)
    return [
        fields_ref[i, :, :LANES], fields_ref[i, :, LANES:], sides(left_ref[at + p], right_ref[at + p], j),
    ]


def tracer_parts(ref, strip_ref, strip_at, wave_strip_at, i):
    at = strip_at if i < 4 else wave_strip_at
    beside = sides(strip_ref[at].astype(f32), strip_ref[at + 1].astype(f32), i % 4)
    return [ref[2 * i].astype(f32), ref[2 * i + 1].astype(f32), beside]


def wave_parts(ref, at, low_at, strip_ref, strip_at, strip_low_at, i):
    first, second = [joined(ref, at + 2 * i + half, low_at + 2 * i + half) for half in range(2)]
    left, right = [joined(strip_ref, strip_at + k, strip_low_at + k) for k in range(2)]
    return [first, second, sides(left, right, i + 1)]


def tracer_kernel(
    last, place_ref, config_ref, near_c_ref, forcing_ref, left_ref, right_ref, near_i_ref,
    state_c_ref, fields_ref, state_i_ref, *refs
):
    if last:
        received_ref, out_ref, received_out, state, forcing, coef = refs
        received_out[...] = received_ref[...]
    else:
        out_ref, state, forcing, coef = refs
    pairs = (
        ((place_ref[NEAR_C] - 1) * ROWS, near_c_ref, state_c_ref),
        ((place_ref[NEAR_I] - 1) * ROWS, near_i_ref, state_i_ref),
        (ROWS, None, None),
    )
    for start, near, main in pairs:
        for i in range(TRACERS):
            if near is None:
                pushed = own_parts(forcing_ref, left_ref, right_ref, 0, WAVES + i)
                parts = own_parts(fields_ref, left_ref, right_ref, 2, WAVES + i)
            else:
                pushed = tracer_parts(near, near, 10, B_WAVE, i)
                parts = tracer_parts(main, near, B_STRIP_T, B_STRIP_W, i)
            place_field(forcing.at[i], start, pushed)
            place_field(state.at[0, i], start + PAD, parts)
    height = 3 * ROWS
    for k in range(2):
        for i in range(TRACERS):
            for j in range(3):
                state[k, i, j, 0:PAD, :] = jnp.zeros((PAD, LANES), f32)
                state[k, i, j, PAD + height : height + 2 * PAD, :] = jnp.zeros((PAD, LANES), f32)
    for j in range(3):
        coef[j] = inside_tile(place_ref, -ROWS, height, j) * DIFFUSION

    lane = lax.broadcasted_iota(jnp.int32, (8, LANES), 1)
    keep = [(1.0 - config_ref[WAVES + c]) - 4.0 * DIFFUSION for c in range(TRACERS)]

    def step(source, dest, first, count):
        for t in range(first, first + count):
            at = PAD + 8 * t
            here = slice(8 * t, 8 * t + 8)
            for c in range(TRACERS):
                mid = [state[source, c, j, at : at + 8, :] for j in range(3)]
                west = westward(mid, lane)
                east = eastward(mid, lane)
                for j in range(3):
                    above = state[source, c, j, at + 1 : at + 9, :]
                    below = state[source, c, j, at - 1 : at + 7, :]
                    around = (above + below) + (east[j] + west[j])
                    state[dest, c, j, at : at + 8, :] = (
                        keep[c] * mid[j] + forcing[c, j, here, :]
                    ) + coef[j, here, :] * around

    def pair_of_steps(first, count):
        def run(_, carry):
            step(0, 1, first, count)
            step(1, 0, first, count)
            return carry
        return run

    lax.fori_loop(0, SUBSTEPS // 4, pair_of_steps(0, 6), 0)
    lax.fori_loop(0, SUBSTEPS // 4, pair_of_steps(1, 4), 0)
    for i in range(TRACERS):
        for half in range(2):
            out_ref[i, :, half * LANES : (half + 1) * LANES] = state[0, i, half, PAD + ROWS : PAD + 2 * ROWS, :]


def tracer_steps(last, place, config, operands):
    tracers, received = shaped((TRACERS, ROWS, COLS)), shaped((FIELDS, ROWS, COLS))
    return pl.pallas_call(
        lambda *refs: tracer_kernel(last, *refs),
        out_shape=(tracers, received) if last else tracers,
        in_specs=[SMEM] * 2 + [VMEM] * len(operands),
        out_specs=(VMEM, VMEM) if last else VMEM,
        scratch_shapes=[
            pltpu.VMEM((2, TRACERS, 3, 3 * ROWS + 2 * PAD, LANES), f32),
            pltpu.VMEM((TRACERS, 3, 3 * ROWS, LANES), f32),
            pltpu.VMEM((3, 3 * ROWS, LANES), f32),
        ],
        compiler_params=params(),
        cost_estimate=pl.CostEstimate(flops=10_000_000, bytes_accessed=4_000_000, transcendentals=0),
        name="tracer_steps",
    )(place, config, *operands)


def wave_kernel(last, place_ref, config_ref, *refs):
    if not last:
        smix_ref, imix_ref, *refs = refs
    (far_i, near_c, forcing_ref, left_ref, right_ref, near_i, far_c,
     state_c, fields_ref, state_i, tracers_ref, *refs) = refs
    if last:
        out_ref, state, forcing, coef = refs
    else:
        received_ref, land_ref, out_ref, export_ref, state, forcing, coef, turned = refs
    height = 5 * ROWS
    tiles = height // 8

    row_of = {k: PAD + place_ref[k] * ROWS for k in (NEAR_C, NEAR_I, FAR_C, FAR_I)}
    for i in range(WAVES):
        place_field(forcing.at[i], PAD + 2 * ROWS, own_parts(forcing_ref, left_ref, right_ref, 0, i))
        place_field(state.at[i], PAD + 2 * ROWS, own_parts(fields_ref, left_ref, right_ref, 2, i))
        for near, main, at in ((near_c, state_c, row_of[NEAR_C]), (near_i, state_i, row_of[NEAR_I])):
            pushed = wave_parts(near, B_WAVE + 2, B_WAVE + 10, near, B_WAVE, B_WAVE + 8, i)
            place_field(forcing.at[i], at, pushed)
            place_field(state.at[i], at, wave_parts(main, A_WAVE, A_WAVE + 6, near, B_STRIP_W, B_STRIP_W + 2, i))
        for far, near, at, main_at in (
            (far_c, near_c, row_of[FAR_C], 2 * row_of[NEAR_C] - (PAD + 2 * ROWS)),
            (far_i, near_i, row_of[FAR_I], 2 * row_of[NEAR_I] - (PAD + 2 * ROWS)),
        ):
            place_field(forcing.at[i], at, wave_parts(far, 2, 10, far, 0, 8, i))
            parts = wave_parts(near, B_BEHIND, B_BEHIND + 6, far, C_STRIP_W, C_STRIP_W + 2, i)
            place_field(state.at[i], main_at, parts, at)
        for j in range(3):
            for ref in (state, forcing):
                ref[i, j, 0:PAD, :] = jnp.zeros((PAD, LANES), f32)
                ref[i, j, PAD + height : height + 2 * PAD, :] = jnp.zeros((PAD, LANES), f32)
    half_a = 0.5 * config_ref[WAVE_SPEED]
    half_b = 0.5 * config_ref[WAVE_SPEED + 1]
    first_row = -2 * ROWS
    for j in range(3):
        coef[0, j] = inside_tile(place_ref, first_row, height, j) * half_a
        coef[1, j] = inside_tile(place_ref, first_row + 1, height, j) * half_b
        coef[2, j] = inside_tile(place_ref, first_row - 1, height, j) * half_b
        coef[3, j] = inside_tile(place_ref, first_row, height, j, 1) * half_b
        coef[4, j] = inside_tile(place_ref, first_row, height, j, -1) * half_b

    lane = lax.broadcasted_iota(jnp.int32, (8, LANES), 1)
    keep = [1.0 - config_ref[c] for c in range(WAVES)]

    def load(ref, i, t, by=0):
        at = PAD + 8 * t + by
        return [ref[i, j, at : at + 8, :] for j in range(3)]

    def along(ref, i, t):
        ahead, behind = load(ref, i, t, 1), load(ref, i, t, -1)
        return [ahead[j] - behind[j] for j in range(3)]

    def across(parts):
        ahead, behind = eastward(parts, lane), westward(parts, lane)
        return [ahead[j] - behind[j] for j in range(3)]

    h = [load(state, 0, t) for t in range(tiles)]
    du = [along(state, 1, t) for t in range(tiles)]
    dv = [across(load(state, 2, t)) for t in range(tiles)]
    for t in range(tiles):
        at = PAD + 8 * t
        push_u, push_v = along(forcing, 1, t), across(load(forcing, 2, t))
        for j in range(3):
            coef[5, j, 8 * t : 8 * t + 8, :] = push_u[j]
            coef[6, j, 8 * t : 8 * t + 8, :] = push_v[j]
    own = (4, 5)
    sum_u = {t: [jnp.zeros((8, LANES), f32)] * 2 for t in (3, 4, 5, 6)}
    sum_v = {t: [jnp.zeros((8, LANES), f32)] * 3 for t in own}
    for step in range(SUBSTEPS):
        first = step // STEPS_PER_PHASE
        final = step == SUBSTEPS - 1
        span = range(first, tiles - first)
        for t in span:
            here = slice(8 * t, 8 * t + 8)
            push = load(forcing, 0, t)
            for j in range(3):
                h[t][j] = (keep[0] * h[t][j] + push[j]) - coef[0, j, here, :] * (du[t][j] + dv[t][j])
                if not final:
                    state[0, j, PAD + 8 * t : PAD + 8 * t + 8, :] = h[t][j]
        for t in sum_u:
            sum_u[t] = [keep[1] * sum_u[t][j] + h[t][j] for j in range(2)]
        for t in own:
            sum_v[t] = [keep[2] * sum_v[t][j] + h[t][j] for j in range(3)]
        if final:
            break
        for t in span:
            here = slice(8 * t, 8 * t + 8)
            east, west = eastward(h[t], lane, 2), westward(h[t], lane, 2)
            up, down = load(state, 0, t, 2), load(state, 0, t, -2)
            for j in range(3):
                mid = h[t][j]
                du[t][j] = (keep[1] * du[t][j] + coef[5, j, here, :]) - (
                    coef[1, j, here, :] * (up[j] - mid) - coef[2, j, here, :] * (mid - down[j])
                )
                dv[t][j] = (keep[2] * dv[t][j] + coef[6, j, here, :]) - (
                    coef[3, j, here, :] * (east[j] - mid) - coef[4, j, here, :] * (mid - west[j])
                )

    def decays(c):
        power, total = c, 1.0 + 0.0 * c
        for _ in range(SUBSTEPS - 1):
            total = total + power
            power = power * c
        return power, total

    for t in sum_u:
        for j in range(2):
            state[0, j, PAD + 8 * t : PAD + 8 * t + 8, :] = sum_u[t][j]
    power_u, total_u = decays(keep[1])
    power_v, total_v = decays(keep[2])
    for j in range(2):
        inside = inside_tile(place_ref, 0, ROWS, j) * half_b
        for t in own:
            at = PAD + 8 * t
            rows = slice(8 * (t - 4), 8 * (t - 4) + 8)
            factor = inside[rows]
            slope_u = state[0, j, at + 1 : at + 9, :] - state[0, j, at - 1 : at + 7, :]
            slope_v = across(sum_v[t])[j]
            new_u = power_u * state[1, j, at : at + 8, :] + total_u * forcing[1, j, at : at + 8, :] - factor * slope_u
            new_v = power_v * state[2, j, at : at + 8, :] + total_v * forcing[2, j, at : at + 8, :] - factor * slope_v
            cols = slice(j * LANES, (j + 1) * LANES)
            out_ref[0, rows, cols] = h[t][j]
            out_ref[1, rows, cols] = new_u
            out_ref[2, rows, cols] = new_v
    for i in range(TRACERS):
        out_ref[WAVES + i] = tracers_ref[i]
    if not last:
        fields = [out_ref[c] for c in range(FIELDS)]
        received = [received_ref[c] for c in range(FIELDS)]
        write_export(fields, received, land_ref[...].astype(f32), smix_ref, imix_ref, turned, export_ref)


def wave_steps(last, place, config, mixes, operands):
    state = shaped((FIELDS, ROWS, COLS))
    scratch = [
        pltpu.VMEM((WAVES, 3, 5 * ROWS + 2 * PAD, LANES), f32),
        pltpu.VMEM((WAVES, 3, 5 * ROWS + 2 * PAD, LANES), f32),
        pltpu.VMEM((7, 3, 5 * ROWS, LANES), f32),
    ]
    if not last:
        scratch.append(pltpu.VMEM((2, TURNED, LANES), f32))
    return pl.pallas_call(
        lambda *refs: wave_kernel(last, *refs),
        out_shape=state if last else (state, shaped((TURNED, COLS), bf16)),
        in_specs=[SMEM] * (2 + len(mixes)) + [VMEM] * len(operands),
        out_specs=VMEM if last else (VMEM,) * 2,
        scratch_shapes=scratch,
        compiler_params=params(),
        name="wave_steps_last" if last else "wave_steps",
    )(place, config, *mixes, *operands)


def exchanged(block, axis, distance, phase):
    count = lax.axis_size(axis)
    route = []
    for low in range(count - distance):
        if (low // distance) % 2 == phase:
            route += [(low, low + distance), (low + distance, low)]
    return lax.ppermute(block, axis, route)


def local(
    section_state, prev_import, land_mask, state_mix, import_mix, damping, wave_speed,
    remap_owner, remap_slot, remap_weight,
):
    smix = state_mix[0]
    imix = import_mix[0]
    gx = lax.axis_index("gx")
    gy = lax.axis_index("gy")
    side_near = 1 - 2 * (gx % 2)
    side_far = 1 - 2 * ((gx // 2) % 2)
    place = jnp.stack([
        gx * ROWS, gy * COLS, lax.axis_size("gx") * ROWS, lax.axis_size("gy") * COLS,
        2 - side_near, 2 + side_near, 2 - 2 * side_far, 2 + 2 * side_far, gy % 2,
    ]).astype(jnp.int32)
    config = jnp.concatenate([damping[0], wave_speed[0]])
    owner = remap_owner[0].reshape(-1)
    slot = remap_slot[0].reshape(-1)
    away = owner - gx
    window = 2 + away * jnp.where(away % 2 == 1, side_near, side_far)
    entry = (window * ROWS + slot // 4) * 2 + (slot % 4) // 2
    second = lax.iota(jnp.int32, owner.shape[0]) % 2
    index = entry + ((slot % 2) ^ second) * (5 * ROWS * 2)
    index = jnp.concatenate([index, (gy % 2).astype(jnp.int32)[None]])
    weight = remap_weight[0].reshape(ROWS, COLS, 128)

    exported, fields, land = export(section_state[0], prev_import[0], land_mask[0], smix, imix)
    for interval in range(ITERS):
        last = interval == ITERS - 1
        opposite = lax.ppermute(exported, "sec", [(0, 1), (1, 0)])
        near = pack(opposite, fields, index, place, config)
        state_c = exchanged(near, "gx", 1, 1)
        state_i = exchanged(near, "gx", 1, 0)
        export_c = exchanged(opposite, "gx", 2, 1)
        export_i = exchanged(opposite, "gx", 2, 0)
        if interval == 0:
            weight = stage(weight, state_c, state_i)
        forcing, to_chip, to_outer, received = remap(
            index, (export_i, state_i, opposite, state_c, export_c), weight, land, fields
        )
        outer = exchanged(to_outer, "gy", 1, 1)
        chip = exchanged(to_chip, "gy", 1, 0)
        out_c, out_i, outer, left, right = pack_forcing(place, forcing, outer, chip, state_c, state_i)
        near_c = exchanged(out_c, "gx", 1, 1)
        near_i = exchanged(out_i, "gx", 1, 0)
        far_c = exchanged(outer, "gx", 2, 1)
        far_i = exchanged(outer, "gx", 2, 0)
        own = (forcing, left, right)
        state = (state_c, fields, state_i)
        operands = (near_c, *own, near_i, *state)
        if last:
            tracers, received = tracer_steps(last, place, config, operands + (received,))
        else:
            tracers = tracer_steps(last, place, config, operands)
        operands = (far_i, near_c, *own, near_i, far_c, *state, tracers)
        if last:
            fields = wave_steps(last, place, config, (), operands)
        else:
            operands += (received, land)
            fields, exported = wave_steps(last, place, config, (smix, imix), operands)
    return (fields[None], received[None])


def solution(mesh):
    in_specs = (
        P("sec", None, "gx", "gy"),
        P("sec", None, "gx", "gy"),
        P("sec", "gx", "gy"),
        P("sec", None, None),
        P("sec", None, None),
        P("sec", None),
        P("sec", None),
        P("sec", "gx", "gy", None),
        P("sec", "gx", "gy", None),
        P("sec", "gx", "gy", None, None),
    )
    out_specs = (P("sec", None, "gx", "gy"), P("sec", None, "gx", "gy"))
    return jax.shard_map(local, mesh=mesh, in_specs=in_specs, out_specs=out_specs, check_vma=False)
```

```python
import jax
import jax.numpy as jnp
from jax import lax
from jax.experimental import pallas as pl
from jax.experimental.pallas import tpu as pltpu
from jax.sharding import PartitionSpec as P

SUBSTEPS = 16
ITERS = 2
DIFFUSION = 0.1
COUPLING = 0.2

FIELDS = 8
WAVES = 3
TRACERS = 5
ROWS = 16
COLS = 256
LANES = 128
TURNED = ROWS * FIELDS
STRIP = 32
STEPS_PER_PHASE = 4

A_WAVE = 10
A_EXPORT = 22
A_PLANES = 38
B_WAVE = 12
B_STRIP_T = 28
B_STRIP_W = 30
B_BEHIND = 34
B_PLANES = 46
C_STRIP_W = 16
C_PLANES = 20

PAD = 8
WAVE_SPEED = 8
ROW0, COL0, ROW_END, COL_END, AFTER_NEAR, AFTER_FAR, GY_ODD = range(10, 17)
SMEM = pl.BlockSpec(memory_space=pltpu.SMEM)
VMEM = pl.BlockSpec(memory_space=pltpu.VMEM)
HBM = pl.BlockSpec(memory_space=pl.ANY)

f32 = jnp.float32
bf16 = jnp.bfloat16


def params(mib=24):
    return pltpu.CompilerParams(vmem_limit_bytes=mib * 1024 * 1024)


def shaped(shape, dtype=f32):
    return jax.ShapeDtypeStruct(shape, dtype)


def spread(config_ref, k, rows=8):
    return jnp.broadcast_to(config_ref[:, k : k + 1], (rows, LANES))


def chosen(flag, ones, others):
    return [jnp.where(flag, one, other) for one, other in zip(ones, others)]


def half_of(value, half):
    return value[:, half * LANES : (half + 1) * LANES]


def write_export(fields, received, wet, smix_ref, imix_ref, turned, out_ref):
    scale = wet * jnp.sqrt(1.0 + fields[1] * fields[1] + fields[2] * fields[2])
    for c in range(FIELDS):
        total = smix_ref[c : c + 1, 0:1] * fields[0]
        for k in range(1, FIELDS):
            total = total + smix_ref[c : c + 1, k : k + 1] * fields[k]
        other = imix_ref[c : c + 1, 0:1] * received[0]
        for k in range(1, FIELDS):
            other = other + imix_ref[c : c + 1, k : k + 1] * received[k]
        value = scale * (total + other)
        for half in range(2):
            turned[half, pl.ds(c, ROWS, stride=FIELDS), :] = half_of(value, half)
    for half in range(2):
        out_ref[:, half * LANES : (half + 1) * LANES] = turned[half].astype(bf16)


def write_strips(fields, at, odd, chip_ref, outer_ref):
    lane = lax.broadcasted_iota(jnp.int32, (ROWS, LANES), 1)
    groups = [fields[3:7], [fields[7]] + fields[0:3]]
    for p, group in enumerate(groups):
        first = group[0][0]
        last = pltpu.roll(group[0][1], STRIP, 1)
        for j in range(1, 4):
            here = lane >= STRIP * j
            first = jnp.where(here, pltpu.roll(group[j][0], STRIP * j, 1), first)
            moved = group[j][1] if j == 3 else pltpu.roll(group[j][1], STRIP * (j + 1), 1)
            last = jnp.where(here, moved, last)
        chip_ref[at + p] = jnp.where(odd, first, last)
        outer_ref[at + p] = jnp.where(odd, last, first)


def export_kernel(
    smix_ref, imix_ref, fields_ref, received_ref, land_ref,
    out_ref, fields_out, land_out, turned, received_buf, sems,
):
    copies = [
        pltpu.make_async_copy(fields_ref, fields_out, sems.at[0]),
        pltpu.make_async_copy(received_ref, received_buf, sems.at[1]),
        pltpu.make_async_copy(land_ref, land_out, sems.at[2]),
    ]
    for copy in copies:
        copy.start()
    for copy in copies:
        copy.wait()
    fields = [fields_out[c] for c in range(FIELDS)]
    received = [received_buf[c] for c in range(FIELDS)]
    write_export(fields, received, land_out[...].astype(f32), smix_ref, imix_ref, turned, out_ref)


def export(fields, received, land, smix, imix):
    return pl.pallas_call(
        export_kernel,
        out_shape=(
            shaped((TURNED, COLS), bf16), shaped((FIELDS, ROWS, COLS)), shaped((ROWS, COLS), jnp.int32),
        ),
        in_specs=[VMEM, VMEM, HBM, HBM, HBM],
        out_specs=(VMEM,) * 3,
        scratch_shapes=[
            pltpu.VMEM((2, TURNED, LANES), f32),
            pltpu.VMEM((FIELDS, ROWS, COLS), f32),
            pltpu.SemaphoreType.DMA((3,)),
        ],
        compiler_params=params(56),
        name="export",
    )(smix, imix, fields, received, land)


def split_to(ref, at, low_at, value):
    high = value.astype(bf16)
    ref[at] = high
    ref[low_at] = (value - high.astype(f32)).astype(bf16)


def write_main(ref, tracer_at, wave_at, wave_low_at, fields_ref):
    for half in range(2):
        cols = slice(half * LANES, (half + 1) * LANES)
        for i in range(TRACERS):
            ref[tracer_at + 2 * i + half] = fields_ref[WAVES + i, :, cols].astype(bf16)
        for i in range(WAVES):
            split_to(ref, wave_at + 2 * i + half, wave_low_at + 2 * i + half, fields_ref[i, :, cols])


def pack_kernel(opposite_ref, fields_ref, index_ref, config_ref, near_ref):
    del index_ref, config_ref
    write_main(near_ref, 0, A_WAVE, A_WAVE + 6, fields_ref)
    for half in range(2):
        for i in range(TURNED // 16):
            near_ref[A_EXPORT + half * 8 + i] = opposite_ref[16 * i : 16 * i + 16, half * LANES : (half + 1) * LANES]


def pack(opposite, fields, index, config):
    return pl.pallas_call(
        pack_kernel,
        out_shape=shaped((A_PLANES, ROWS, LANES), bf16),
        in_specs=[VMEM] * 2 + [HBM] * 2,
        out_specs=VMEM,
        compiler_params=params(),
        name="pack",
    )(opposite, fields, index, config)


def pack_forcing_kernel(
    config_ref, forcing_ref, outer_ref, chip_ref, state_c_ref, state_i_ref,
    out_c_ref, out_i_ref, far_ref, left_ref, right_ref,
):
    odd = spread(config_ref, GY_ODD, ROWS) > 0.5
    for p in range(4):
        left_ref[p] = jnp.where(odd, chip_ref[p], outer_ref[p])
        right_ref[p] = jnp.where(odd, outer_ref[p], chip_ref[p])
    for ref, behind in ((out_c_ref, state_i_ref), (out_i_ref, state_c_ref)):
        write_main(ref, 0, B_WAVE + 2, B_WAVE + 10, forcing_ref)
        for k, strips in enumerate((left_ref, right_ref)):
            ref[10 + k] = strips[0].astype(bf16)
            split_to(ref, B_WAVE + k, B_WAVE + 8 + k, strips[1])
            ref[B_STRIP_T + k] = strips[2].astype(bf16)
            split_to(ref, B_STRIP_W + k, B_STRIP_W + 2 + k, strips[3])
        for p in range(12):
            ref[B_BEHIND + p] = behind[A_WAVE + p]
    for p in range(16):
        far_ref[p] = out_c_ref[B_WAVE + p]
    for p in range(4):
        far_ref[C_STRIP_W + p] = out_c_ref[B_STRIP_W + p]


def pack_forcing(config, forcing, outer, chip, state_c, state_i):
    payload, strips = shaped((B_PLANES, ROWS, LANES), bf16), shaped((4, ROWS, LANES))
    return pl.pallas_call(
        pack_forcing_kernel,
        out_shape=(payload, payload, shaped((C_PLANES, ROWS, LANES), bf16), strips, strips),
        in_specs=[VMEM] * 6,
        out_specs=(VMEM,) * 5,
        compiler_params=params(),
        name="pack_forcing",
    )(config, forcing, outer, chip, state_c, state_i)


def stage_kernel(weight_ref, near_c_ref, near_i_ref, out_ref):
    del near_c_ref, near_i_ref
    out_ref[...] = weight_ref[...]


def stage(weight, near_c, near_i):
    return pl.pallas_call(
        stage_kernel,
        out_shape=shaped(weight.shape, weight.dtype),
        in_specs=[VMEM, HBM, HBM],
        out_specs=VMEM,
        compiler_params=params(),
        name="stage_weights",
    )(weight, near_c, near_i)


def remap_kernel(
    index_ref, far_i_ref, near_i_ref, opposite_ref, near_c_ref, far_c_ref, weight_ref, land_ref, fields_ref,
    forcing_ref, chip_ref, outer_ref, import_ref, table, turned,
):
    half_count = 5 * ROWS * 2
    windows = [far_c_ref, near_c_ref, opposite_ref, near_i_ref, far_i_ref]
    for w, ref in enumerate(windows):
        for half in range(2):
            for i in range(TURNED // 16):
                if w in (1, 3):
                    chunk = ref[A_EXPORT + half * 8 + i]
                else:
                    chunk = ref[16 * i : 16 * i + 16, half * LANES : (half + 1) * LANES]
                chunk = chunk.astype(f32)
                for sub in range(2):
                    part = chunk[sub * 8 : sub * 8 + 8]
                    at = (w * ROWS + i * 2 + sub) * 2 + half
                    table[at] = part
                    table[half_count + at] = pltpu.roll(part, 64, 1)
    lane8 = lax.broadcasted_iota(jnp.int32, (8, LANES), 1)
    low_half = lane8 < 64
    ones = jnp.ones((8, LANES), f32)
    for x in range(ROWS):
        pieces = []
        for seg in range(4):
            at = (x * 4 + seg) * 2
            pieces.append(jnp.where(low_half, table[index_ref[at]], table[index_ref[at + 1]]))
        picked = jnp.concatenate(pieces + [ones], axis=0).astype(bf16)
        product = lax.dot_general(
            picked, weight_ref[x], (((1,), (1,)), ((), ())), preferred_element_type=f32
        )
        for half in range(2):
            cols = half_of(product, half)
            summed = jnp.where(low_half, cols[16 * half : 16 * half + 8], cols[16 * half + 8 : 16 * half + 16])
            turned[half, x * 8 : x * 8 + 8, :] = summed / cols[32:40]
    wet = land_ref[...].astype(f32)
    forcing = []
    for c in range(FIELDS):
        parts = []
        for half in range(2):
            value = turned[half, pl.ds(c, ROWS, stride=FIELDS), :]
            import_ref[c, :, half * LANES : (half + 1) * LANES] = value
            part = COUPLING * half_of(wet, half) * value
            forcing_ref[c, :, half * LANES : (half + 1) * LANES] = part
            parts.append(part)
        forcing.append(parts)
    state = [[half_of(fields_ref[c], half) for half in range(2)] for c in range(FIELDS)]
    odd = index_ref[TURNED] == 1
    write_strips(forcing, 0, odd, chip_ref, outer_ref)
    write_strips(state, 2, odd, chip_ref, outer_ref)


def remap(index, windows, weight, land, fields):
    strips = shaped((4, ROWS, LANES))
    return pl.pallas_call(
        remap_kernel,
        out_shape=(shaped((FIELDS, ROWS, COLS)), strips, strips, shaped((FIELDS, ROWS, COLS))),
        in_specs=[SMEM] + [VMEM] * 8,
        out_specs=(VMEM,) * 4,
        scratch_shapes=[
            pltpu.VMEM((2 * 5 * ROWS * 2, FIELDS, LANES), f32),
            pltpu.VMEM((2, TURNED, LANES), f32),
        ],
        compiler_params=params(),
        name="remap",
    )(index, *windows, weight, land, fields)


def sides(left, right, j):
    lane = lax.broadcasted_iota(jnp.int32, (ROWS, LANES), 1)
    if j:
        right = pltpu.roll(right, LANES - STRIP * j, 1)
    if j != 3:
        left = pltpu.roll(left, 96 - STRIP * j, 1)
    return jnp.where(lane < STRIP, right, jnp.where(lane >= 96, left, 0.0))


def place_field(dest, start, parts):
    for j, part in enumerate(parts):
        dest[j, start : start + ROWS, :] = part


def joined(ref, at, low_at):
    return ref[at].astype(f32) + ref[low_at].astype(f32)


def inside_tile(config_ref, first_row, count, j, shift=0):
    shape = (count, LANES)
    row = (lax.broadcasted_iota(jnp.int32, shape, 0) + first_row).astype(f32) + spread(config_ref, ROW0, count)
    col = lax.broadcasted_iota(jnp.int32, shape, 1) + j * LANES
    if j == 2:
        col = jnp.where(col >= 3 * LANES - STRIP, col - 3 * LANES, col)
    col = (col + shift).astype(f32) + spread(config_ref, COL0, count)
    ok = (row >= 0.0) & (row < spread(config_ref, ROW_END, count))
    ok = ok & (col >= 0.0) & (col < spread(config_ref, COL_END, count))
    return jnp.where(ok, 1.0, 0.0)


def westward(parts, lane, by=1):
    moved = [pltpu.roll(part, by, 1) for part in parts]
    return [jnp.where(lane < by, moved[j - 1], moved[j]) for j in range(3)]


def eastward(parts, lane, by=1):
    moved = [pltpu.roll(part, LANES - by, 1) for part in parts]
    return [jnp.where(lane >= LANES - by, moved[(j + 1) % 3], moved[j]) for j in range(3)]


def own_parts(fields_ref, left_ref, right_ref, at, i):
    p, j = (0, i - WAVES) if WAVES <= i < FIELDS - 1 else (1, (i + 1) % FIELDS)
    return [
        fields_ref[i, :, :LANES], fields_ref[i, :, LANES:], sides(left_ref[at + p], right_ref[at + p], j),
    ]


def tracer_parts(ref, strip_ref, strip_at, wave_strip_at, i):
    at = strip_at if i < 4 else wave_strip_at
    beside = sides(strip_ref[at].astype(f32), strip_ref[at + 1].astype(f32), i % 4)
    return [ref[2 * i].astype(f32), ref[2 * i + 1].astype(f32), beside]


def wave_main(ref, at, low_at, i):
    return [joined(ref, at + 2 * i + half, low_at + 2 * i + half) for half in range(2)]


def wave_strip(ref, at, low_at, i):
    left, right = [joined(ref, at + k, low_at + k) for k in range(2)]
    return [sides(left, right, i + 1)]


def tracer_kernel(
    last, config_ref, near_c_ref, forcing_ref, left_ref, right_ref, near_i_ref,
    state_c_ref, fields_ref, state_i_ref, *refs
):
    if last:
        received_ref, out_ref, received_out, state, forcing, coef = refs
        received_out[...] = received_ref[...]
    else:
        out_ref, state, forcing, coef = refs
    after = spread(config_ref, AFTER_NEAR, ROWS) > 0.5
    for i in range(TRACERS):
        pushed, parts = [], []
        for near, main in ((near_c_ref, state_c_ref), (near_i_ref, state_i_ref)):
            pushed.append(tracer_parts(near, near, 10, B_WAVE, i))
            parts.append(tracer_parts(main, near, B_STRIP_T, B_STRIP_W, i))
        place_field(forcing.at[i], 0, chosen(after, pushed[1], pushed[0]))
        place_field(forcing.at[i], ROWS, own_parts(forcing_ref, left_ref, right_ref, 0, WAVES + i))
        place_field(forcing.at[i], 2 * ROWS, chosen(after, pushed[0], pushed[1]))
        place_field(state.at[0, i], PAD, chosen(after, parts[1], parts[0]))
        place_field(state.at[0, i], PAD + ROWS, own_parts(fields_ref, left_ref, right_ref, 2, WAVES + i))
        place_field(state.at[0, i], PAD + 2 * ROWS, chosen(after, parts[0], parts[1]))
    height = 3 * ROWS
    for k in range(2):
        for i in range(TRACERS):
            for j in range(3):
                state[k, i, j, 0:PAD, :] = jnp.zeros((PAD, LANES), f32)
                state[k, i, j, PAD + height : height + 2 * PAD, :] = jnp.zeros((PAD, LANES), f32)
    for j in range(3):
        coef[j] = inside_tile(config_ref, -ROWS, height, j) * DIFFUSION

    lane = lax.broadcasted_iota(jnp.int32, (8, LANES), 1)
    keep = [(1.0 - spread(config_ref, WAVES + c)) - 4.0 * DIFFUSION for c in range(TRACERS)]

    def step(source, dest, first, count):
        for t in range(first, first + count):
            at = PAD + 8 * t
            here = slice(8 * t, 8 * t + 8)
            for c in range(TRACERS):
                mid = [state[source, c, j, at : at + 8, :] for j in range(3)]
                west = westward(mid, lane)
                east = eastward(mid, lane)
                for j in range(3):
                    above = state[source, c, j, at + 1 : at + 9, :]
                    below = state[source, c, j, at - 1 : at + 7, :]
                    around = (above + below) + (east[j] + west[j])
                    state[dest, c, j, at : at + 8, :] = (
                        keep[c] * mid[j] + forcing[c, j, here, :]
                    ) + coef[j, here, :] * around

    def pair_of_steps(first, count):
        def run(_, carry):
            step(0, 1, first, count)
            step(1, 0, first, count)
            return carry
        return run

    lax.fori_loop(0, SUBSTEPS // 4, pair_of_steps(0, 6), 0)
    lax.fori_loop(0, SUBSTEPS // 4, pair_of_steps(1, 4), 0)
    for i in range(TRACERS):
        for half in range(2):
            out_ref[i, :, half * LANES : (half + 1) * LANES] = state[0, i, half, PAD + ROWS : PAD + 2 * ROWS, :]


def tracer_steps(last, config, operands):
    tracers, received = shaped((TRACERS, ROWS, COLS)), shaped((FIELDS, ROWS, COLS))
    return pl.pallas_call(
        lambda *refs: tracer_kernel(last, *refs),
        out_shape=(tracers, received) if last else tracers,
        in_specs=[VMEM] * (1 + len(operands)),
        out_specs=(VMEM, VMEM) if last else VMEM,
        scratch_shapes=[
            pltpu.VMEM((2, TRACERS, 3, 3 * ROWS + 2 * PAD, LANES), f32),
            pltpu.VMEM((TRACERS, 3, 3 * ROWS, LANES), f32),
            pltpu.VMEM((3, 3 * ROWS, LANES), f32),
        ],
        compiler_params=params(),
        cost_estimate=pl.CostEstimate(flops=10_000_000, bytes_accessed=4_000_000, transcendentals=0),
        name="tracer_steps",
    )(config, *operands)


def wave_kernel(last, config_ref, *refs):
    if not last:
        smix_ref, imix_ref, *refs = refs
    (far_i, near_c, forcing_ref, left_ref, right_ref, near_i, far_c,
     state_c, fields_ref, state_i, tracers_ref, *refs) = refs
    if last:
        out_ref, state, forcing, coef = refs
    else:
        received_ref, land_ref, out_ref, export_ref, state, forcing, coef, turned = refs
    height = 5 * ROWS
    tiles = height // 8

    after = spread(config_ref, AFTER_NEAR, ROWS) > 0.5
    after_far = spread(config_ref, AFTER_FAR, ROWS) > 0.5
    for i in range(WAVES):
        place_field(forcing.at[i], PAD + 2 * ROWS, own_parts(forcing_ref, left_ref, right_ref, 0, i))
        place_field(state.at[i], PAD + 2 * ROWS, own_parts(fields_ref, left_ref, right_ref, 2, i))
        pushed, parts, behind = [], [], []
        for near, main in ((near_c, state_c), (near_i, state_i)):
            pushed.append(wave_main(near, B_WAVE + 2, B_WAVE + 10, i) + wave_strip(near, B_WAVE, B_WAVE + 8, i))
            parts.append(wave_main(main, A_WAVE, A_WAVE + 6, i) + wave_strip(near, B_STRIP_W, B_STRIP_W + 2, i))
            behind.append(wave_main(near, B_BEHIND, B_BEHIND + 6, i))
        far_pushed = [wave_main(far, 2, 10, i) + wave_strip(far, 0, 8, i) for far in (far_c, far_i)]
        far_strip = [wave_strip(far, C_STRIP_W, C_STRIP_W + 2, i) for far in (far_c, far_i)]
        for k, slot in ((1, 0), (0, 4)):
            near_slot = (slot + 2) // 2
            place_field(forcing.at[i], PAD + near_slot * ROWS, chosen(after, pushed[k], pushed[1 - k]))
            place_field(state.at[i], PAD + near_slot * ROWS, chosen(after, parts[k], parts[1 - k]))
            place_field(forcing.at[i], PAD + slot * ROWS, chosen(after_far, far_pushed[k], far_pushed[1 - k]))
            main = chosen(after, behind[k], behind[1 - k])
            strip = chosen(after_far, far_strip[k], far_strip[1 - k])
            place_field(state.at[i], PAD + slot * ROWS, main + strip)
        for j in range(3):
            for ref in (state, forcing):
                ref[i, j, 0:PAD, :] = jnp.zeros((PAD, LANES), f32)
                ref[i, j, PAD + height : height + 2 * PAD, :] = jnp.zeros((PAD, LANES), f32)
    half_a = 0.5 * config_ref[:, WAVE_SPEED : WAVE_SPEED + 1]
    half_b = 0.5 * config_ref[:, WAVE_SPEED + 1 : WAVE_SPEED + 2]
    first_row = -2 * ROWS
    for j in range(3):
        coef[0, j] = inside_tile(config_ref, first_row, height, j) * half_a
        coef[1, j] = inside_tile(config_ref, first_row + 1, height, j) * half_b
        coef[2, j] = inside_tile(config_ref, first_row - 1, height, j) * half_b
        coef[3, j] = inside_tile(config_ref, first_row, height, j, 1) * half_b
        coef[4, j] = inside_tile(config_ref, first_row, height, j, -1) * half_b

    lane = lax.broadcasted_iota(jnp.int32, (8, LANES), 1)
    keep = [1.0 - spread(config_ref, c) for c in range(WAVES)]

    def load(ref, i, t, by=0):
        at = PAD + 8 * t + by
        return [ref[i, j, at : at + 8, :] for j in range(3)]

    def along(ref, i, t):
        ahead, behind = load(ref, i, t, 1), load(ref, i, t, -1)
        return [ahead[j] - behind[j] for j in range(3)]

    def across(parts):
        ahead, behind = eastward(parts, lane), westward(parts, lane)
        return [ahead[j] - behind[j] for j in range(3)]

    h = [load(state, 0, t) for t in range(tiles)]
    du = [along(state, 1, t) for t in range(tiles)]
    dv = [across(load(state, 2, t)) for t in range(tiles)]
    for t in range(tiles):
        at = PAD + 8 * t
        push_u, push_v = along(forcing, 1, t), across(load(forcing, 2, t))
        for j in range(3):
            coef[5, j, 8 * t : 8 * t + 8, :] = push_u[j]
            coef[6, j, 8 * t : 8 * t + 8, :] = push_v[j]
    own = (4, 5)
    sum_u = {t: [jnp.zeros((8, LANES), f32)] * 2 for t in (3, 4, 5, 6)}
    sum_v = {t: [jnp.zeros((8, LANES), f32)] * 3 for t in own}
    for step in range(SUBSTEPS):
        first = step // STEPS_PER_PHASE
        final = step == SUBSTEPS - 1
        span = range(first, tiles - first)
        for t in span:
            here = slice(8 * t, 8 * t + 8)
            push = load(forcing, 0, t)
            for j in range(3):
                h[t][j] = (keep[0] * h[t][j] + push[j]) - coef[0, j, here, :] * (du[t][j] + dv[t][j])
                if not final:
                    state[0, j, PAD + 8 * t : PAD + 8 * t + 8, :] = h[t][j]
        for t in sum_u:
            sum_u[t] = [keep[1] * sum_u[t][j] + h[t][j] for j in range(2)]
        for t in own:
            sum_v[t] = [keep[2] * sum_v[t][j] + h[t][j] for j in range(3)]
        if final:
            break
        for t in span:
            here = slice(8 * t, 8 * t + 8)
            east, west = eastward(h[t], lane, 2), westward(h[t], lane, 2)
            up, down = load(state, 0, t, 2), load(state, 0, t, -2)
            for j in range(3):
                mid = h[t][j]
                du[t][j] = (keep[1] * du[t][j] + coef[5, j, here, :]) - (
                    coef[1, j, here, :] * (up[j] - mid) - coef[2, j, here, :] * (mid - down[j])
                )
                dv[t][j] = (keep[2] * dv[t][j] + coef[6, j, here, :]) - (
                    coef[3, j, here, :] * (east[j] - mid) - coef[4, j, here, :] * (mid - west[j])
                )

    def decays(c):
        power, total = c, 1.0 + 0.0 * c
        for _ in range(SUBSTEPS - 1):
            total = total + power
            power = power * c
        return power, total

    for t in sum_u:
        for j in range(2):
            state[0, j, PAD + 8 * t : PAD + 8 * t + 8, :] = sum_u[t][j]
    power_u, total_u = decays(keep[1])
    power_v, total_v = decays(keep[2])
    for j in range(2):
        inside = inside_tile(config_ref, 0, ROWS, j) * half_b
        for t in own:
            at = PAD + 8 * t
            rows = slice(8 * (t - 4), 8 * (t - 4) + 8)
            factor = inside[rows]
            slope_u = state[0, j, at + 1 : at + 9, :] - state[0, j, at - 1 : at + 7, :]
            slope_v = across(sum_v[t])[j]
            new_u = power_u * state[1, j, at : at + 8, :] + total_u * forcing[1, j, at : at + 8, :] - factor * slope_u
            new_v = power_v * state[2, j, at : at + 8, :] + total_v * forcing[2, j, at : at + 8, :] - factor * slope_v
            cols = slice(j * LANES, (j + 1) * LANES)
            out_ref[0, rows, cols] = h[t][j]
            out_ref[1, rows, cols] = new_u
            out_ref[2, rows, cols] = new_v
    for i in range(TRACERS):
        out_ref[WAVES + i] = tracers_ref[i]
    if not last:
        fields = [out_ref[c] for c in range(FIELDS)]
        received = [received_ref[c] for c in range(FIELDS)]
        write_export(fields, received, land_ref[...].astype(f32), smix_ref, imix_ref, turned, export_ref)


def wave_steps(last, config, mixes, operands):
    state = shaped((FIELDS, ROWS, COLS))
    scratch = [
        pltpu.VMEM((WAVES, 3, 5 * ROWS + 2 * PAD, LANES), f32),
        pltpu.VMEM((WAVES, 3, 5 * ROWS + 2 * PAD, LANES), f32),
        pltpu.VMEM((7, 3, 5 * ROWS, LANES), f32),
    ]
    if not last:
        scratch.append(pltpu.VMEM((2, TURNED, LANES), f32))
    return pl.pallas_call(
        lambda *refs: wave_kernel(last, *refs),
        out_shape=state if last else (state, shaped((TURNED, COLS), bf16)),
        in_specs=[VMEM] * (1 + len(mixes) + len(operands)),
        out_specs=VMEM if last else (VMEM,) * 2,
        scratch_shapes=scratch,
        compiler_params=params(),
        name="wave_steps_last" if last else "wave_steps",
    )(config, *mixes, *operands)


def exchanged(block, axis, distance, phase):
    count = lax.axis_size(axis)
    route = []
    for low in range(count - distance):
        if (low // distance) % 2 == phase:
            route += [(low, low + distance), (low + distance, low)]
    return lax.ppermute(block, axis, route)


def local(
    section_state, prev_import, land_mask, state_mix, import_mix, damping, wave_speed,
    remap_owner, remap_slot, remap_weight,
):
    smix = state_mix[0]
    imix = import_mix[0]
    gx = lax.axis_index("gx")
    gy = lax.axis_index("gy")
    side_near = 1 - 2 * (gx % 2)
    side_far = 1 - 2 * ((gx // 2) % 2)
    place = jnp.stack([
        gx * ROWS, gy * COLS, lax.axis_size("gx") * ROWS, lax.axis_size("gy") * COLS,
        gx % 2, (gx // 2) % 2, gy % 2,
    ])
    config = jnp.concatenate([damping[0], wave_speed[0], place.astype(f32)])[None]
    owner = remap_owner[0].reshape(-1)
    slot = remap_slot[0].reshape(-1)
    away = owner - gx
    window = 2 + away * jnp.where(away % 2 == 1, side_near, side_far)
    entry = (window * ROWS + slot // 4) * 2 + (slot % 4) // 2
    second = lax.iota(jnp.int32, owner.shape[0]) % 2
    index = entry + ((slot % 2) ^ second) * (5 * ROWS * 2)
    index = jnp.concatenate([index, (gy % 2).astype(jnp.int32)[None]])
    weight = remap_weight[0].reshape(ROWS, COLS, 128)

    exported, fields, land = export(section_state[0], prev_import[0], land_mask[0], smix, imix)
    for interval in range(ITERS):
        last = interval == ITERS - 1
        opposite = lax.ppermute(exported, "sec", [(0, 1), (1, 0)])
        near = pack(opposite, fields, index, config)
        state_c = exchanged(near, "gx", 1, 1)
        state_i = exchanged(near, "gx", 1, 0)
        export_c = exchanged(opposite, "gx", 2, 1)
        export_i = exchanged(opposite, "gx", 2, 0)
        if interval == 0:
            weight = stage(weight, state_c, state_i)
        forcing, to_chip, to_outer, received = remap(
            index, (export_i, state_i, opposite, state_c, export_c), weight, land, fields
        )
        outer = exchanged(to_outer, "gy", 1, 1)
        chip = exchanged(to_chip, "gy", 1, 0)
        out_c, out_i, outer, left, right = pack_forcing(config, forcing, outer, chip, state_c, state_i)
        near_c = exchanged(out_c, "gx", 1, 1)
        near_i = exchanged(out_i, "gx", 1, 0)
        far_c = exchanged(outer, "gx", 2, 1)
        far_i = exchanged(outer, "gx", 2, 0)
        own = (forcing, left, right)
        state = (state_c, fields, state_i)
        operands = (near_c, *own, near_i, *state)
        if last:
            tracers, received = tracer_steps(last, config, operands + (received,))
        else:
            tracers = tracer_steps(last, config, operands)
        operands = (far_i, near_c, *own, near_i, far_c, *state, tracers)
        if last:
            fields = wave_steps(last, config, (), operands)
        else:
            operands += (received, land)
            fields, exported = wave_steps(last, config, (smix, imix), operands)
    return (fields[None], received[None])


def solution(mesh):
    in_specs = (
        P("sec", None, "gx", "gy"),
        P("sec", None, "gx", "gy"),
        P("sec", "gx", "gy"),
        P("sec", None, None),
        P("sec", None, None),
        P("sec", None),
        P("sec", None),
        P("sec", "gx", "gy", None),
        P("sec", "gx", "gy", None),
        P("sec", "gx", "gy", None, None),
    )
    out_specs = (P("sec", None, "gx", "gy"), P("sec", None, "gx", "gy"))
    return jax.shard_map(local, mesh=mesh, in_specs=in_specs, out_specs=out_specs, check_vma=False)
```

```python
import jax
import jax.numpy as jnp
from jax import lax
from jax.experimental import pallas as pl
from jax.experimental.pallas import tpu as pltpu
from jax.sharding import PartitionSpec as P

SUBSTEPS = 16
ITERS = 2
DIFFUSION = 0.1
COUPLING = 0.2

FIELDS = 8
WAVES = 3
TRACERS = 5
ROWS = 16
COLS = 256
LANES = 128
TURNED = ROWS * FIELDS
STRIP = 32
STEPS_PER_PHASE = 4

A_WAVE = 10
A_EXPORT = 22
A_PLANES = 38
B_WAVE = 12
B_STRIP_T = 28
B_STRIP_W = 30
B_BEHIND = 34
B_PLANES = 40
C_STRIP_W = 8
C_PLANES = 10

PAD = 8
WAVE_SPEED = 8
ROW0, COL0, ROW_END, COL_END, AFTER_NEAR, AFTER_FAR, GY_ODD = range(10, 17)
SMEM = pl.BlockSpec(memory_space=pltpu.SMEM)
VMEM = pl.BlockSpec(memory_space=pltpu.VMEM)
HBM = pl.BlockSpec(memory_space=pl.ANY)

f32 = jnp.float32
bf16 = jnp.bfloat16


def params(mib=24):
    return pltpu.CompilerParams(vmem_limit_bytes=mib * 1024 * 1024)


def shaped(shape, dtype=f32):
    return jax.ShapeDtypeStruct(shape, dtype)


def spread(config_ref, k, rows=8):
    return jnp.broadcast_to(config_ref[:, k : k + 1], (rows, LANES))


def chosen(flag, ones, others):
    return [jnp.where(flag, one, other) for one, other in zip(ones, others)]


def half_of(value, half):
    return value[:, half * LANES : (half + 1) * LANES]


def write_export(fields, received, wet, smix_ref, imix_ref, turned, out_ref):
    scale = wet * jnp.sqrt(1.0 + fields[1] * fields[1] + fields[2] * fields[2])
    for c in range(FIELDS):
        total = smix_ref[c : c + 1, 0:1] * fields[0]
        for k in range(1, FIELDS):
            total = total + smix_ref[c : c + 1, k : k + 1] * fields[k]
        other = imix_ref[c : c + 1, 0:1] * received[0]
        for k in range(1, FIELDS):
            other = other + imix_ref[c : c + 1, k : k + 1] * received[k]
        value = scale * (total + other)
        for half in range(2):
            turned[half, pl.ds(c, ROWS, stride=FIELDS), :] = half_of(value, half)
    for half in range(2):
        out_ref[:, half * LANES : (half + 1) * LANES] = turned[half].astype(bf16)


def write_strips(fields, at, odd, chip_ref, outer_ref):
    lane = lax.broadcasted_iota(jnp.int32, (ROWS, LANES), 1)
    groups = [fields[3:7], [fields[7]] + fields[0:3]]
    for p, group in enumerate(groups):
        first = group[0][0]
        last = pltpu.roll(group[0][1], STRIP, 1)
        for j in range(1, 4):
            here = lane >= STRIP * j
            first = jnp.where(here, pltpu.roll(group[j][0], STRIP * j, 1), first)
            moved = group[j][1] if j == 3 else pltpu.roll(group[j][1], STRIP * (j + 1), 1)
            last = jnp.where(here, moved, last)
        chip_ref[at + p] = jnp.where(odd, first, last)
        outer_ref[at + p] = jnp.where(odd, last, first)


def export_kernel(
    smix_hbm, imix_hbm, fields_hbm, received_hbm, land_hbm, out_ref,
    smix_ref, imix_ref, fields_ref, received_ref, land_ref, turned, sems,
):
    pairs = (
        (fields_hbm, fields_ref), (received_hbm, received_ref), (land_hbm, land_ref),
        (smix_hbm, smix_ref), (imix_hbm, imix_ref),
    )
    copies = [pltpu.make_async_copy(source, dest, sems.at[k]) for k, (source, dest) in enumerate(pairs)]
    for copy in copies:
        copy.start()
    for copy in copies:
        copy.wait()
    fields = [fields_ref[c] for c in range(FIELDS)]
    received = [received_ref[c] for c in range(FIELDS)]
    write_export(fields, received, land_ref[...].astype(f32), smix_ref, imix_ref, turned, out_ref)


def export(fields, received, land, smix, imix):
    return pl.pallas_call(
        export_kernel,
        out_shape=shaped((TURNED, COLS), bf16),
        in_specs=[HBM] * 5,
        out_specs=VMEM,
        scratch_shapes=[
            pltpu.VMEM((FIELDS, FIELDS), f32),
            pltpu.VMEM((FIELDS, FIELDS), f32),
            pltpu.VMEM((FIELDS, ROWS, COLS), f32),
            pltpu.VMEM((FIELDS, ROWS, COLS), f32),
            pltpu.VMEM((ROWS, COLS), jnp.int32),
            pltpu.VMEM((2, TURNED, LANES), f32),
            pltpu.SemaphoreType.DMA((5,)),
        ],
        compiler_params=params(56),
        name="export",
    )(smix, imix, fields, received, land)


def split_to(ref, at, low_at, value):
    high = value.astype(bf16)
    ref[at] = high
    ref[low_at] = (value - high.astype(f32)).astype(bf16)


def write_main(ref, tracer_at, wave_at, wave_low_at, fields_ref):
    for half in range(2):
        cols = slice(half * LANES, (half + 1) * LANES)
        for i in range(TRACERS):
            ref[tracer_at + 2 * i + half] = fields_ref[WAVES + i, :, cols].astype(bf16)
        for i in range(WAVES):
            split_to(ref, wave_at + 2 * i + half, wave_low_at + 2 * i + half, fields_ref[i, :, cols])


def pack_kernel(opposite_ref, fields_ref, index_ref, config_ref, near_ref):
    del index_ref, config_ref
    write_main(near_ref, 0, A_WAVE, A_WAVE + 6, fields_ref)
    for half in range(2):
        for i in range(TURNED // 16):
            near_ref[A_EXPORT + half * 8 + i] = opposite_ref[16 * i : 16 * i + 16, half * LANES : (half + 1) * LANES]


def pack(opposite, fields, index, config):
    return pl.pallas_call(
        pack_kernel,
        out_shape=shaped((A_PLANES, ROWS, LANES), bf16),
        in_specs=[VMEM] * 2 + [HBM] * 2,
        out_specs=VMEM,
        compiler_params=params(),
        name="pack",
    )(opposite, fields, index, config)


def pack_forcing_kernel(
    config_ref, forcing_ref, outer_ref, chip_ref, state_c_ref, state_i_ref,
    out_c_ref, out_i_ref, far_ref, left_ref, right_ref,
):
    odd = spread(config_ref, GY_ODD, ROWS) > 0.5
    for p in range(4):
        left_ref[p] = jnp.where(odd, chip_ref[p], outer_ref[p])
        right_ref[p] = jnp.where(odd, outer_ref[p], chip_ref[p])
    for ref, behind in ((out_c_ref, state_i_ref), (out_i_ref, state_c_ref)):
        write_main(ref, 0, B_WAVE + 2, B_WAVE + 10, forcing_ref)
        for k, strips in enumerate((left_ref, right_ref)):
            ref[10 + k] = strips[0].astype(bf16)
            split_to(ref, B_WAVE + k, B_WAVE + 8 + k, strips[1])
            ref[B_STRIP_T + k] = strips[2].astype(bf16)
            split_to(ref, B_STRIP_W + k, B_STRIP_W + 2 + k, strips[3])
        for p in range(6):
            ref[B_BEHIND + p] = behind[A_WAVE + p]
    for p in range(8):
        far_ref[p] = out_c_ref[B_WAVE + p]
    for p in range(2):
        far_ref[C_STRIP_W + p] = out_c_ref[B_STRIP_W + p]


def pack_forcing(config, forcing, outer, chip, state_c, state_i):
    payload, strips = shaped((B_PLANES, ROWS, LANES), bf16), shaped((4, ROWS, LANES))
    return pl.pallas_call(
        pack_forcing_kernel,
        out_shape=(payload, payload, shaped((C_PLANES, ROWS, LANES), bf16), strips, strips),
        in_specs=[VMEM] * 6,
        out_specs=(VMEM,) * 5,
        compiler_params=params(),
        name="pack_forcing",
    )(config, forcing, outer, chip, state_c, state_i)


def stage_kernel(weight_ref, near_c_ref, near_i_ref, out_ref):
    del near_c_ref, near_i_ref
    out_ref[...] = weight_ref[...]


def stage(weight, near_c, near_i):
    return pl.pallas_call(
        stage_kernel,
        out_shape=shaped(weight.shape, weight.dtype),
        in_specs=[VMEM, HBM, HBM],
        out_specs=VMEM,
        compiler_params=params(),
        name="stage_weights",
    )(weight, near_c, near_i)


def remap_kernel(
    index_ref, far_i_ref, near_i_ref, opposite_ref, near_c_ref, far_c_ref, weight_ref, land_ref, fields_ref,
    forcing_ref, chip_ref, outer_ref, import_ref, table, turned,
):
    half_count = 5 * ROWS * 2
    windows = [far_c_ref, near_c_ref, opposite_ref, near_i_ref, far_i_ref]
    for w, ref in enumerate(windows):
        for half in range(2):
            for i in range(TURNED // 16):
                if w in (1, 3):
                    chunk = ref[A_EXPORT + half * 8 + i]
                else:
                    chunk = ref[16 * i : 16 * i + 16, half * LANES : (half + 1) * LANES]
                chunk = chunk.astype(f32)
                for sub in range(2):
                    part = chunk[sub * 8 : sub * 8 + 8]
                    at = (w * ROWS + i * 2 + sub) * 2 + half
                    table[at] = part
                    table[half_count + at] = pltpu.roll(part, 64, 1)
    lane8 = lax.broadcasted_iota(jnp.int32, (8, LANES), 1)
    low_half = lane8 < 64
    ones = jnp.ones((8, LANES), f32)
    for x in range(ROWS):
        pieces = []
        for seg in range(4):
            at = (x * 4 + seg) * 2
            pieces.append(jnp.where(low_half, table[index_ref[at]], table[index_ref[at + 1]]))
        picked = jnp.concatenate(pieces + [ones], axis=0).astype(bf16)
        product = lax.dot_general(
            picked, weight_ref[x], (((1,), (1,)), ((), ())), preferred_element_type=f32
        )
        for half in range(2):
            cols = half_of(product, half)
            summed = jnp.where(low_half, cols[16 * half : 16 * half + 8], cols[16 * half + 8 : 16 * half + 16])
            turned[half, x * 8 : x * 8 + 8, :] = summed / cols[32:40]
    wet = land_ref[...].astype(f32)
    forcing = []
    for c in range(FIELDS):
        parts = []
        for half in range(2):
            value = turned[half, pl.ds(c, ROWS, stride=FIELDS), :]
            import_ref[c, :, half * LANES : (half + 1) * LANES] = value
            part = COUPLING * half_of(wet, half) * value
            forcing_ref[c, :, half * LANES : (half + 1) * LANES] = part
            parts.append(part)
        forcing.append(parts)
    state = [[half_of(fields_ref[c], half) for half in range(2)] for c in range(FIELDS)]
    odd = index_ref[TURNED] == 1
    write_strips(forcing, 0, odd, chip_ref, outer_ref)
    write_strips(state, 2, odd, chip_ref, outer_ref)


def remap(index, windows, weight, land, fields):
    strips = shaped((4, ROWS, LANES))
    return pl.pallas_call(
        remap_kernel,
        out_shape=(shaped((FIELDS, ROWS, COLS)), strips, strips, shaped((FIELDS, ROWS, COLS))),
        in_specs=[SMEM] + [VMEM] * 8,
        out_specs=(VMEM,) * 4,
        scratch_shapes=[
            pltpu.VMEM((2 * 5 * ROWS * 2, FIELDS, LANES), f32),
            pltpu.VMEM((2, TURNED, LANES), f32),
        ],
        compiler_params=params(),
        name="remap",
    )(index, *windows, weight, land, fields)


def sides(left, right, j):
    lane = lax.broadcasted_iota(jnp.int32, (ROWS, LANES), 1)
    if j:
        right = pltpu.roll(right, LANES - STRIP * j, 1)
    if j != 3:
        left = pltpu.roll(left, 96 - STRIP * j, 1)
    return jnp.where(lane < STRIP, right, jnp.where(lane >= 96, left, 0.0))


def place_field(dest, start, parts):
    for j, part in enumerate(parts):
        dest[j, start : start + ROWS, :] = part


def joined(ref, at, low_at):
    return ref[at].astype(f32) + ref[low_at].astype(f32)


def inside_tile(config_ref, first_row, count, j, shift=0):
    shape = (count, LANES)
    row = (lax.broadcasted_iota(jnp.int32, shape, 0) + first_row).astype(f32) + spread(config_ref, ROW0, count)
    col = lax.broadcasted_iota(jnp.int32, shape, 1) + j * LANES
    if j == 2:
        col = jnp.where(col >= 3 * LANES - STRIP, col - 3 * LANES, col)
    col = (col + shift).astype(f32) + spread(config_ref, COL0, count)
    ok = (row >= 0.0) & (row < spread(config_ref, ROW_END, count))
    ok = ok & (col >= 0.0) & (col < spread(config_ref, COL_END, count))
    return jnp.where(ok, 1.0, 0.0)


def westward(parts, lane, by=1):
    moved = [pltpu.roll(part, by, 1) for part in parts]
    return [jnp.where(lane < by, moved[j - 1], moved[j]) for j in range(3)]


def eastward(parts, lane, by=1):
    moved = [pltpu.roll(part, LANES - by, 1) for part in parts]
    return [jnp.where(lane >= LANES - by, moved[(j + 1) % 3], moved[j]) for j in range(3)]


def own_parts(fields_ref, left_ref, right_ref, at, i):
    p, j = (0, i - WAVES) if WAVES <= i < FIELDS - 1 else (1, (i + 1) % FIELDS)
    return [
        fields_ref[i, :, :LANES], fields_ref[i, :, LANES:], sides(left_ref[at + p], right_ref[at + p], j),
    ]


def tracer_parts(ref, strip_ref, strip_at, wave_strip_at, i):
    at = strip_at if i < 4 else wave_strip_at
    beside = sides(strip_ref[at].astype(f32), strip_ref[at + 1].astype(f32), i % 4)
    return [ref[2 * i].astype(f32), ref[2 * i + 1].astype(f32), beside]


def wave_main(ref, at, i, low=None):
    planes = [2 * i, 2 * i + 1]
    return [ref[at + p].astype(f32) if low is None else joined(ref, at + p, at + low + p) for p in planes]


def wave_strip(ref, at, i, low=None):
    left, right = [ref[at + k].astype(f32) if low is None else joined(ref, at + k, at + low + k) for k in range(2)]
    return [sides(left, right, i + 1)]


def tracer_kernel(
    last, config_ref, near_c_ref, forcing_ref, left_ref, right_ref, near_i_ref,
    state_c_ref, fields_ref, state_i_ref, *refs
):
    if last:
        received_ref, out_ref, received_out, state, forcing, coef = refs
        received_out[...] = received_ref[...]
    else:
        out_ref, state, forcing, coef = refs
    after = spread(config_ref, AFTER_NEAR, ROWS) > 0.5
    for i in range(TRACERS):
        pushed, parts = [], []
        for near, main in ((near_c_ref, state_c_ref), (near_i_ref, state_i_ref)):
            pushed.append(tracer_parts(near, near, 10, B_WAVE, i))
            parts.append(tracer_parts(main, near, B_STRIP_T, B_STRIP_W, i))
        place_field(forcing.at[i], 0, chosen(after, pushed[1], pushed[0]))
        place_field(forcing.at[i], ROWS, own_parts(forcing_ref, left_ref, right_ref, 0, WAVES + i))
        place_field(forcing.at[i], 2 * ROWS, chosen(after, pushed[0], pushed[1]))
        place_field(state.at[0, i], PAD, chosen(after, parts[1], parts[0]))
        place_field(state.at[0, i], PAD + ROWS, own_parts(fields_ref, left_ref, right_ref, 2, WAVES + i))
        place_field(state.at[0, i], PAD + 2 * ROWS, chosen(after, parts[0], parts[1]))
    height = 3 * ROWS
    for k in range(2):
        for i in range(TRACERS):
            for j in range(3):
                state[k, i, j, 0:PAD, :] = jnp.zeros((PAD, LANES), f32)
                state[k, i, j, PAD + height : height + 2 * PAD, :] = jnp.zeros((PAD, LANES), f32)
    for j in range(3):
        coef[j] = inside_tile(config_ref, -ROWS, height, j) * DIFFUSION

    lane = lax.broadcasted_iota(jnp.int32, (8, LANES), 1)
    keep = [(1.0 - spread(config_ref, WAVES + c)) - 4.0 * DIFFUSION for c in range(TRACERS)]

    def step(source, dest, first, count):
        for t in range(first, first + count):
            at = PAD + 8 * t
            here = slice(8 * t, 8 * t + 8)
            for c in range(TRACERS):
                mid = [state[source, c, j, at : at + 8, :] for j in range(3)]
                west = westward(mid, lane)
                east = eastward(mid, lane)
                for j in range(3):
                    above = state[source, c, j, at + 1 : at + 9, :]
                    below = state[source, c, j, at - 1 : at + 7, :]
                    around = (above + below) + (east[j] + west[j])
                    state[dest, c, j, at : at + 8, :] = (
                        keep[c] * mid[j] + forcing[c, j, here, :]
                    ) + coef[j, here, :] * around

    def pair_of_steps(first, count):
        def run(_, carry):
            step(0, 1, first, count)
            step(1, 0, first, count)
            return carry
        return run

    lax.fori_loop(0, SUBSTEPS // 4, pair_of_steps(0, 6), 0)
    lax.fori_loop(0, SUBSTEPS // 4, pair_of_steps(1, 4), 0)
    for i in range(TRACERS):
        for half in range(2):
            out_ref[i, :, half * LANES : (half + 1) * LANES] = state[0, i, half, PAD + ROWS : PAD + 2 * ROWS, :]


def tracer_steps(last, config, operands):
    tracers, received = shaped((TRACERS, ROWS, COLS)), shaped((FIELDS, ROWS, COLS))
    return pl.pallas_call(
        lambda *refs: tracer_kernel(last, *refs),
        out_shape=(tracers, received) if last else tracers,
        in_specs=[VMEM] * (1 + len(operands)),
        out_specs=(VMEM, VMEM) if last else VMEM,
        scratch_shapes=[
            pltpu.VMEM((2, TRACERS, 3, 3 * ROWS + 2 * PAD, LANES), f32),
            pltpu.VMEM((TRACERS, 3, 3 * ROWS, LANES), f32),
            pltpu.VMEM((3, 3 * ROWS, LANES), f32),
        ],
        compiler_params=params(),
        cost_estimate=pl.CostEstimate(flops=10_000_000, bytes_accessed=4_000_000, transcendentals=0),
        name="tracer_steps",
    )(config, *operands)


def wave_kernel(last, config_ref, *refs):
    if not last:
        smix_ref, imix_ref, *refs = refs
    (far_i, near_c, forcing_ref, left_ref, right_ref, near_i, far_c,
     state_c, fields_ref, state_i, tracers_ref, *refs) = refs
    if last:
        out_ref, state, forcing, coef = refs
    else:
        received_ref, land_ref, out_ref, export_ref, state, forcing, coef, turned = refs
    height = 5 * ROWS
    tiles = height // 8

    after = spread(config_ref, AFTER_NEAR, ROWS) > 0.5
    after_far = spread(config_ref, AFTER_FAR, ROWS) > 0.5
    for i in range(WAVES):
        place_field(forcing.at[i], PAD + 2 * ROWS, own_parts(forcing_ref, left_ref, right_ref, 0, i))
        place_field(state.at[i], PAD + 2 * ROWS, own_parts(fields_ref, left_ref, right_ref, 2, i))
        pushed, parts, behind = [], [], []
        for near, main in ((near_c, state_c), (near_i, state_i)):
            pushed.append(wave_main(near, B_WAVE + 2, i, 8) + wave_strip(near, B_WAVE, i, 8))
            parts.append(wave_main(main, A_WAVE, i, 6) + wave_strip(near, B_STRIP_W, i, 2))
            behind.append(wave_main(near, B_BEHIND, i))
        far_pushed = [wave_main(far, 2, i) + wave_strip(far, 0, i) for far in (far_c, far_i)]
        far_strip = [wave_strip(far, C_STRIP_W, i) for far in (far_c, far_i)]
        for k, slot in ((1, 0), (0, 4)):
            near_slot = (slot + 2) // 2
            place_field(forcing.at[i], PAD + near_slot * ROWS, chosen(after, pushed[k], pushed[1 - k]))
            place_field(state.at[i], PAD + near_slot * ROWS, chosen(after, parts[k], parts[1 - k]))
            place_field(forcing.at[i], PAD + slot * ROWS, chosen(after_far, far_pushed[k], far_pushed[1 - k]))
            main = chosen(after, behind[k], behind[1 - k])
            strip = chosen(after_far, far_strip[k], far_strip[1 - k])
            place_field(state.at[i], PAD + slot * ROWS, main + strip)
        for j in range(3):
            for ref in (state, forcing):
                ref[i, j, 0:PAD, :] = jnp.zeros((PAD, LANES), f32)
                ref[i, j, PAD + height : height + 2 * PAD, :] = jnp.zeros((PAD, LANES), f32)
    half_a = 0.5 * config_ref[:, WAVE_SPEED : WAVE_SPEED + 1]
    half_b = 0.5 * config_ref[:, WAVE_SPEED + 1 : WAVE_SPEED + 2]
    first_row = -2 * ROWS
    for j in range(3):
        coef[0, j] = inside_tile(config_ref, first_row, height, j) * half_a
        coef[1, j] = inside_tile(config_ref, first_row + 1, height, j) * half_b
        coef[2, j] = inside_tile(config_ref, first_row - 1, height, j) * half_b
        coef[3, j] = inside_tile(config_ref, first_row, height, j, 1) * half_b
        coef[4, j] = inside_tile(config_ref, first_row, height, j, -1) * half_b

    lane = lax.broadcasted_iota(jnp.int32, (8, LANES), 1)
    keep = [1.0 - spread(config_ref, c) for c in range(WAVES)]

    def load(ref, i, t, by=0):
        at = PAD + 8 * t + by
        return [ref[i, j, at : at + 8, :] for j in range(3)]

    def along(ref, i, t):
        ahead, behind = load(ref, i, t, 1), load(ref, i, t, -1)
        return [ahead[j] - behind[j] for j in range(3)]

    def across(parts):
        ahead, behind = eastward(parts, lane), westward(parts, lane)
        return [ahead[j] - behind[j] for j in range(3)]

    h = [load(state, 0, t) for t in range(tiles)]
    du = [along(state, 1, t) for t in range(tiles)]
    dv = [across(load(state, 2, t)) for t in range(tiles)]
    for t in range(tiles):
        at = PAD + 8 * t
        push_u, push_v = along(forcing, 1, t), across(load(forcing, 2, t))
        for j in range(3):
            coef[5, j, 8 * t : 8 * t + 8, :] = push_u[j]
            coef[6, j, 8 * t : 8 * t + 8, :] = push_v[j]
    own = (4, 5)
    sum_u = {t: [jnp.zeros((8, LANES), f32)] * 2 for t in (3, 4, 5, 6)}
    sum_v = {t: [jnp.zeros((8, LANES), f32)] * 3 for t in own}
    for step in range(SUBSTEPS):
        first = step // STEPS_PER_PHASE
        final = step == SUBSTEPS - 1
        span = range(first, tiles - first)
        for t in span:
            here = slice(8 * t, 8 * t + 8)
            push = load(forcing, 0, t)
            for j in range(3):
                h[t][j] = (keep[0] * h[t][j] + push[j]) - coef[0, j, here, :] * (du[t][j] + dv[t][j])
                if not final:
                    state[0, j, PAD + 8 * t : PAD + 8 * t + 8, :] = h[t][j]
        for t in sum_u:
            sum_u[t] = [keep[1] * sum_u[t][j] + h[t][j] for j in range(2)]
        for t in own:
            sum_v[t] = [keep[2] * sum_v[t][j] + h[t][j] for j in range(3)]
        if final:
            break
        for t in span:
            here = slice(8 * t, 8 * t + 8)
            east, west = eastward(h[t], lane, 2), westward(h[t], lane, 2)
            up, down = load(state, 0, t, 2), load(state, 0, t, -2)
            for j in range(3):
                mid = h[t][j]
                du[t][j] = (keep[1] * du[t][j] + coef[5, j, here, :]) - (
                    coef[1, j, here, :] * (up[j] - mid) - coef[2, j, here, :] * (mid - down[j])
                )
                dv[t][j] = (keep[2] * dv[t][j] + coef[6, j, here, :]) - (
                    coef[3, j, here, :] * (east[j] - mid) - coef[4, j, here, :] * (mid - west[j])
                )

    def decays(c):
        power, total = c, 1.0 + 0.0 * c
        for _ in range(SUBSTEPS - 1):
            total = total + power
            power = power * c
        return power, total

    for t in sum_u:
        for j in range(2):
            state[0, j, PAD + 8 * t : PAD + 8 * t + 8, :] = sum_u[t][j]
    power_u, total_u = decays(keep[1])
    power_v, total_v = decays(keep[2])
    for j in range(2):
        inside = inside_tile(config_ref, 0, ROWS, j) * half_b
        for t in own:
            at = PAD + 8 * t
            rows = slice(8 * (t - 4), 8 * (t - 4) + 8)
            factor = inside[rows]
            slope_u = state[0, j, at + 1 : at + 9, :] - state[0, j, at - 1 : at + 7, :]
            slope_v = across(sum_v[t])[j]
            new_u = power_u * state[1, j, at : at + 8, :] + total_u * forcing[1, j, at : at + 8, :] - factor * slope_u
            new_v = power_v * state[2, j, at : at + 8, :] + total_v * forcing[2, j, at : at + 8, :] - factor * slope_v
            cols = slice(j * LANES, (j + 1) * LANES)
            out_ref[0, rows, cols] = h[t][j]
            out_ref[1, rows, cols] = new_u
            out_ref[2, rows, cols] = new_v
    for i in range(TRACERS):
        out_ref[WAVES + i] = tracers_ref[i]
    if not last:
        fields = [out_ref[c] for c in range(FIELDS)]
        received = [received_ref[c] for c in range(FIELDS)]
        write_export(fields, received, land_ref[...].astype(f32), smix_ref, imix_ref, turned, export_ref)


def wave_steps(last, config, mixes, operands):
    state = shaped((FIELDS, ROWS, COLS))
    scratch = [
        pltpu.VMEM((WAVES, 3, 5 * ROWS + 2 * PAD, LANES), f32),
        pltpu.VMEM((WAVES, 3, 5 * ROWS + 2 * PAD, LANES), f32),
        pltpu.VMEM((7, 3, 5 * ROWS, LANES), f32),
    ]
    if not last:
        scratch.append(pltpu.VMEM((2, TURNED, LANES), f32))
    return pl.pallas_call(
        lambda *refs: wave_kernel(last, *refs),
        out_shape=state if last else (state, shaped((TURNED, COLS), bf16)),
        in_specs=[VMEM] * (1 + len(mixes) + len(operands)),
        out_specs=VMEM if last else (VMEM,) * 2,
        scratch_shapes=scratch,
        compiler_params=params(),
        name="wave_steps_last" if last else "wave_steps",
    )(config, *mixes, *operands)


def exchanged(block, axis, distance, phase):
    count = lax.axis_size(axis)
    route = []
    for low in range(count - distance):
        if (low // distance) % 2 == phase:
            route += [(low, low + distance), (low + distance, low)]
    return lax.ppermute(block, axis, route)


def local(
    section_state, prev_import, land_mask, state_mix, import_mix, damping, wave_speed,
    remap_owner, remap_slot, remap_weight,
):
    smix = state_mix[0]
    imix = import_mix[0]
    gx = lax.axis_index("gx")
    gy = lax.axis_index("gy")
    side_near = 1 - 2 * (gx % 2)
    side_far = 1 - 2 * ((gx // 2) % 2)
    place = jnp.stack([
        gx * ROWS, gy * COLS, lax.axis_size("gx") * ROWS, lax.axis_size("gy") * COLS,
        gx % 2, (gx // 2) % 2, gy % 2,
    ])
    config = jnp.concatenate([damping[0], wave_speed[0], place.astype(f32)])[None]
    owner = remap_owner[0].reshape(-1)
    slot = remap_slot[0].reshape(-1)
    away = owner - gx
    window = 2 + away * jnp.where(away % 2 == 1, side_near, side_far)
    entry = (window * ROWS + slot // 4) * 2 + (slot % 4) // 2
    second = lax.iota(jnp.int32, owner.shape[0]) % 2
    index = entry + ((slot % 2) ^ second) * (5 * ROWS * 2)
    index = jnp.concatenate([index, (gy % 2).astype(jnp.int32)[None]])
    weight = remap_weight[0].reshape(ROWS, COLS, 128)

    fields, land = section_state[0], land_mask[0]
    exported = export(fields, prev_import[0], land, smix, imix)
    for interval in range(ITERS):
        last = interval == ITERS - 1
        opposite = lax.ppermute(exported, "sec", [(0, 1), (1, 0)])
        near = pack(opposite, fields, index, config)
        state_c = exchanged(near, "gx", 1, 1)
        state_i = exchanged(near, "gx", 1, 0)
        export_c = exchanged(opposite, "gx", 2, 1)
        export_i = exchanged(opposite, "gx", 2, 0)
        if interval == 0:
            weight = stage(weight, state_c, state_i)
        forcing, to_chip, to_outer, received = remap(
            index, (export_i, state_i, opposite, state_c, export_c), weight, land, fields
        )
        outer = exchanged(to_outer, "gy", 1, 1)
        chip = exchanged(to_chip, "gy", 1, 0)
        out_c, out_i, outer, left, right = pack_forcing(config, forcing, outer, chip, state_c, state_i)
        near_c = exchanged(out_c, "gx", 1, 1)
        near_i = exchanged(out_i, "gx", 1, 0)
        far_c = exchanged(outer, "gx", 2, 1)
        far_i = exchanged(outer, "gx", 2, 0)
        own = (forcing, left, right)
        state = (state_c, fields, state_i)
        operands = (near_c, *own, near_i, *state)
        if last:
            tracers, received = tracer_steps(last, config, operands + (received,))
        else:
            tracers = tracer_steps(last, config, operands)
        operands = (far_i, near_c, *own, near_i, far_c, *state, tracers)
        if last:
            fields = wave_steps(last, config, (), operands)
        else:
            operands += (received, land)
            fields, exported = wave_steps(last, config, (smix, imix), operands)
    return (fields[None], received[None])


def solution(mesh):
    in_specs = (
        P("sec", None, "gx", "gy"),
        P("sec", None, "gx", "gy"),
        P("sec", "gx", "gy"),
        P("sec", None, None),
        P("sec", None, None),
        P("sec", None),
        P("sec", None),
        P("sec", "gx", "gy", None),
        P("sec", "gx", "gy", None),
        P("sec", "gx", "gy", None, None),
    )
    out_specs = (P("sec", None, "gx", "gy"), P("sec", None, "gx", "gy"))
    return jax.shard_map(local, mesh=mesh, in_specs=in_specs, out_specs=out_specs, check_vma=False)
```

```python
import jax
import jax.numpy as jnp
from jax import lax
from jax.experimental import pallas as pl
from jax.experimental.pallas import tpu as pltpu
from jax.sharding import PartitionSpec as P

SUBSTEPS = 16
ITERS = 2
DIFFUSION = 0.1
COUPLING = 0.2

FIELDS = 8
WAVES = 3
TRACERS = 5
ROWS = 16
COLS = 256
LANES = 128
TURNED = ROWS * FIELDS
STRIP = 32
STEPS_PER_PHASE = 4

A_WAVE = 10
A_EXPORT = 22
A_PLANES = 38
B_WAVE = 12
B_STRIP_T = 28
B_STRIP_W = 30
B_BEHIND = 34
B_PLANES = 40
C_STRIP_W = 8
C_PLANES = 10

PAD = 8
WAVE_SPEED = 8
ROW0, COL0, ROW_END, COL_END, AFTER_NEAR, AFTER_FAR, GY_ODD = range(10, 17)
SMEM = pl.BlockSpec(memory_space=pltpu.SMEM)
VMEM = pl.BlockSpec(memory_space=pltpu.VMEM)
HBM = pl.BlockSpec(memory_space=pl.ANY)

f32 = jnp.float32
bf16 = jnp.bfloat16


def params(mib=24):
    return pltpu.CompilerParams(vmem_limit_bytes=mib * 1024 * 1024)


def shaped(shape, dtype=f32):
    return jax.ShapeDtypeStruct(shape, dtype)


def spread(config_ref, k, rows=8):
    return jnp.broadcast_to(config_ref[:, k : k + 1], (rows, LANES))


def chosen(flag, ones, others):
    return [jnp.where(flag, one, other) for one, other in zip(ones, others)]


def half_of(value, half):
    return value[:, half * LANES : (half + 1) * LANES]


def write_export(fields, received, wet, smix_ref, imix_ref, turned, out_ref):
    scale = wet * jnp.sqrt(1.0 + fields[1] * fields[1] + fields[2] * fields[2])
    for c in range(FIELDS):
        total = smix_ref[c : c + 1, 0:1] * fields[0]
        for k in range(1, FIELDS):
            total = total + smix_ref[c : c + 1, k : k + 1] * fields[k]
        other = imix_ref[c : c + 1, 0:1] * received[0]
        for k in range(1, FIELDS):
            other = other + imix_ref[c : c + 1, k : k + 1] * received[k]
        value = scale * (total + other)
        for half in range(2):
            turned[half, pl.ds(c, ROWS, stride=FIELDS), :] = half_of(value, half)
    for half in range(2):
        out_ref[:, half * LANES : (half + 1) * LANES] = turned[half].astype(bf16)


def write_strips(fields, at, odd, chip_ref, outer_ref):
    lane = lax.broadcasted_iota(jnp.int32, (ROWS, LANES), 1)
    groups = [fields[3:7], [fields[7]] + fields[0:3]]
    for p, group in enumerate(groups):
        first = group[0][0]
        last = pltpu.roll(group[0][1], STRIP, 1)
        for j in range(1, 4):
            here = lane >= STRIP * j
            first = jnp.where(here, pltpu.roll(group[j][0], STRIP * j, 1), first)
            moved = group[j][1] if j == 3 else pltpu.roll(group[j][1], STRIP * (j + 1), 1)
            last = jnp.where(here, moved, last)
        chip_ref[at + p] = jnp.where(odd, first, last)
        outer_ref[at + p] = jnp.where(odd, last, first)


def export_kernel(
    smix_hbm, imix_hbm, fields_hbm, received_hbm, land_hbm, out_ref,
    smix_ref, imix_ref, fields_ref, received_ref, land_ref, turned, sems,
):
    pairs = (
        (fields_hbm, fields_ref), (received_hbm, received_ref), (land_hbm, land_ref),
        (smix_hbm, smix_ref), (imix_hbm, imix_ref),
    )
    copies = [pltpu.make_async_copy(source, dest, sems.at[k]) for k, (source, dest) in enumerate(pairs)]
    for copy in copies:
        copy.start()
    for copy in copies:
        copy.wait()
    fields = [fields_ref[c] for c in range(FIELDS)]
    received = [received_ref[c] for c in range(FIELDS)]
    write_export(fields, received, land_ref[...].astype(f32), smix_ref, imix_ref, turned, out_ref)


def export(fields, received, land, smix, imix):
    return pl.pallas_call(
        export_kernel,
        out_shape=shaped((TURNED, COLS), bf16),
        in_specs=[HBM] * 5,
        out_specs=VMEM,
        scratch_shapes=[
            pltpu.VMEM((FIELDS, FIELDS), f32),
            pltpu.VMEM((FIELDS, FIELDS), f32),
            pltpu.VMEM((FIELDS, ROWS, COLS), f32),
            pltpu.VMEM((FIELDS, ROWS, COLS), f32),
            pltpu.VMEM((ROWS, COLS), jnp.int32),
            pltpu.VMEM((2, TURNED, LANES), f32),
            pltpu.SemaphoreType.DMA((5,)),
        ],
        compiler_params=params(56),
        name="export",
    )(smix, imix, fields, received, land)


def split_to(ref, at, low_at, value):
    high = value.astype(bf16)
    ref[at] = high
    ref[low_at] = (value - high.astype(f32)).astype(bf16)


def write_main(ref, tracer_at, wave_at, wave_low_at, fields_ref):
    for half in range(2):
        cols = slice(half * LANES, (half + 1) * LANES)
        for i in range(TRACERS):
            ref[tracer_at + 2 * i + half] = fields_ref[WAVES + i, :, cols].astype(bf16)
        for i in range(WAVES):
            split_to(ref, wave_at + 2 * i + half, wave_low_at + 2 * i + half, fields_ref[i, :, cols])


def pack_kernel(opposite_ref, fields_ref, index_ref, config_ref, mixes_ref, near_ref):
    del index_ref, config_ref, mixes_ref
    write_main(near_ref, 0, A_WAVE, A_WAVE + 6, fields_ref)
    for half in range(2):
        for i in range(TURNED // 16):
            near_ref[A_EXPORT + half * 8 + i] = opposite_ref[16 * i : 16 * i + 16, half * LANES : (half + 1) * LANES]


def pack(opposite, fields, index, config, mixes):
    return pl.pallas_call(
        pack_kernel,
        out_shape=shaped((A_PLANES, ROWS, LANES), bf16),
        in_specs=[VMEM] * 2 + [HBM] * 3,
        out_specs=VMEM,
        compiler_params=params(),
        name="pack",
    )(opposite, fields, index, config, mixes)


def pack_forcing_kernel(
    config_ref, forcing_ref, outer_ref, chip_ref, state_c_ref, state_i_ref,
    out_c_ref, out_i_ref, far_ref, left_ref, right_ref,
):
    odd = spread(config_ref, GY_ODD, ROWS) > 0.5
    for p in range(4):
        left_ref[p] = jnp.where(odd, chip_ref[p], outer_ref[p])
        right_ref[p] = jnp.where(odd, outer_ref[p], chip_ref[p])
    for ref, behind in ((out_c_ref, state_i_ref), (out_i_ref, state_c_ref)):
        write_main(ref, 0, B_WAVE + 2, B_WAVE + 10, forcing_ref)
        for k, strips in enumerate((left_ref, right_ref)):
            ref[10 + k] = strips[0].astype(bf16)
            split_to(ref, B_WAVE + k, B_WAVE + 8 + k, strips[1])
            ref[B_STRIP_T + k] = strips[2].astype(bf16)
            split_to(ref, B_STRIP_W + k, B_STRIP_W + 2 + k, strips[3])
        for p in range(6):
            ref[B_BEHIND + p] = behind[A_WAVE + p]
    for p in range(8):
        far_ref[p] = out_c_ref[B_WAVE + p]
    for p in range(2):
        far_ref[C_STRIP_W + p] = out_c_ref[B_STRIP_W + p]


def pack_forcing(config, forcing, outer, chip, state_c, state_i):
    payload, strips = shaped((B_PLANES, ROWS, LANES), bf16), shaped((4, ROWS, LANES))
    return pl.pallas_call(
        pack_forcing_kernel,
        out_shape=(payload, payload, shaped((C_PLANES, ROWS, LANES), bf16), strips, strips),
        in_specs=[VMEM] * 6,
        out_specs=(VMEM,) * 5,
        compiler_params=params(),
        name="pack_forcing",
    )(config, forcing, outer, chip, state_c, state_i)


def stage_kernel(weight_ref, near_c_ref, near_i_ref, out_ref):
    del near_c_ref, near_i_ref
    out_ref[...] = weight_ref[...]


def stage(weight, near_c, near_i):
    return pl.pallas_call(
        stage_kernel,
        out_shape=shaped(weight.shape, weight.dtype),
        in_specs=[VMEM, HBM, HBM],
        out_specs=VMEM,
        compiler_params=params(),
        name="stage_weights",
    )(weight, near_c, near_i)


def remap_kernel(
    index_hbm, far_c_ref, near_c_ref, opposite_ref, near_i_ref, far_i_ref, weight_ref, land_ref, fields_ref,
    forcing_ref, chip_ref, outer_ref, import_ref, table, turned, index_ref, sem,
):
    copy = pltpu.make_async_copy(index_hbm, index_ref, sem)
    copy.start()
    half_count = 5 * ROWS * 2
    windows = [far_c_ref, near_c_ref, opposite_ref, near_i_ref, far_i_ref]
    for w, ref in enumerate(windows):
        for half in range(2):
            for i in range(TURNED // 16):
                if w in (1, 3):
                    chunk = ref[A_EXPORT + half * 8 + i]
                else:
                    chunk = ref[16 * i : 16 * i + 16, half * LANES : (half + 1) * LANES]
                chunk = chunk.astype(f32)
                for sub in range(2):
                    part = chunk[sub * 8 : sub * 8 + 8]
                    at = (w * ROWS + i * 2 + sub) * 2 + half
                    table[at] = part
                    table[half_count + at] = pltpu.roll(part, 64, 1)
    lane8 = lax.broadcasted_iota(jnp.int32, (8, LANES), 1)
    low_half = lane8 < 64
    ones = jnp.ones((8, LANES), f32)
    copy.wait()
    for x in range(ROWS):
        pieces = []
        for seg in range(4):
            at = (x * 4 + seg) * 2
            pieces.append(jnp.where(low_half, table[index_ref[at]], table[index_ref[at + 1]]))
        picked = jnp.concatenate(pieces + [ones], axis=0).astype(bf16)
        product = lax.dot_general(
            picked, weight_ref[x], (((1,), (1,)), ((), ())), preferred_element_type=f32
        )
        for half in range(2):
            cols = half_of(product, half)
            summed = jnp.where(low_half, cols[16 * half : 16 * half + 8], cols[16 * half + 8 : 16 * half + 16])
            turned[half, x * 8 : x * 8 + 8, :] = summed / cols[32:40]
    wet = land_ref[...].astype(f32)
    forcing = []
    for c in range(FIELDS):
        parts = []
        for half in range(2):
            value = turned[half, pl.ds(c, ROWS, stride=FIELDS), :]
            import_ref[c, :, half * LANES : (half + 1) * LANES] = value
            part = COUPLING * half_of(wet, half) * value
            forcing_ref[c, :, half * LANES : (half + 1) * LANES] = part
            parts.append(part)
        forcing.append(parts)
    state = [[half_of(fields_ref[c], half) for half in range(2)] for c in range(FIELDS)]
    odd = index_ref[TURNED] == 1
    write_strips(forcing, 0, odd, chip_ref, outer_ref)
    write_strips(state, 2, odd, chip_ref, outer_ref)


def remap(index, windows, weight, land, fields):
    strips = shaped((4, ROWS, LANES))
    return pl.pallas_call(
        remap_kernel,
        out_shape=(shaped((FIELDS, ROWS, COLS)), strips, strips, shaped((FIELDS, ROWS, COLS))),
        in_specs=[HBM] + [VMEM] * 8,
        out_specs=(VMEM,) * 4,
        scratch_shapes=[
            pltpu.VMEM((2 * 5 * ROWS * 2, FIELDS, LANES), f32),
            pltpu.VMEM((2, TURNED, LANES), f32),
            pltpu.SMEM((2 * TURNED,), jnp.int32),
            pltpu.SemaphoreType.DMA,
        ],
        compiler_params=params(),
        name="remap",
    )(index, *windows, weight, land, fields)


def sides(left, right, j):
    lane = lax.broadcasted_iota(jnp.int32, (ROWS, LANES), 1)
    if j:
        right = pltpu.roll(right, LANES - STRIP * j, 1)
    if j != 3:
        left = pltpu.roll(left, 96 - STRIP * j, 1)
    return jnp.where(lane < STRIP, right, jnp.where(lane >= 96, left, 0.0))


def place_field(dest, start, parts):
    for j, part in enumerate(parts):
        dest[j, start : start + ROWS, :] = part


def joined(ref, at, low_at):
    return ref[at].astype(f32) + ref[low_at].astype(f32)


def inside_tile(config_ref, first_row, count, j, shift=0):
    shape = (count, LANES)
    row = (lax.broadcasted_iota(jnp.int32, shape, 0) + first_row).astype(f32) + spread(config_ref, ROW0, count)
    col = lax.broadcasted_iota(jnp.int32, shape, 1) + j * LANES
    if j == 2:
        col = jnp.where(col >= 3 * LANES - STRIP, col - 3 * LANES, col)
    col = (col + shift).astype(f32) + spread(config_ref, COL0, count)
    ok = (row >= 0.0) & (row < spread(config_ref, ROW_END, count))
    ok = ok & (col >= 0.0) & (col < spread(config_ref, COL_END, count))
    return jnp.where(ok, 1.0, 0.0)


def westward(parts, lane, by=1):
    moved = [pltpu.roll(part, by, 1) for part in parts]
    return [jnp.where(lane < by, moved[j - 1], moved[j]) for j in range(3)]


def eastward(parts, lane, by=1):
    moved = [pltpu.roll(part, LANES - by, 1) for part in parts]
    return [jnp.where(lane >= LANES - by, moved[(j + 1) % 3], moved[j]) for j in range(3)]


def own_parts(fields_ref, left_ref, right_ref, at, i):
    p, j = (0, i - WAVES) if WAVES <= i < FIELDS - 1 else (1, (i + 1) % FIELDS)
    return [
        fields_ref[i, :, :LANES], fields_ref[i, :, LANES:], sides(left_ref[at + p], right_ref[at + p], j),
    ]


def tracer_parts(ref, strip_ref, strip_at, wave_strip_at, i):
    at = strip_at if i < 4 else wave_strip_at
    beside = sides(strip_ref[at].astype(f32), strip_ref[at + 1].astype(f32), i % 4)
    return [ref[2 * i].astype(f32), ref[2 * i + 1].astype(f32), beside]


def wave_main(ref, at, i, low=None):
    planes = [2 * i, 2 * i + 1]
    return [ref[at + p].astype(f32) if low is None else joined(ref, at + p, at + low + p) for p in planes]


def wave_strip(ref, at, i, low=None):
    left, right = [ref[at + k].astype(f32) if low is None else joined(ref, at + k, at + low + k) for k in range(2)]
    return [sides(left, right, i + 1)]


def tracer_kernel(
    last, config_ref, near_c_ref, forcing_ref, left_ref, right_ref, near_i_ref,
    state_c_ref, fields_ref, state_i_ref, *refs
):
    if last:
        received_ref, received_out, *refs = refs
        received_out[...] = received_ref[...]
    out_ref, wave_state, wave_forcing, wave_coef, state, forcing, coef = refs
    after = spread(config_ref, AFTER_NEAR, ROWS) > 0.5
    for i in range(TRACERS):
        pushed, parts = [], []
        for near, main in ((near_c_ref, state_c_ref), (near_i_ref, state_i_ref)):
            pushed.append(tracer_parts(near, near, 10, B_WAVE, i))
            parts.append(tracer_parts(main, near, B_STRIP_T, B_STRIP_W, i))
        place_field(forcing.at[i], 0, chosen(after, pushed[1], pushed[0]))
        place_field(forcing.at[i], ROWS, own_parts(forcing_ref, left_ref, right_ref, 0, WAVES + i))
        place_field(forcing.at[i], 2 * ROWS, chosen(after, pushed[0], pushed[1]))
        place_field(state.at[0, i], PAD, chosen(after, parts[1], parts[0]))
        place_field(state.at[0, i], PAD + ROWS, own_parts(fields_ref, left_ref, right_ref, 2, WAVES + i))
        place_field(state.at[0, i], PAD + 2 * ROWS, chosen(after, parts[0], parts[1]))
    for i in range(WAVES):
        pushed, parts = [], []
        for near, main in ((near_c_ref, state_c_ref), (near_i_ref, state_i_ref)):
            pushed.append(wave_main(near, B_WAVE + 2, i, 8) + wave_strip(near, B_WAVE, i, 8))
            parts.append(wave_main(main, A_WAVE, i, 6) + wave_strip(near, B_STRIP_W, i, 2))
        place_field(wave_forcing.at[i], ROWS, own_parts(forcing_ref, left_ref, right_ref, 0, i))
        place_field(wave_state.at[i], ROWS, own_parts(fields_ref, left_ref, right_ref, 2, i))
        for k, slot in ((1, 0), (0, 2)):
            place_field(wave_forcing.at[i], slot * ROWS, chosen(after, pushed[k], pushed[1 - k]))
            place_field(wave_state.at[i], slot * ROWS, chosen(after, parts[k], parts[1 - k]))
    half_a = 0.5 * config_ref[:, WAVE_SPEED : WAVE_SPEED + 1]
    half_b = 0.5 * config_ref[:, WAVE_SPEED + 1 : WAVE_SPEED + 2]
    first_row, rows = -2 * ROWS, 5 * ROWS
    for j in range(3):
        wave_coef[0, j] = inside_tile(config_ref, first_row, rows, j) * half_a
        wave_coef[1, j] = inside_tile(config_ref, first_row + 1, rows, j) * half_b
        wave_coef[2, j] = inside_tile(config_ref, first_row - 1, rows, j) * half_b
        wave_coef[3, j] = inside_tile(config_ref, first_row, rows, j, 1) * half_b
        wave_coef[4, j] = inside_tile(config_ref, first_row, rows, j, -1) * half_b
    height = 3 * ROWS
    for k in range(2):
        for i in range(TRACERS):
            for j in range(3):
                state[k, i, j, 0:PAD, :] = jnp.zeros((PAD, LANES), f32)
                state[k, i, j, PAD + height : height + 2 * PAD, :] = jnp.zeros((PAD, LANES), f32)
    for j in range(3):
        coef[j] = inside_tile(config_ref, -ROWS, height, j) * DIFFUSION

    lane = lax.broadcasted_iota(jnp.int32, (8, LANES), 1)
    keep = [(1.0 - spread(config_ref, WAVES + c)) - 4.0 * DIFFUSION for c in range(TRACERS)]

    def step(source, dest, first, count):
        for t in range(first, first + count):
            at = PAD + 8 * t
            here = slice(8 * t, 8 * t + 8)
            for c in range(TRACERS):
                mid = [state[source, c, j, at : at + 8, :] for j in range(3)]
                west = westward(mid, lane)
                east = eastward(mid, lane)
                for j in range(3):
                    above = state[source, c, j, at + 1 : at + 9, :]
                    below = state[source, c, j, at - 1 : at + 7, :]
                    around = (above + below) + (east[j] + west[j])
                    state[dest, c, j, at : at + 8, :] = (
                        keep[c] * mid[j] + forcing[c, j, here, :]
                    ) + coef[j, here, :] * around

    def pair_of_steps(first, count):
        def run(_, carry):
            step(0, 1, first, count)
            step(1, 0, first, count)
            return carry
        return run

    lax.fori_loop(0, SUBSTEPS // 4, pair_of_steps(0, 6), 0)
    lax.fori_loop(0, SUBSTEPS // 4, pair_of_steps(1, 4), 0)
    for i in range(TRACERS):
        for half in range(2):
            out_ref[i, :, half * LANES : (half + 1) * LANES] = state[0, i, half, PAD + ROWS : PAD + 2 * ROWS, :]


def tracer_steps(last, config, operands):
    inner = shaped((WAVES, 3, 3 * ROWS, LANES))
    outs = [shaped((TRACERS, ROWS, COLS)), inner, inner, shaped((5, 3, 5 * ROWS, LANES))]
    if last:
        outs = [shaped((FIELDS, ROWS, COLS))] + outs
    return pl.pallas_call(
        lambda *refs: tracer_kernel(last, *refs),
        out_shape=tuple(outs),
        in_specs=[VMEM] * (1 + len(operands)),
        out_specs=(VMEM,) * len(outs),
        scratch_shapes=[
            pltpu.VMEM((2, TRACERS, 3, 3 * ROWS + 2 * PAD, LANES), f32),
            pltpu.VMEM((TRACERS, 3, 3 * ROWS, LANES), f32),
            pltpu.VMEM((3, 3 * ROWS, LANES), f32),
        ],
        compiler_params=params(),
        cost_estimate=pl.CostEstimate(flops=10_000_000, bytes_accessed=4_000_000, transcendentals=0),
        name="tracer_steps",
    )(config, *operands)


def wave_kernel(last, config_ref, *refs):
    if not last:
        mixes_ref, *refs = refs
        smix_ref, imix_ref = mixes_ref.at[pl.ds(0, FIELDS)], mixes_ref.at[pl.ds(FIELDS, FIELDS)]
    far_i, near_c, near_i, far_c, tracers_ref, inner_state, inner_forcing, coef, *refs = refs
    if last:
        out_ref, state, forcing, push = refs
    else:
        received_ref, land_ref, out_ref, export_ref, state, forcing, push, turned = refs
    height = 5 * ROWS
    tiles = height // 8

    after = spread(config_ref, AFTER_NEAR, ROWS) > 0.5
    after_far = spread(config_ref, AFTER_FAR, ROWS) > 0.5
    for i in range(WAVES):
        for j in range(3):
            for ref, inner in ((state, inner_state), (forcing, inner_forcing)):
                ref[i, j, PAD + ROWS : PAD + 4 * ROWS, :] = inner[i, j]
                ref[i, j, 0:PAD, :] = jnp.zeros((PAD, LANES), f32)
                ref[i, j, PAD + height : height + 2 * PAD, :] = jnp.zeros((PAD, LANES), f32)
        behind = [wave_main(near, B_BEHIND, i) for near in (near_c, near_i)]
        far_pushed = [wave_main(far, 2, i) + wave_strip(far, 0, i) for far in (far_c, far_i)]
        far_strip = [wave_strip(far, C_STRIP_W, i) for far in (far_c, far_i)]
        for k, slot in ((1, 0), (0, 4)):
            place_field(forcing.at[i], PAD + slot * ROWS, chosen(after_far, far_pushed[k], far_pushed[1 - k]))
            main = chosen(after, behind[k], behind[1 - k])
            strip = chosen(after_far, far_strip[k], far_strip[1 - k])
            place_field(state.at[i], PAD + slot * ROWS, main + strip)
    half_b = 0.5 * config_ref[:, WAVE_SPEED + 1 : WAVE_SPEED + 2]

    lane = lax.broadcasted_iota(jnp.int32, (8, LANES), 1)
    keep = [1.0 - spread(config_ref, c) for c in range(WAVES)]

    def load(ref, i, t, by=0):
        at = PAD + 8 * t + by
        return [ref[i, j, at : at + 8, :] for j in range(3)]

    def along(ref, i, t):
        ahead, behind = load(ref, i, t, 1), load(ref, i, t, -1)
        return [ahead[j] - behind[j] for j in range(3)]

    def across(parts):
        ahead, behind = eastward(parts, lane), westward(parts, lane)
        return [ahead[j] - behind[j] for j in range(3)]

    h = [load(state, 0, t) for t in range(tiles)]
    du = [along(state, 1, t) for t in range(tiles)]
    dv = [across(load(state, 2, t)) for t in range(tiles)]
    for t in range(tiles):
        at = PAD + 8 * t
        push_u, push_v = along(forcing, 1, t), across(load(forcing, 2, t))
        for j in range(3):
            push[0, j, 8 * t : 8 * t + 8, :] = push_u[j]
            push[1, j, 8 * t : 8 * t + 8, :] = push_v[j]
    own = (4, 5)
    sum_u = {t: [jnp.zeros((8, LANES), f32)] * 2 for t in (3, 4, 5, 6)}
    sum_v = {t: [jnp.zeros((8, LANES), f32)] * 3 for t in own}
    for step in range(SUBSTEPS):
        first = step // STEPS_PER_PHASE
        final = step == SUBSTEPS - 1
        span = range(first, tiles - first)
        for t in span:
            here = slice(8 * t, 8 * t + 8)
            lift = load(forcing, 0, t)
            for j in range(3):
                h[t][j] = (keep[0] * h[t][j] + lift[j]) - coef[0, j, here, :] * (du[t][j] + dv[t][j])
                if not final:
                    state[0, j, PAD + 8 * t : PAD + 8 * t + 8, :] = h[t][j]
        for t in sum_u:
            sum_u[t] = [keep[1] * sum_u[t][j] + h[t][j] for j in range(2)]
        for t in own:
            sum_v[t] = [keep[2] * sum_v[t][j] + h[t][j] for j in range(3)]
        if final:
            break
        for t in span:
            here = slice(8 * t, 8 * t + 8)
            east, west = eastward(h[t], lane, 2), westward(h[t], lane, 2)
            up, down = load(state, 0, t, 2), load(state, 0, t, -2)
            for j in range(3):
                mid = h[t][j]
                du[t][j] = (keep[1] * du[t][j] + push[0, j, here, :]) - (
                    coef[1, j, here, :] * (up[j] - mid) - coef[2, j, here, :] * (mid - down[j])
                )
                dv[t][j] = (keep[2] * dv[t][j] + push[1, j, here, :]) - (
                    coef[3, j, here, :] * (east[j] - mid) - coef[4, j, here, :] * (mid - west[j])
                )

    def decays(c):
        power, total = c, 1.0 + 0.0 * c
        for _ in range(SUBSTEPS - 1):
            total = total + power
            power = power * c
        return power, total

    for t in sum_u:
        for j in range(2):
            state[0, j, PAD + 8 * t : PAD + 8 * t + 8, :] = sum_u[t][j]
    power_u, total_u = decays(keep[1])
    power_v, total_v = decays(keep[2])
    for j in range(2):
        inside = inside_tile(config_ref, 0, ROWS, j) * half_b
        for t in own:
            at = PAD + 8 * t
            rows = slice(8 * (t - 4), 8 * (t - 4) + 8)
            factor = inside[rows]
            slope_u = state[0, j, at + 1 : at + 9, :] - state[0, j, at - 1 : at + 7, :]
            slope_v = across(sum_v[t])[j]
            new_u = power_u * state[1, j, at : at + 8, :] + total_u * forcing[1, j, at : at + 8, :] - factor * slope_u
            new_v = power_v * state[2, j, at : at + 8, :] + total_v * forcing[2, j, at : at + 8, :] - factor * slope_v
            cols = slice(j * LANES, (j + 1) * LANES)
            out_ref[0, rows, cols] = h[t][j]
            out_ref[1, rows, cols] = new_u
            out_ref[2, rows, cols] = new_v
    for i in range(TRACERS):
        out_ref[WAVES + i] = tracers_ref[i]
    if not last:
        fields = [out_ref[c] for c in range(FIELDS)]
        received = [received_ref[c] for c in range(FIELDS)]
        write_export(fields, received, land_ref[...].astype(f32), smix_ref, imix_ref, turned, export_ref)


def wave_steps(last, config, mixes, operands):
    state = shaped((FIELDS, ROWS, COLS))
    scratch = [
        pltpu.VMEM((WAVES, 3, 5 * ROWS + 2 * PAD, LANES), f32),
        pltpu.VMEM((WAVES, 3, 5 * ROWS + 2 * PAD, LANES), f32),
        pltpu.VMEM((2, 3, 5 * ROWS, LANES), f32),
    ]
    if not last:
        scratch.append(pltpu.VMEM((2, TURNED, LANES), f32))
    return pl.pallas_call(
        lambda *refs: wave_kernel(last, *refs),
        out_shape=state if last else (state, shaped((TURNED, COLS), bf16)),
        in_specs=[VMEM] * (1 + len(mixes) + len(operands)),
        out_specs=VMEM if last else (VMEM,) * 2,
        scratch_shapes=scratch,
        compiler_params=params(),
        name="wave_steps_last" if last else "wave_steps",
    )(config, *mixes, *operands)


def exchanged(block, axis, distance, phase):
    count = lax.axis_size(axis)
    route = []
    for low in range(count - distance):
        if (low // distance) % 2 == phase:
            route += [(low, low + distance), (low + distance, low)]
    return lax.ppermute(block, axis, route)


def local(
    section_state, prev_import, land_mask, state_mix, import_mix, damping, wave_speed,
    remap_owner, remap_slot, remap_weight,
):
    smix = state_mix[0]
    imix = import_mix[0]
    gx = lax.axis_index("gx")
    gy = lax.axis_index("gy")
    side_near = 1 - 2 * (gx % 2)
    side_far = 1 - 2 * ((gx // 2) % 2)
    place = jnp.stack([
        gx * ROWS, gy * COLS, lax.axis_size("gx") * ROWS, lax.axis_size("gy") * COLS,
        gx % 2, (gx // 2) % 2, gy % 2,
    ])
    config = jnp.concatenate([damping[0], wave_speed[0], place.astype(f32)])[None]
    owner = remap_owner[0].reshape(-1)
    slot = remap_slot[0].reshape(-1)
    away = owner - gx
    window = 2 + away * jnp.where(away % 2 == 1, side_near, side_far)
    entry = (window * ROWS + slot // 4) * 2 + (slot % 4) // 2
    second = lax.iota(jnp.int32, owner.shape[0]) % 2
    index = entry + ((slot % 2) ^ second) * (5 * ROWS * 2)
    index = jnp.concatenate([index, jnp.full((TURNED,), gy % 2, jnp.int32)])
    weight = remap_weight[0].reshape(ROWS, COLS, 128)
    mixes = jnp.concatenate([smix, imix], axis=0)

    fields, land = section_state[0], land_mask[0]
    exported = export(fields, prev_import[0], land, smix, imix)
    for interval in range(ITERS):
        last = interval == ITERS - 1
        opposite = lax.ppermute(exported, "sec", [(0, 1), (1, 0)])
        near = pack(opposite, fields, index, config, mixes)
        state_c = exchanged(near, "gx", 1, 1)
        state_i = exchanged(near, "gx", 1, 0)
        export_c = exchanged(opposite, "gx", 2, 1)
        export_i = exchanged(opposite, "gx", 2, 0)
        if interval == 0:
            weight = stage(weight, state_c, state_i)
        forcing, to_chip, to_outer, received = remap(
            index, (export_c, state_c, opposite, state_i, export_i), weight, land, fields
        )
        outer = exchanged(to_outer, "gy", 1, 1)
        chip = exchanged(to_chip, "gy", 1, 0)
        out_c, out_i, outer, left, right = pack_forcing(config, forcing, outer, chip, state_c, state_i)
        near_c = exchanged(out_c, "gx", 1, 1)
        near_i = exchanged(out_i, "gx", 1, 0)
        far_c = exchanged(outer, "gx", 2, 1)
        far_i = exchanged(outer, "gx", 2, 0)
        own = (forcing, left, right)
        state = (state_c, fields, state_i)
        operands = (near_c, *own, near_i, *state)
        if last:
            received, *prepared = tracer_steps(last, config, operands + (received,))
        else:
            prepared = tracer_steps(last, config, operands)
        operands = (far_i, near_c, near_i, far_c, *prepared)
        if last:
            fields = wave_steps(last, config, (), operands)
        else:
            operands += (received, land)
            fields, exported = wave_steps(last, config, (mixes,), operands)
    return (fields[None], received[None])


def solution(mesh):
    in_specs = (
        P("sec", None, "gx", "gy"),
        P("sec", None, "gx", "gy"),
        P("sec", "gx", "gy"),
        P("sec", None, None),
        P("sec", None, None),
        P("sec", None),
        P("sec", None),
        P("sec", "gx", "gy", None),
        P("sec", "gx", "gy", None),
        P("sec", "gx", "gy", None, None),
    )
    out_specs = (P("sec", None, "gx", "gy"), P("sec", None, "gx", "gy"))
    return jax.shard_map(local, mesh=mesh, in_specs=in_specs, out_specs=out_specs, check_vma=False)
```

```python
import jax
import jax.numpy as jnp
from jax import lax
from jax.experimental import pallas as pl
from jax.experimental.pallas import tpu as pltpu
from jax.sharding import PartitionSpec as P

SUBSTEPS = 16
ITERS = 2
DIFFUSION = 0.1
COUPLING = 0.2

FIELDS = 8
WAVES = 3
TRACERS = 5
ROWS = 16
COLS = 256
LANES = 128
TURNED = ROWS * FIELDS
STRIP = 32
STEPS_PER_PHASE = 4

A_WAVE = 10
A_EXPORT = 22
A_PLANES = 38
B_WAVE = 12
B_STRIP_T = 28
B_STRIP_W = 30
B_BEHIND = 34
B_PLANES = 40
C_STRIP_W = 8
C_PLANES = 10

PAD = 8
WAVE_SPEED = 8
ROW0, COL0, ROW_END, COL_END, AFTER_NEAR, AFTER_FAR, GY_ODD = range(10, 17)
SMEM = pl.BlockSpec(memory_space=pltpu.SMEM)
VMEM = pl.BlockSpec(memory_space=pltpu.VMEM)
HBM = pl.BlockSpec(memory_space=pl.ANY)

f32 = jnp.float32
bf16 = jnp.bfloat16


def params(mib=24):
    return pltpu.CompilerParams(vmem_limit_bytes=mib * 1024 * 1024)


def shaped(shape, dtype=f32):
    return jax.ShapeDtypeStruct(shape, dtype)


def spread(config_ref, k, rows=8):
    return jnp.broadcast_to(config_ref[:, k : k + 1], (rows, LANES))


def chosen(flag, ones, others):
    return [jnp.where(flag, one, other) for one, other in zip(ones, others)]


def half_of(value, half):
    return value[:, half * LANES : (half + 1) * LANES]


def write_export(fields, received, wet, smix_ref, imix_ref, turned, out_ref):
    scale = wet * jnp.sqrt(1.0 + fields[1] * fields[1] + fields[2] * fields[2])
    for c in range(FIELDS):
        total = smix_ref[c : c + 1, 0:1] * fields[0]
        for k in range(1, FIELDS):
            total = total + smix_ref[c : c + 1, k : k + 1] * fields[k]
        other = imix_ref[c : c + 1, 0:1] * received[0]
        for k in range(1, FIELDS):
            other = other + imix_ref[c : c + 1, k : k + 1] * received[k]
        value = scale * (total + other)
        for half in range(2):
            turned[half, pl.ds(c, ROWS, stride=FIELDS), :] = half_of(value, half)
    for half in range(2):
        out_ref[:, half * LANES : (half + 1) * LANES] = turned[half].astype(bf16)


def write_strips(fields, at, odd, chip_ref, outer_ref):
    lane = lax.broadcasted_iota(jnp.int32, (ROWS, LANES), 1)
    groups = [fields[3:7], [fields[7]] + fields[0:3]]
    for p, group in enumerate(groups):
        first = group[0][0]
        last = pltpu.roll(group[0][1], STRIP, 1)
        for j in range(1, 4):
            here = lane >= STRIP * j
            first = jnp.where(here, pltpu.roll(group[j][0], STRIP * j, 1), first)
            moved = group[j][1] if j == 3 else pltpu.roll(group[j][1], STRIP * (j + 1), 1)
            last = jnp.where(here, moved, last)
        chip_ref[at + p] = jnp.where(odd, first, last)
        outer_ref[at + p] = jnp.where(odd, last, first)


def export_kernel(
    smix_hbm, imix_hbm, fields_hbm, received_hbm, land_hbm, out_ref,
    smix_ref, imix_ref, fields_ref, received_ref, land_ref, turned, sems,
):
    pairs = (
        (fields_hbm, fields_ref), (received_hbm, received_ref), (land_hbm, land_ref),
        (smix_hbm, smix_ref), (imix_hbm, imix_ref),
    )
    copies = [pltpu.make_async_copy(source, dest, sems.at[k]) for k, (source, dest) in enumerate(pairs)]
    for copy in copies:
        copy.start()
    for copy in copies:
        copy.wait()
    fields = [fields_ref[c] for c in range(FIELDS)]
    received = [received_ref[c] for c in range(FIELDS)]
    write_export(fields, received, land_ref[...].astype(f32), smix_ref, imix_ref, turned, out_ref)


def export(fields, received, land, smix, imix):
    return pl.pallas_call(
        export_kernel,
        out_shape=shaped((TURNED, COLS), bf16),
        in_specs=[HBM] * 5,
        out_specs=VMEM,
        scratch_shapes=[
            pltpu.VMEM((FIELDS, FIELDS), f32),
            pltpu.VMEM((FIELDS, FIELDS), f32),
            pltpu.VMEM((FIELDS, ROWS, COLS), f32),
            pltpu.VMEM((FIELDS, ROWS, COLS), f32),
            pltpu.VMEM((ROWS, COLS), jnp.int32),
            pltpu.VMEM((2, TURNED, LANES), f32),
            pltpu.SemaphoreType.DMA((5,)),
        ],
        compiler_params=params(56),
        name="export",
    )(smix, imix, fields, received, land)


def split_to(ref, at, low_at, value):
    high = value.astype(bf16)
    ref[at] = high
    ref[low_at] = (value - high.astype(f32)).astype(bf16)


def write_main(ref, tracer_at, wave_at, wave_low_at, fields_ref):
    for half in range(2):
        cols = slice(half * LANES, (half + 1) * LANES)
        for i in range(TRACERS):
            ref[tracer_at + 2 * i + half] = fields_ref[WAVES + i, :, cols].astype(bf16)
        for i in range(WAVES):
            split_to(ref, wave_at + 2 * i + half, wave_low_at + 2 * i + half, fields_ref[i, :, cols])


def pack_kernel(opposite_ref, fields_ref, index_ref, config_ref, mixes_ref, near_ref):
    del index_ref, config_ref, mixes_ref
    write_main(near_ref, 0, A_WAVE, A_WAVE + 6, fields_ref)
    for half in range(2):
        for i in range(TURNED // 16):
            near_ref[A_EXPORT + half * 8 + i] = opposite_ref[16 * i : 16 * i + 16, half * LANES : (half + 1) * LANES]


def pack(opposite, fields, index, config, mixes):
    return pl.pallas_call(
        pack_kernel,
        out_shape=shaped((A_PLANES, ROWS, LANES), bf16),
        in_specs=[VMEM] * 2 + [HBM] * 3,
        out_specs=VMEM,
        compiler_params=params(),
        name="pack",
    )(opposite, fields, index, config, mixes)


def pack_forcing_kernel(
    config_ref, forcing_ref, outer_ref, chip_ref, state_c_ref, state_i_ref,
    out_c_ref, out_i_ref, far_ref, left_ref, right_ref,
):
    odd = spread(config_ref, GY_ODD, ROWS) > 0.5
    for p in range(4):
        left_ref[p] = jnp.where(odd, chip_ref[p], outer_ref[p])
        right_ref[p] = jnp.where(odd, outer_ref[p], chip_ref[p])
    for ref, behind in ((out_c_ref, state_i_ref), (out_i_ref, state_c_ref)):
        write_main(ref, 0, B_WAVE + 2, B_WAVE + 10, forcing_ref)
        for k, strips in enumerate((left_ref, right_ref)):
            ref[10 + k] = strips[0].astype(bf16)
            split_to(ref, B_WAVE + k, B_WAVE + 8 + k, strips[1])
            ref[B_STRIP_T + k] = strips[2].astype(bf16)
            split_to(ref, B_STRIP_W + k, B_STRIP_W + 2 + k, strips[3])
        for p in range(6):
            ref[B_BEHIND + p] = behind[A_WAVE + p]
    for p in range(8):
        far_ref[p] = out_c_ref[B_WAVE + p]
    for p in range(2):
        far_ref[C_STRIP_W + p] = out_c_ref[B_STRIP_W + p]


def pack_forcing(config, forcing, outer, chip, state_c, state_i):
    payload, strips = shaped((B_PLANES, ROWS, LANES), bf16), shaped((4, ROWS, LANES))
    return pl.pallas_call(
        pack_forcing_kernel,
        out_shape=(payload, payload, shaped((C_PLANES, ROWS, LANES), bf16), strips, strips),
        in_specs=[VMEM] * 6,
        out_specs=(VMEM,) * 5,
        compiler_params=params(),
        name="pack_forcing",
    )(config, forcing, outer, chip, state_c, state_i)


def stage_kernel(weight_ref, near_c_ref, near_i_ref, out_ref):
    del near_c_ref, near_i_ref
    out_ref[...] = weight_ref[...]


def stage(weight, near_c, near_i):
    return pl.pallas_call(
        stage_kernel,
        out_shape=shaped(weight.shape, weight.dtype),
        in_specs=[VMEM, HBM, HBM],
        out_specs=VMEM,
        compiler_params=params(),
        name="stage_weights",
    )(weight, near_c, near_i)


def remap_kernel(
    index_hbm, far_c_ref, near_c_ref, opposite_ref, near_i_ref, far_i_ref, weight_ref, land_ref, fields_ref,
    forcing_ref, chip_ref, outer_ref, import_ref, table, turned, index_ref, sem,
):
    copy = pltpu.make_async_copy(index_hbm, index_ref, sem)
    copy.start()
    half_count = 5 * ROWS * 2
    windows = [far_c_ref, near_c_ref, opposite_ref, near_i_ref, far_i_ref]
    for w, ref in enumerate(windows):
        for half in range(2):
            for i in range(TURNED // 16):
                if w in (1, 3):
                    chunk = ref[A_EXPORT + half * 8 + i]
                else:
                    chunk = ref[16 * i : 16 * i + 16, half * LANES : (half + 1) * LANES]
                chunk = chunk.astype(f32)
                for sub in range(2):
                    part = chunk[sub * 8 : sub * 8 + 8]
                    at = (w * ROWS + i * 2 + sub) * 2 + half
                    table[at] = part
                    table[half_count + at] = pltpu.roll(part, 64, 1)
    lane8 = lax.broadcasted_iota(jnp.int32, (8, LANES), 1)
    low_half = lane8 < 64
    ones = jnp.ones((8, LANES), f32)
    copy.wait()
    for x in range(ROWS):
        pieces = []
        for seg in range(4):
            at = (x * 4 + seg) * 2
            pieces.append(jnp.where(low_half, table[index_ref[at]], table[index_ref[at + 1]]))
        picked = jnp.concatenate(pieces + [ones], axis=0).astype(bf16)
        product = lax.dot_general(
            picked, weight_ref[x], (((1,), (1,)), ((), ())), preferred_element_type=f32
        )
        for half in range(2):
            cols = half_of(product, half)
            summed = jnp.where(low_half, cols[16 * half : 16 * half + 8], cols[16 * half + 8 : 16 * half + 16])
            turned[half, x * 8 : x * 8 + 8, :] = summed / cols[32:40]
    wet = land_ref[...].astype(f32)
    forcing = []
    for c in range(FIELDS):
        parts = []
        for half in range(2):
            value = turned[half, pl.ds(c, ROWS, stride=FIELDS), :]
            import_ref[c, :, half * LANES : (half + 1) * LANES] = value
            part = COUPLING * half_of(wet, half) * value
            forcing_ref[c, :, half * LANES : (half + 1) * LANES] = part
            parts.append(part)
        forcing.append(parts)
    state = [[half_of(fields_ref[c], half) for half in range(2)] for c in range(FIELDS)]
    odd = index_ref[TURNED] == 1
    write_strips(forcing, 0, odd, chip_ref, outer_ref)
    write_strips(state, 2, odd, chip_ref, outer_ref)


def remap(index, windows, weight, land, fields):
    strips = shaped((4, ROWS, LANES))
    return pl.pallas_call(
        remap_kernel,
        out_shape=(shaped((FIELDS, ROWS, COLS)), strips, strips, shaped((FIELDS, ROWS, COLS))),
        in_specs=[HBM] + [VMEM] * 8,
        out_specs=(VMEM,) * 4,
        scratch_shapes=[
            pltpu.VMEM((2 * 5 * ROWS * 2, FIELDS, LANES), f32),
            pltpu.VMEM((2, TURNED, LANES), f32),
            pltpu.SMEM((2 * TURNED,), jnp.int32),
            pltpu.SemaphoreType.DMA,
        ],
        compiler_params=params(),
        name="remap",
    )(index, *windows, weight, land, fields)


def sides(left, right, j):
    lane = lax.broadcasted_iota(jnp.int32, (ROWS, LANES), 1)
    if j:
        right = pltpu.roll(right, LANES - STRIP * j, 1)
    if j != 3:
        left = pltpu.roll(left, 96 - STRIP * j, 1)
    return jnp.where(lane < STRIP, right, jnp.where(lane >= 96, left, 0.0))


def place_field(dest, start, parts):
    for j, part in enumerate(parts):
        dest[j, start : start + ROWS, :] = part


def joined(ref, at, low_at):
    return ref[at].astype(f32) + ref[low_at].astype(f32)


def inside_tile(config_ref, first_row, count, j, shift=0):
    shape = (count, LANES)
    row = (lax.broadcasted_iota(jnp.int32, shape, 0) + first_row).astype(f32) + spread(config_ref, ROW0, count)
    col = lax.broadcasted_iota(jnp.int32, shape, 1) + j * LANES
    if j == 2:
        col = jnp.where(col >= 3 * LANES - STRIP, col - 3 * LANES, col)
    col = (col + shift).astype(f32) + spread(config_ref, COL0, count)
    ok = (row >= 0.0) & (row < spread(config_ref, ROW_END, count))
    ok = ok & (col >= 0.0) & (col < spread(config_ref, COL_END, count))
    return jnp.where(ok, 1.0, 0.0)


def westward(parts, lane, by=1):
    moved = [pltpu.roll(part, by, 1) for part in parts]
    return [jnp.where(lane < by, moved[j - 1], moved[j]) for j in range(3)]


def eastward(parts, lane, by=1):
    moved = [pltpu.roll(part, LANES - by, 1) for part in parts]
    return [jnp.where(lane >= LANES - by, moved[(j + 1) % 3], moved[j]) for j in range(3)]


def own_parts(fields_ref, left_ref, right_ref, at, i):
    p, j = (0, i - WAVES) if WAVES <= i < FIELDS - 1 else (1, (i + 1) % FIELDS)
    return [
        fields_ref[i, :, :LANES], fields_ref[i, :, LANES:], sides(left_ref[at + p], right_ref[at + p], j),
    ]


def tracer_parts(ref, strip_ref, strip_at, wave_strip_at, i):
    at = strip_at if i < 4 else wave_strip_at
    beside = sides(strip_ref[at].astype(f32), strip_ref[at + 1].astype(f32), i % 4)
    return [ref[2 * i].astype(f32), ref[2 * i + 1].astype(f32), beside]


def wave_main(ref, at, i, low=None):
    planes = [2 * i, 2 * i + 1]
    return [ref[at + p].astype(f32) if low is None else joined(ref, at + p, at + low + p) for p in planes]


def wave_strip(ref, at, i, low=None):
    left, right = [ref[at + k].astype(f32) if low is None else joined(ref, at + k, at + low + k) for k in range(2)]
    return [sides(left, right, i + 1)]


def tracer_kernel(
    last, config_ref, near_c_ref, forcing_ref, left_ref, right_ref, near_i_ref,
    state_c_ref, fields_ref, state_i_ref, *refs
):
    if last:
        received_ref, received_out, *refs = refs
        received_out[...] = received_ref[...]
    out_ref, wave_state, wave_forcing, wave_coef, state, forcing, coef = refs
    after = spread(config_ref, AFTER_NEAR, ROWS) > 0.5
    for i in range(TRACERS):
        pushed, parts = [], []
        for near, main in ((near_c_ref, state_c_ref), (near_i_ref, state_i_ref)):
            pushed.append(tracer_parts(near, near, 10, B_WAVE, i))
            parts.append(tracer_parts(main, near, B_STRIP_T, B_STRIP_W, i))
        place_field(forcing.at[i], 0, chosen(after, pushed[1], pushed[0]))
        place_field(forcing.at[i], ROWS, own_parts(forcing_ref, left_ref, right_ref, 0, WAVES + i))
        place_field(forcing.at[i], 2 * ROWS, chosen(after, pushed[0], pushed[1]))
        place_field(state.at[0, i], PAD, chosen(after, parts[1], parts[0]))
        place_field(state.at[0, i], PAD + ROWS, own_parts(fields_ref, left_ref, right_ref, 2, WAVES + i))
        place_field(state.at[0, i], PAD + 2 * ROWS, chosen(after, parts[0], parts[1]))
    for i in range(WAVES):
        pushed, parts = [], []
        for near, main in ((near_c_ref, state_c_ref), (near_i_ref, state_i_ref)):
            pushed.append(wave_main(near, B_WAVE + 2, i, 8) + wave_strip(near, B_WAVE, i, 8))
            parts.append(wave_main(main, A_WAVE, i, 6) + wave_strip(near, B_STRIP_W, i, 2))
        place_field(wave_forcing.at[i], ROWS, own_parts(forcing_ref, left_ref, right_ref, 0, i))
        place_field(wave_state.at[i], ROWS, own_parts(fields_ref, left_ref, right_ref, 2, i))
        for k, slot in ((1, 0), (0, 2)):
            place_field(wave_forcing.at[i], slot * ROWS, chosen(after, pushed[k], pushed[1 - k]))
            place_field(wave_state.at[i], slot * ROWS, chosen(after, parts[k], parts[1 - k]))
    half_a = 0.5 * config_ref[:, WAVE_SPEED : WAVE_SPEED + 1]
    half_b = 0.5 * config_ref[:, WAVE_SPEED + 1 : WAVE_SPEED + 2]
    first_row, rows = -2 * ROWS, 5 * ROWS
    for j in range(3):
        wave_coef[0, j] = inside_tile(config_ref, first_row, rows, j) * half_a
        wave_coef[1, j] = inside_tile(config_ref, first_row + 1, rows, j) * half_b
        wave_coef[2, j] = inside_tile(config_ref, first_row - 1, rows, j) * half_b
        wave_coef[3, j] = inside_tile(config_ref, first_row, rows, j, 1) * half_b
        wave_coef[4, j] = inside_tile(config_ref, first_row, rows, j, -1) * half_b
    height = 3 * ROWS
    for k in range(2):
        for i in range(TRACERS):
            for j in range(3):
                state[k, i, j, 0:PAD, :] = jnp.zeros((PAD, LANES), f32)
                state[k, i, j, PAD + height : height + 2 * PAD, :] = jnp.zeros((PAD, LANES), f32)
    for j in range(3):
        coef[j] = inside_tile(config_ref, -ROWS, height, j) * DIFFUSION

    lane = lax.broadcasted_iota(jnp.int32, (8, LANES), 1)
    keep = [(1.0 - spread(config_ref, WAVES + c)) - 4.0 * DIFFUSION for c in range(TRACERS)]

    def step(source, dest, first, count):
        for t in range(first, first + count):
            at = PAD + 8 * t
            here = slice(8 * t, 8 * t + 8)
            for c in range(TRACERS):
                mid = [state[source, c, j, at : at + 8, :] for j in range(3)]
                west = westward(mid, lane)
                east = eastward(mid, lane)
                for j in range(3):
                    above = state[source, c, j, at + 1 : at + 9, :]
                    below = state[source, c, j, at - 1 : at + 7, :]
                    around = (above + below) + (east[j] + west[j])
                    state[dest, c, j, at : at + 8, :] = (
                        keep[c] * mid[j] + forcing[c, j, here, :]
                    ) + coef[j, here, :] * around

    def pair_of_steps(first, count):
        def run(_, carry):
            step(0, 1, first, count)
            step(1, 0, first, count)
            return carry
        return run

    lax.fori_loop(0, SUBSTEPS // 4, pair_of_steps(0, 6), 0)
    lax.fori_loop(0, SUBSTEPS // 4, pair_of_steps(1, 4), 0)
    for i in range(TRACERS):
        for half in range(2):
            out_ref[i, :, half * LANES : (half + 1) * LANES] = state[0, i, half, PAD + ROWS : PAD + 2 * ROWS, :]


def tracer_steps(last, config, operands):
    inner = shaped((WAVES, 3, 3 * ROWS, LANES))
    outs = [shaped((TRACERS, ROWS, COLS)), inner, inner, shaped((5, 3, 5 * ROWS, LANES))]
    if last:
        outs = [shaped((FIELDS, ROWS, COLS))] + outs
    return pl.pallas_call(
        lambda *refs: tracer_kernel(last, *refs),
        out_shape=tuple(outs),
        in_specs=[VMEM] * (1 + len(operands)),
        out_specs=(VMEM,) * len(outs),
        scratch_shapes=[
            pltpu.VMEM((2, TRACERS, 3, 3 * ROWS + 2 * PAD, LANES), f32),
            pltpu.VMEM((TRACERS, 3, 3 * ROWS, LANES), f32),
            pltpu.VMEM((3, 3 * ROWS, LANES), f32),
        ],
        compiler_params=params(),
        cost_estimate=pl.CostEstimate(flops=10_000_000, bytes_accessed=4_000_000, transcendentals=0),
        name="tracer_steps",
    )(config, *operands)


def wave_kernel(last, config_ref, *refs):
    if not last:
        mixes_ref, *refs = refs
        smix_ref, imix_ref = mixes_ref.at[pl.ds(0, FIELDS)], mixes_ref.at[pl.ds(FIELDS, FIELDS)]
    first, near_c, near_i, second, tracers_ref, inner_state, inner_forcing, coef, *refs = refs
    far_c, far_i = (first, second) if last else (second, first)
    if last:
        out_ref, state, forcing, push = refs
    else:
        received_ref, land_ref, out_ref, export_ref, state, forcing, push, turned = refs
    height = 5 * ROWS
    tiles = height // 8

    after = spread(config_ref, AFTER_NEAR, ROWS) > 0.5
    after_far = spread(config_ref, AFTER_FAR, ROWS) > 0.5
    for i in range(WAVES):
        for j in range(3):
            for ref, inner in ((state, inner_state), (forcing, inner_forcing)):
                ref[i, j, PAD + ROWS : PAD + 4 * ROWS, :] = inner[i, j]
                ref[i, j, 0:PAD, :] = jnp.zeros((PAD, LANES), f32)
                ref[i, j, PAD + height : height + 2 * PAD, :] = jnp.zeros((PAD, LANES), f32)
        behind = [wave_main(near, B_BEHIND, i) for near in (near_c, near_i)]
        far_pushed = [wave_main(far, 2, i) + wave_strip(far, 0, i) for far in (far_c, far_i)]
        far_strip = [wave_strip(far, C_STRIP_W, i) for far in (far_c, far_i)]
        for k, slot in ((1, 0), (0, 4)):
            place_field(forcing.at[i], PAD + slot * ROWS, chosen(after_far, far_pushed[k], far_pushed[1 - k]))
            main = chosen(after, behind[k], behind[1 - k])
            strip = chosen(after_far, far_strip[k], far_strip[1 - k])
            place_field(state.at[i], PAD + slot * ROWS, main + strip)
    half_b = 0.5 * config_ref[:, WAVE_SPEED + 1 : WAVE_SPEED + 2]

    lane = lax.broadcasted_iota(jnp.int32, (8, LANES), 1)
    keep = [1.0 - spread(config_ref, c) for c in range(WAVES)]

    def load(ref, i, t, by=0):
        at = PAD + 8 * t + by
        return [ref[i, j, at : at + 8, :] for j in range(3)]

    def along(ref, i, t):
        ahead, behind = load(ref, i, t, 1), load(ref, i, t, -1)
        return [ahead[j] - behind[j] for j in range(3)]

    def across(parts):
        ahead, behind = eastward(parts, lane), westward(parts, lane)
        return [ahead[j] - behind[j] for j in range(3)]

    h = [load(state, 0, t) for t in range(tiles)]
    du = [along(state, 1, t) for t in range(tiles)]
    dv = [across(load(state, 2, t)) for t in range(tiles)]
    for t in range(tiles):
        at = PAD + 8 * t
        push_u, push_v = along(forcing, 1, t), across(load(forcing, 2, t))
        for j in range(3):
            push[0, j, 8 * t : 8 * t + 8, :] = push_u[j]
            push[1, j, 8 * t : 8 * t + 8, :] = push_v[j]
    own = (4, 5)
    sum_u = {t: [jnp.zeros((8, LANES), f32)] * 2 for t in (3, 4, 5, 6)}
    sum_v = {t: [jnp.zeros((8, LANES), f32)] * 3 for t in own}
    for step in range(SUBSTEPS):
        first = step // STEPS_PER_PHASE
        final = step == SUBSTEPS - 1
        span = range(first, tiles - first)
        for t in span:
            here = slice(8 * t, 8 * t + 8)
            lift = load(forcing, 0, t)
            for j in range(3):
                h[t][j] = (keep[0] * h[t][j] + lift[j]) - coef[0, j, here, :] * (du[t][j] + dv[t][j])
                if not final:
                    state[0, j, PAD + 8 * t : PAD + 8 * t + 8, :] = h[t][j]
        for t in sum_u:
            sum_u[t] = [keep[1] * sum_u[t][j] + h[t][j] for j in range(2)]
        for t in own:
            sum_v[t] = [keep[2] * sum_v[t][j] + h[t][j] for j in range(3)]
        if final:
            break
        for t in span:
            here = slice(8 * t, 8 * t + 8)
            east, west = eastward(h[t], lane, 2), westward(h[t], lane, 2)
            up, down = load(state, 0, t, 2), load(state, 0, t, -2)
            for j in range(3):
                mid = h[t][j]
                du[t][j] = (keep[1] * du[t][j] + push[0, j, here, :]) - (
                    coef[1, j, here, :] * (up[j] - mid) - coef[2, j, here, :] * (mid - down[j])
                )
                dv[t][j] = (keep[2] * dv[t][j] + push[1, j, here, :]) - (
                    coef[3, j, here, :] * (east[j] - mid) - coef[4, j, here, :] * (mid - west[j])
                )

    def decays(c):
        power, total = c, 1.0 + 0.0 * c
        for _ in range(SUBSTEPS - 1):
            total = total + power
            power = power * c
        return power, total

    for t in sum_u:
        for j in range(2):
            state[0, j, PAD + 8 * t : PAD + 8 * t + 8, :] = sum_u[t][j]
    power_u, total_u = decays(keep[1])
    power_v, total_v = decays(keep[2])
    for j in range(2):
        inside = inside_tile(config_ref, 0, ROWS, j) * half_b
        for t in own:
            at = PAD + 8 * t
            rows = slice(8 * (t - 4), 8 * (t - 4) + 8)
            factor = inside[rows]
            slope_u = state[0, j, at + 1 : at + 9, :] - state[0, j, at - 1 : at + 7, :]
            slope_v = across(sum_v[t])[j]
            new_u = power_u * state[1, j, at : at + 8, :] + total_u * forcing[1, j, at : at + 8, :] - factor * slope_u
            new_v = power_v * state[2, j, at : at + 8, :] + total_v * forcing[2, j, at : at + 8, :] - factor * slope_v
            cols = slice(j * LANES, (j + 1) * LANES)
            out_ref[0, rows, cols] = h[t][j]
            out_ref[1, rows, cols] = new_u
            out_ref[2, rows, cols] = new_v
    for i in range(TRACERS):
        out_ref[WAVES + i] = tracers_ref[i]
    if not last:
        fields = [out_ref[c] for c in range(FIELDS)]
        received = [received_ref[c] for c in range(FIELDS)]
        write_export(fields, received, land_ref[...].astype(f32), smix_ref, imix_ref, turned, export_ref)


def wave_steps(last, config, mixes, operands):
    state = shaped((FIELDS, ROWS, COLS))
    scratch = [
        pltpu.VMEM((WAVES, 3, 5 * ROWS + 2 * PAD, LANES), f32),
        pltpu.VMEM((WAVES, 3, 5 * ROWS + 2 * PAD, LANES), f32),
        pltpu.VMEM((2, 3, 5 * ROWS, LANES), f32),
    ]
    if not last:
        scratch.append(pltpu.VMEM((2, TURNED, LANES), f32))
    return pl.pallas_call(
        lambda *refs: wave_kernel(last, *refs),
        out_shape=state if last else (state, shaped((TURNED, COLS), bf16)),
        in_specs=[VMEM] * (1 + len(mixes) + len(operands)),
        out_specs=VMEM if last else (VMEM,) * 2,
        scratch_shapes=scratch,
        compiler_params=params(),
        name="wave_steps_last" if last else "wave_steps",
    )(config, *mixes, *operands)


def exchanged(block, axis, distance, phase):
    count = lax.axis_size(axis)
    route = []
    for low in range(count - distance):
        if (low // distance) % 2 == phase:
            route += [(low, low + distance), (low + distance, low)]
    return lax.ppermute(block, axis, route)


def local(
    section_state, prev_import, land_mask, state_mix, import_mix, damping, wave_speed,
    remap_owner, remap_slot, remap_weight,
):
    smix = state_mix[0]
    imix = import_mix[0]
    gx = lax.axis_index("gx")
    gy = lax.axis_index("gy")
    side_near = 1 - 2 * (gx % 2)
    side_far = 1 - 2 * ((gx // 2) % 2)
    place = jnp.stack([
        gx * ROWS, gy * COLS, lax.axis_size("gx") * ROWS, lax.axis_size("gy") * COLS,
        gx % 2, (gx // 2) % 2, gy % 2,
    ])
    config = jnp.concatenate([damping[0], wave_speed[0], place.astype(f32)])[None]
    owner = remap_owner[0].reshape(-1)
    slot = remap_slot[0].reshape(-1)
    away = owner - gx
    window = 2 + away * jnp.where(away % 2 == 1, side_near, side_far)
    entry = (window * ROWS + slot // 4) * 2 + (slot % 4) // 2
    second = lax.iota(jnp.int32, owner.shape[0]) % 2
    index = entry + ((slot % 2) ^ second) * (5 * ROWS * 2)
    index = jnp.concatenate([index, jnp.full((TURNED,), gy % 2, jnp.int32)])
    weight = remap_weight[0].reshape(ROWS, COLS, 128)
    mixes = jnp.concatenate([smix, imix], axis=0)

    fields, land = section_state[0], land_mask[0]
    exported = export(fields, prev_import[0], land, smix, imix)
    for interval in range(ITERS):
        last = interval == ITERS - 1
        opposite = lax.ppermute(exported, "sec", [(0, 1), (1, 0)])
        near = pack(opposite, fields, index, config, mixes)
        state_c = exchanged(near, "gx", 1, 1)
        state_i = exchanged(near, "gx", 1, 0)
        export_c = exchanged(opposite, "gx", 2, 1)
        export_i = exchanged(opposite, "gx", 2, 0)
        if interval == 0:
            weight = stage(weight, state_c, state_i)
        forcing, to_chip, to_outer, received = remap(
            index, (export_c, state_c, opposite, state_i, export_i), weight, land, fields
        )
        outer = exchanged(to_outer, "gy", 1, 1)
        chip = exchanged(to_chip, "gy", 1, 0)
        out_c, out_i, outer, left, right = pack_forcing(config, forcing, outer, chip, state_c, state_i)
        near_c = exchanged(out_c, "gx", 1, 1)
        near_i = exchanged(out_i, "gx", 1, 0)
        far_c = exchanged(outer, "gx", 2, 1)
        far_i = exchanged(outer, "gx", 2, 0)
        own = (forcing, left, right)
        state = (state_c, fields, state_i)
        operands = (near_c, *own, near_i, *state)
        if last:
            received, *prepared = tracer_steps(last, config, operands + (received,))
        else:
            prepared = tracer_steps(last, config, operands)
        operands = (far_c, near_c, near_i, far_i) if last else (far_i, near_c, near_i, far_c)
        operands += tuple(prepared)
        if last:
            fields = wave_steps(last, config, (), operands)
        else:
            operands += (received, land)
            fields, exported = wave_steps(last, config, (mixes,), operands)
    return (fields[None], received[None])


def solution(mesh):
    in_specs = (
        P("sec", None, "gx", "gy"),
        P("sec", None, "gx", "gy"),
        P("sec", "gx", "gy"),
        P("sec", None, None),
        P("sec", None, None),
        P("sec", None),
        P("sec", None),
        P("sec", "gx", "gy", None),
        P("sec", "gx", "gy", None),
        P("sec", "gx", "gy", None, None),
    )
    out_specs = (P("sec", None, "gx", "gy"), P("sec", None, "gx", "gy"))
    return jax.shard_map(local, mesh=mesh, in_specs=in_specs, out_specs=out_specs, check_vma=False)
```

```python
import jax
import jax.numpy as jnp
from jax import lax
from jax.experimental import pallas as pl
from jax.experimental.pallas import tpu as pltpu
from jax.sharding import PartitionSpec as P

SUBSTEPS = 16
ITERS = 2
DIFFUSION = 0.1
COUPLING = 0.2

FIELDS = 8
WAVES = 3
TRACERS = 5
ROWS = 16
COLS = 256
LANES = 128
TURNED = ROWS * FIELDS
STRIP = 32
STEPS_PER_PHASE = 4

A_WAVE = 10
A_EXPORT = 22
A_PLANES = 38
B_WAVE = 12
B_STRIP_T = 20
B_STRIP_W = 22
B_BEHIND = 26
B_PLANES = 32
C_STRIP_W = 8
C_PLANES = 10

PAD = 8
WAVE_SPEED = 8
ROW0, COL0, ROW_END, COL_END, AFTER_NEAR, AFTER_FAR, GY_ODD = range(10, 17)
SMEM = pl.BlockSpec(memory_space=pltpu.SMEM)
VMEM = pl.BlockSpec(memory_space=pltpu.VMEM)
HBM = pl.BlockSpec(memory_space=pl.ANY)

f32 = jnp.float32
bf16 = jnp.bfloat16


def params(mib=24):
    return pltpu.CompilerParams(vmem_limit_bytes=mib * 1024 * 1024)


def shaped(shape, dtype=f32):
    return jax.ShapeDtypeStruct(shape, dtype)


def spread(config_ref, k, rows=8):
    return jnp.broadcast_to(config_ref[:, k : k + 1], (rows, LANES))


def chosen(flag, ones, others):
    return [jnp.where(flag, one, other) for one, other in zip(ones, others)]


def half_of(value, half):
    return value[:, half * LANES : (half + 1) * LANES]


def write_export(fields, received, wet, smix_ref, imix_ref, turned, out_ref):
    scale = wet * jnp.sqrt(1.0 + fields[1] * fields[1] + fields[2] * fields[2])
    for c in range(FIELDS):
        total = smix_ref[c : c + 1, 0:1] * fields[0]
        for k in range(1, FIELDS):
            total = total + smix_ref[c : c + 1, k : k + 1] * fields[k]
        other = imix_ref[c : c + 1, 0:1] * received[0]
        for k in range(1, FIELDS):
            other = other + imix_ref[c : c + 1, k : k + 1] * received[k]
        value = scale * (total + other)
        for half in range(2):
            turned[half, pl.ds(c, ROWS, stride=FIELDS), :] = half_of(value, half)
    for half in range(2):
        out_ref[:, half * LANES : (half + 1) * LANES] = turned[half].astype(bf16)


def write_strips(fields, at, odd, chip_ref, outer_ref):
    lane = lax.broadcasted_iota(jnp.int32, (ROWS, LANES), 1)
    groups = [fields[3:7], [fields[7]] + fields[0:3]]
    for p, group in enumerate(groups):
        first = group[0][0]
        last = pltpu.roll(group[0][1], STRIP, 1)
        for j in range(1, 4):
            here = lane >= STRIP * j
            first = jnp.where(here, pltpu.roll(group[j][0], STRIP * j, 1), first)
            moved = group[j][1] if j == 3 else pltpu.roll(group[j][1], STRIP * (j + 1), 1)
            last = jnp.where(here, moved, last)
        chip_ref[at + p] = jnp.where(odd, first, last)
        outer_ref[at + p] = jnp.where(odd, last, first)


def export_kernel(
    smix_hbm, imix_hbm, fields_hbm, received_hbm, land_hbm, out_ref,
    smix_ref, imix_ref, fields_ref, received_ref, land_ref, turned, sems,
):
    pairs = (
        (fields_hbm, fields_ref), (received_hbm, received_ref), (land_hbm, land_ref),
        (smix_hbm, smix_ref), (imix_hbm, imix_ref),
    )
    copies = [pltpu.make_async_copy(source, dest, sems.at[k]) for k, (source, dest) in enumerate(pairs)]
    for copy in copies:
        copy.start()
    for copy in copies:
        copy.wait()
    fields = [fields_ref[c] for c in range(FIELDS)]
    received = [received_ref[c] for c in range(FIELDS)]
    write_export(fields, received, land_ref[...].astype(f32), smix_ref, imix_ref, turned, out_ref)


def export(fields, received, land, smix, imix):
    return pl.pallas_call(
        export_kernel,
        out_shape=shaped((TURNED, COLS), bf16),
        in_specs=[HBM] * 5,
        out_specs=VMEM,
        scratch_shapes=[
            pltpu.VMEM((FIELDS, FIELDS), f32),
            pltpu.VMEM((FIELDS, FIELDS), f32),
            pltpu.VMEM((FIELDS, ROWS, COLS), f32),
            pltpu.VMEM((FIELDS, ROWS, COLS), f32),
            pltpu.VMEM((ROWS, COLS), jnp.int32),
            pltpu.VMEM((2, TURNED, LANES), f32),
            pltpu.SemaphoreType.DMA((5,)),
        ],
        compiler_params=params(56),
        name="export",
    )(smix, imix, fields, received, land)


def split_to(ref, at, low_at, value):
    high = value.astype(bf16)
    ref[at] = high
    ref[low_at] = (value - high.astype(f32)).astype(bf16)


def write_main(ref, tracer_at, wave_at, fields_ref, low=None):
    for half in range(2):
        cols = slice(half * LANES, (half + 1) * LANES)
        for i in range(TRACERS):
            ref[tracer_at + 2 * i + half] = fields_ref[WAVES + i, :, cols].astype(bf16)
        for i in range(WAVES):
            at = wave_at + 2 * i + half
            if low is None:
                ref[at] = fields_ref[i, :, cols].astype(bf16)
            else:
                split_to(ref, at, at + low, fields_ref[i, :, cols])


def pack_kernel(opposite_ref, fields_ref, index_ref, config_ref, mixes_ref, near_ref):
    del index_ref, config_ref, mixes_ref
    write_main(near_ref, 0, A_WAVE, fields_ref, 6)
    for half in range(2):
        for i in range(TURNED // 16):
            near_ref[A_EXPORT + half * 8 + i] = opposite_ref[16 * i : 16 * i + 16, half * LANES : (half + 1) * LANES]


def pack(opposite, fields, index, config, mixes):
    return pl.pallas_call(
        pack_kernel,
        out_shape=shaped((A_PLANES, ROWS, LANES), bf16),
        in_specs=[VMEM] * 2 + [HBM] * 3,
        out_specs=VMEM,
        compiler_params=params(),
        name="pack",
    )(opposite, fields, index, config, mixes)


def pack_forcing_kernel(
    config_ref, forcing_ref, outer_ref, chip_ref, state_c_ref, state_i_ref,
    out_c_ref, out_i_ref, far_ref, left_ref, right_ref,
):
    odd = spread(config_ref, GY_ODD, ROWS) > 0.5
    for p in range(4):
        left_ref[p] = jnp.where(odd, chip_ref[p], outer_ref[p])
        right_ref[p] = jnp.where(odd, outer_ref[p], chip_ref[p])
    for ref, behind in ((out_c_ref, state_i_ref), (out_i_ref, state_c_ref)):
        write_main(ref, 0, B_WAVE + 2, forcing_ref)
        for k, strips in enumerate((left_ref, right_ref)):
            ref[10 + k] = strips[0].astype(bf16)
            ref[B_WAVE + k] = strips[1].astype(bf16)
            ref[B_STRIP_T + k] = strips[2].astype(bf16)
            split_to(ref, B_STRIP_W + k, B_STRIP_W + 2 + k, strips[3])
        for p in range(6):
            ref[B_BEHIND + p] = behind[A_WAVE + p]
    for p in range(8):
        far_ref[p] = out_c_ref[B_WAVE + p]
    for p in range(2):
        far_ref[C_STRIP_W + p] = out_c_ref[B_STRIP_W + p]


def pack_forcing(config, forcing, outer, chip, state_c, state_i):
    payload, strips = shaped((B_PLANES, ROWS, LANES), bf16), shaped((4, ROWS, LANES))
    return pl.pallas_call(
        pack_forcing_kernel,
        out_shape=(payload, payload, shaped((C_PLANES, ROWS, LANES), bf16), strips, strips),
        in_specs=[VMEM] * 6,
        out_specs=(VMEM,) * 5,
        compiler_params=params(),
        name="pack_forcing",
    )(config, forcing, outer, chip, state_c, state_i)


def stage_kernel(weight_ref, near_c_ref, near_i_ref, out_ref):
    del near_c_ref, near_i_ref
    out_ref[...] = weight_ref[...]


def stage(weight, near_c, near_i):
    return pl.pallas_call(
        stage_kernel,
        out_shape=shaped(weight.shape, weight.dtype),
        in_specs=[VMEM, HBM, HBM],
        out_specs=VMEM,
        compiler_params=params(),
        name="stage_weights",
    )(weight, near_c, near_i)


def remap_kernel(
    index_hbm, far_c_ref, near_c_ref, opposite_ref, near_i_ref, far_i_ref, weight_ref, land_ref, fields_ref,
    forcing_ref, chip_ref, outer_ref, import_ref, table, turned, index_ref, sem,
):
    copy = pltpu.make_async_copy(index_hbm, index_ref, sem)
    copy.start()
    half_count = 5 * ROWS * 2
    windows = [far_c_ref, near_c_ref, opposite_ref, near_i_ref, far_i_ref]
    for w, ref in enumerate(windows):
        for half in range(2):
            for i in range(TURNED // 16):
                if w in (1, 3):
                    chunk = ref[A_EXPORT + half * 8 + i]
                else:
                    chunk = ref[16 * i : 16 * i + 16, half * LANES : (half + 1) * LANES]
                chunk = chunk.astype(f32)
                for sub in range(2):
                    part = chunk[sub * 8 : sub * 8 + 8]
                    at = (w * ROWS + i * 2 + sub) * 2 + half
                    table[at] = part
                    table[half_count + at] = pltpu.roll(part, 64, 1)
    lane8 = lax.broadcasted_iota(jnp.int32, (8, LANES), 1)
    low_half = lane8 < 64
    ones = jnp.ones((8, LANES), f32)
    copy.wait()
    for x in range(ROWS):
        pieces = []
        for seg in range(4):
            at = (x * 4 + seg) * 2
            pieces.append(jnp.where(low_half, table[index_ref[at]], table[index_ref[at + 1]]))
        picked = jnp.concatenate(pieces + [ones], axis=0).astype(bf16)
        product = lax.dot_general(
            picked, weight_ref[x], (((1,), (1,)), ((), ())), preferred_element_type=f32
        )
        for half in range(2):
            cols = half_of(product, half)
            summed = jnp.where(low_half, cols[16 * half : 16 * half + 8], cols[16 * half + 8 : 16 * half + 16])
            turned[half, x * 8 : x * 8 + 8, :] = summed / cols[32:40]
    wet = land_ref[...].astype(f32)
    forcing = []
    for c in range(FIELDS):
        parts = []
        for half in range(2):
            value = turned[half, pl.ds(c, ROWS, stride=FIELDS), :]
            import_ref[c, :, half * LANES : (half + 1) * LANES] = value
            part = COUPLING * half_of(wet, half) * value
            forcing_ref[c, :, half * LANES : (half + 1) * LANES] = part
            parts.append(part)
        forcing.append(parts)
    state = [[half_of(fields_ref[c], half) for half in range(2)] for c in range(FIELDS)]
    odd = index_ref[TURNED] == 1
    write_strips(forcing, 0, odd, chip_ref, outer_ref)
    write_strips(state, 2, odd, chip_ref, outer_ref)


def remap(index, windows, weight, land, fields):
    strips = shaped((4, ROWS, LANES))
    return pl.pallas_call(
        remap_kernel,
        out_shape=(shaped((FIELDS, ROWS, COLS)), strips, strips, shaped((FIELDS, ROWS, COLS))),
        in_specs=[HBM] + [VMEM] * 8,
        out_specs=(VMEM,) * 4,
        scratch_shapes=[
            pltpu.VMEM((2 * 5 * ROWS * 2, FIELDS, LANES), f32),
            pltpu.VMEM((2, TURNED, LANES), f32),
            pltpu.SMEM((2 * TURNED,), jnp.int32),
            pltpu.SemaphoreType.DMA,
        ],
        compiler_params=params(),
        name="remap",
    )(index, *windows, weight, land, fields)


def sides(left, right, j):
    lane = lax.broadcasted_iota(jnp.int32, (ROWS, LANES), 1)
    if j:
        right = pltpu.roll(right, LANES - STRIP * j, 1)
    if j != 3:
        left = pltpu.roll(left, 96 - STRIP * j, 1)
    return jnp.where(lane < STRIP, right, jnp.where(lane >= 96, left, 0.0))


def place_field(dest, start, parts):
    for j, part in enumerate(parts):
        dest[j, start : start + ROWS, :] = part


def joined(ref, at, low_at):
    return ref[at].astype(f32) + ref[low_at].astype(f32)


def inside_tile(config_ref, first_row, count, j, shift=0):
    shape = (count, LANES)
    row = (lax.broadcasted_iota(jnp.int32, shape, 0) + first_row).astype(f32) + spread(config_ref, ROW0, count)
    col = lax.broadcasted_iota(jnp.int32, shape, 1) + j * LANES
    if j == 2:
        col = jnp.where(col >= 3 * LANES - STRIP, col - 3 * LANES, col)
    col = (col + shift).astype(f32) + spread(config_ref, COL0, count)
    ok = (row >= 0.0) & (row < spread(config_ref, ROW_END, count))
    ok = ok & (col >= 0.0) & (col < spread(config_ref, COL_END, count))
    return jnp.where(ok, 1.0, 0.0)


def westward(parts, lane, by=1):
    moved = [pltpu.roll(part, by, 1) for part in parts]
    return [jnp.where(lane < by, moved[j - 1], moved[j]) for j in range(3)]


def eastward(parts, lane, by=1):
    moved = [pltpu.roll(part, LANES - by, 1) for part in parts]
    return [jnp.where(lane >= LANES - by, moved[(j + 1) % 3], moved[j]) for j in range(3)]


def own_parts(fields_ref, left_ref, right_ref, at, i):
    p, j = (0, i - WAVES) if WAVES <= i < FIELDS - 1 else (1, (i + 1) % FIELDS)
    return [
        fields_ref[i, :, :LANES], fields_ref[i, :, LANES:], sides(left_ref[at + p], right_ref[at + p], j),
    ]


def tracer_parts(ref, strip_ref, strip_at, wave_strip_at, i):
    at = strip_at if i < 4 else wave_strip_at
    beside = sides(strip_ref[at].astype(f32), strip_ref[at + 1].astype(f32), i % 4)
    return [ref[2 * i].astype(f32), ref[2 * i + 1].astype(f32), beside]


def wave_main(ref, at, i, low=None):
    planes = [2 * i, 2 * i + 1]
    return [ref[at + p].astype(f32) if low is None else joined(ref, at + p, at + low + p) for p in planes]


def wave_strip(ref, at, i, low=None):
    left, right = [ref[at + k].astype(f32) if low is None else joined(ref, at + k, at + low + k) for k in range(2)]
    return [sides(left, right, i + 1)]


def tracer_kernel(
    last, config_ref, near_c_ref, forcing_ref, left_ref, right_ref, near_i_ref,
    state_c_ref, fields_ref, state_i_ref, *refs
):
    if last:
        received_ref, received_out, *refs = refs
        received_out[...] = received_ref[...]
    out_ref, wave_state, wave_forcing, wave_coef, state, forcing, coef = refs
    after = spread(config_ref, AFTER_NEAR, ROWS) > 0.5
    for i in range(TRACERS):
        pushed, parts = [], []
        for near, main in ((near_c_ref, state_c_ref), (near_i_ref, state_i_ref)):
            pushed.append(tracer_parts(near, near, 10, B_WAVE, i))
            parts.append(tracer_parts(main, near, B_STRIP_T, B_STRIP_W, i))
        place_field(forcing.at[i], 0, chosen(after, pushed[1], pushed[0]))
        place_field(forcing.at[i], ROWS, own_parts(forcing_ref, left_ref, right_ref, 0, WAVES + i))
        place_field(forcing.at[i], 2 * ROWS, chosen(after, pushed[0], pushed[1]))
        place_field(state.at[0, i], PAD, chosen(after, parts[1], parts[0]))
        place_field(state.at[0, i], PAD + ROWS, own_parts(fields_ref, left_ref, right_ref, 2, WAVES + i))
        place_field(state.at[0, i], PAD + 2 * ROWS, chosen(after, parts[0], parts[1]))
    for i in range(WAVES):
        pushed, parts = [], []
        for near, main in ((near_c_ref, state_c_ref), (near_i_ref, state_i_ref)):
            pushed.append(wave_main(near, B_WAVE + 2, i) + wave_strip(near, B_WAVE, i))
            parts.append(wave_main(main, A_WAVE, i, 6) + wave_strip(near, B_STRIP_W, i, 2))
        place_field(wave_forcing.at[i], ROWS, own_parts(forcing_ref, left_ref, right_ref, 0, i))
        place_field(wave_state.at[i], ROWS, own_parts(fields_ref, left_ref, right_ref, 2, i))
        for k, slot in ((1, 0), (0, 2)):
            place_field(wave_forcing.at[i], slot * ROWS, chosen(after, pushed[k], pushed[1 - k]))
            place_field(wave_state.at[i], slot * ROWS, chosen(after, parts[k], parts[1 - k]))
    half_a = 0.5 * config_ref[:, WAVE_SPEED : WAVE_SPEED + 1]
    half_b = 0.5 * config_ref[:, WAVE_SPEED + 1 : WAVE_SPEED + 2]
    first_row, rows = -2 * ROWS, 5 * ROWS
    for j in range(3):
        wave_coef[0, j] = inside_tile(config_ref, first_row, rows, j) * half_a
        wave_coef[1, j] = inside_tile(config_ref, first_row + 1, rows, j) * half_b
        wave_coef[2, j] = inside_tile(config_ref, first_row - 1, rows, j) * half_b
        wave_coef[3, j] = inside_tile(config_ref, first_row, rows, j, 1) * half_b
        wave_coef[4, j] = inside_tile(config_ref, first_row, rows, j, -1) * half_b
    height = 3 * ROWS
    for k in range(2):
        for i in range(TRACERS):
            for j in range(3):
                state[k, i, j, 0:PAD, :] = jnp.zeros((PAD, LANES), f32)
                state[k, i, j, PAD + height : height + 2 * PAD, :] = jnp.zeros((PAD, LANES), f32)
    for j in range(3):
        coef[j] = inside_tile(config_ref, -ROWS, height, j) * DIFFUSION

    lane = lax.broadcasted_iota(jnp.int32, (8, LANES), 1)
    keep = [(1.0 - spread(config_ref, WAVES + c)) - 4.0 * DIFFUSION for c in range(TRACERS)]

    def step(source, dest, first, count):
        for t in range(first, first + count):
            at = PAD + 8 * t
            here = slice(8 * t, 8 * t + 8)
            for c in range(TRACERS):
                mid = [state[source, c, j, at : at + 8, :] for j in range(3)]
                west = westward(mid, lane)
                east = eastward(mid, lane)
                for j in range(3):
                    above = state[source, c, j, at + 1 : at + 9, :]
                    below = state[source, c, j, at - 1 : at + 7, :]
                    around = (above + below) + (east[j] + west[j])
                    state[dest, c, j, at : at + 8, :] = (
                        keep[c] * mid[j] + forcing[c, j, here, :]
                    ) + coef[j, here, :] * around

    def pair_of_steps(first, count):
        def run(_, carry):
            step(0, 1, first, count)
            step(1, 0, first, count)
            return carry
        return run

    lax.fori_loop(0, SUBSTEPS // 4, pair_of_steps(0, 6), 0)
    lax.fori_loop(0, SUBSTEPS // 4, pair_of_steps(1, 4), 0)
    for i in range(TRACERS):
        for half in range(2):
            out_ref[i, :, half * LANES : (half + 1) * LANES] = state[0, i, half, PAD + ROWS : PAD + 2 * ROWS, :]


def tracer_steps(last, config, operands):
    inner = shaped((WAVES, 3, 3 * ROWS, LANES))
    outs = [shaped((TRACERS, ROWS, COLS)), inner, inner, shaped((5, 3, 5 * ROWS, LANES))]
    if last:
        outs = [shaped((FIELDS, ROWS, COLS))] + outs
    return pl.pallas_call(
        lambda *refs: tracer_kernel(last, *refs),
        out_shape=tuple(outs),
        in_specs=[VMEM] * (1 + len(operands)),
        out_specs=(VMEM,) * len(outs),
        scratch_shapes=[
            pltpu.VMEM((2, TRACERS, 3, 3 * ROWS + 2 * PAD, LANES), f32),
            pltpu.VMEM((TRACERS, 3, 3 * ROWS, LANES), f32),
            pltpu.VMEM((3, 3 * ROWS, LANES), f32),
        ],
        compiler_params=params(),
        cost_estimate=pl.CostEstimate(flops=10_000_000, bytes_accessed=4_000_000, transcendentals=0),
        name="tracer_steps",
    )(config, *operands)


def wave_kernel(last, config_ref, *refs):
    if not last:
        mixes_ref, *refs = refs
        smix_ref, imix_ref = mixes_ref.at[pl.ds(0, FIELDS)], mixes_ref.at[pl.ds(FIELDS, FIELDS)]
    first, near_c, near_i, second, tracers_ref, inner_state, inner_forcing, coef, *refs = refs
    far_c, far_i = (first, second) if last else (second, first)
    if last:
        out_ref, state, forcing, push = refs
    else:
        received_ref, land_ref, out_ref, export_ref, state, forcing, push, turned = refs
    height = 5 * ROWS
    tiles = height // 8

    after = spread(config_ref, AFTER_NEAR, ROWS) > 0.5
    after_far = spread(config_ref, AFTER_FAR, ROWS) > 0.5
    for i in range(WAVES):
        for j in range(3):
            for ref, inner in ((state, inner_state), (forcing, inner_forcing)):
                ref[i, j, PAD + ROWS : PAD + 4 * ROWS, :] = inner[i, j]
                ref[i, j, 0:PAD, :] = jnp.zeros((PAD, LANES), f32)
                ref[i, j, PAD + height : height + 2 * PAD, :] = jnp.zeros((PAD, LANES), f32)
        behind = [wave_main(near, B_BEHIND, i) for near in (near_c, near_i)]
        far_pushed = [wave_main(far, 2, i) + wave_strip(far, 0, i) for far in (far_c, far_i)]
        far_strip = [wave_strip(far, C_STRIP_W, i) for far in (far_c, far_i)]
        for k, slot in ((1, 0), (0, 4)):
            place_field(forcing.at[i], PAD + slot * ROWS, chosen(after_far, far_pushed[k], far_pushed[1 - k]))
            main = chosen(after, behind[k], behind[1 - k])
            strip = chosen(after_far, far_strip[k], far_strip[1 - k])
            place_field(state.at[i], PAD + slot * ROWS, main + strip)
    half_b = 0.5 * config_ref[:, WAVE_SPEED + 1 : WAVE_SPEED + 2]

    lane = lax.broadcasted_iota(jnp.int32, (8, LANES), 1)
    keep = [1.0 - spread(config_ref, c) for c in range(WAVES)]

    def load(ref, i, t, by=0):
        at = PAD + 8 * t + by
        return [ref[i, j, at : at + 8, :] for j in range(3)]

    def along(ref, i, t):
        ahead, behind = load(ref, i, t, 1), load(ref, i, t, -1)
        return [ahead[j] - behind[j] for j in range(3)]

    def across(parts):
        ahead, behind = eastward(parts, lane), westward(parts, lane)
        return [ahead[j] - behind[j] for j in range(3)]

    h = [load(state, 0, t) for t in range(tiles)]
    du = [along(state, 1, t) for t in range(tiles)]
    dv = [across(load(state, 2, t)) for t in range(tiles)]
    for t in range(tiles):
        at = PAD + 8 * t
        push_u, push_v = along(forcing, 1, t), across(load(forcing, 2, t))
        for j in range(3):
            push[0, j, 8 * t : 8 * t + 8, :] = push_u[j]
            push[1, j, 8 * t : 8 * t + 8, :] = push_v[j]
    own = (4, 5)
    sum_u = {t: [jnp.zeros((8, LANES), f32)] * 2 for t in (3, 4, 5, 6)}
    sum_v = {t: [jnp.zeros((8, LANES), f32)] * 3 for t in own}
    for step in range(SUBSTEPS):
        first = step // STEPS_PER_PHASE
        final = step == SUBSTEPS - 1
        span = range(first, tiles - first)
        for t in span:
            here = slice(8 * t, 8 * t + 8)
            lift = load(forcing, 0, t)
            for j in range(3):
                h[t][j] = (keep[0] * h[t][j] + lift[j]) - coef[0, j, here, :] * (du[t][j] + dv[t][j])
                if not final:
                    state[0, j, PAD + 8 * t : PAD + 8 * t + 8, :] = h[t][j]
        for t in sum_u:
            sum_u[t] = [keep[1] * sum_u[t][j] + h[t][j] for j in range(2)]
        for t in own:
            sum_v[t] = [keep[2] * sum_v[t][j] + h[t][j] for j in range(3)]
        if final:
            break
        for t in span:
            here = slice(8 * t, 8 * t + 8)
            east, west = eastward(h[t], lane, 2), westward(h[t], lane, 2)
            up, down = load(state, 0, t, 2), load(state, 0, t, -2)
            for j in range(3):
                mid = h[t][j]
                du[t][j] = (keep[1] * du[t][j] + push[0, j, here, :]) - (
                    coef[1, j, here, :] * (up[j] - mid) - coef[2, j, here, :] * (mid - down[j])
                )
                dv[t][j] = (keep[2] * dv[t][j] + push[1, j, here, :]) - (
                    coef[3, j, here, :] * (east[j] - mid) - coef[4, j, here, :] * (mid - west[j])
                )

    def decays(c):
        power, total = c, 1.0 + 0.0 * c
        for _ in range(SUBSTEPS - 1):
            total = total + power
            power = power * c
        return power, total

    for t in sum_u:
        for j in range(2):
            state[0, j, PAD + 8 * t : PAD + 8 * t + 8, :] = sum_u[t][j]
    power_u, total_u = decays(keep[1])
    power_v, total_v = decays(keep[2])
    for j in range(2):
        inside = inside_tile(config_ref, 0, ROWS, j) * half_b
        for t in own:
            at = PAD + 8 * t
            rows = slice(8 * (t - 4), 8 * (t - 4) + 8)
            factor = inside[rows]
            slope_u = state[0, j, at + 1 : at + 9, :] - state[0, j, at - 1 : at + 7, :]
            slope_v = across(sum_v[t])[j]
            new_u = power_u * state[1, j, at : at + 8, :] + total_u * forcing[1, j, at : at + 8, :] - factor * slope_u
            new_v = power_v * state[2, j, at : at + 8, :] + total_v * forcing[2, j, at : at + 8, :] - factor * slope_v
            cols = slice(j * LANES, (j + 1) * LANES)
            out_ref[0, rows, cols] = h[t][j]
            out_ref[1, rows, cols] = new_u
            out_ref[2, rows, cols] = new_v
    for i in range(TRACERS):
        out_ref[WAVES + i] = tracers_ref[i]
    if not last:
        fields = [out_ref[c] for c in range(FIELDS)]
        received = [received_ref[c] for c in range(FIELDS)]
        write_export(fields, received, land_ref[...].astype(f32), smix_ref, imix_ref, turned, export_ref)


def wave_steps(last, config, mixes, operands):
    state = shaped((FIELDS, ROWS, COLS))
    scratch = [
        pltpu.VMEM((WAVES, 3, 5 * ROWS + 2 * PAD, LANES), f32),
        pltpu.VMEM((WAVES, 3, 5 * ROWS + 2 * PAD, LANES), f32),
        pltpu.VMEM((2, 3, 5 * ROWS, LANES), f32),
    ]
    if not last:
        scratch.append(pltpu.VMEM((2, TURNED, LANES), f32))
    return pl.pallas_call(
        lambda *refs: wave_kernel(last, *refs),
        out_shape=state if last else (state, shaped((TURNED, COLS), bf16)),
        in_specs=[VMEM] * (1 + len(mixes) + len(operands)),
        out_specs=VMEM if last else (VMEM,) * 2,
        scratch_shapes=scratch,
        compiler_params=params(),
        name="wave_steps_last" if last else "wave_steps",
    )(config, *mixes, *operands)


def exchanged(block, axis, distance, phase):
    count = lax.axis_size(axis)
    route = []
    for low in range(count - distance):
        if (low // distance) % 2 == phase:
            route += [(low, low + distance), (low + distance, low)]
    return lax.ppermute(block, axis, route)


def local(
    section_state, prev_import, land_mask, state_mix, import_mix, damping, wave_speed,
    remap_owner, remap_slot, remap_weight,
):
    smix = state_mix[0]
    imix = import_mix[0]
    gx = lax.axis_index("gx")
    gy = lax.axis_index("gy")
    side_near = 1 - 2 * (gx % 2)
    side_far = 1 - 2 * ((gx // 2) % 2)
    place = jnp.stack([
        gx * ROWS, gy * COLS, lax.axis_size("gx") * ROWS, lax.axis_size("gy") * COLS,
        gx % 2, (gx // 2) % 2, gy % 2,
    ])
    config = jnp.concatenate([damping[0], wave_speed[0], place.astype(f32)])[None]
    owner = remap_owner[0].reshape(-1)
    slot = remap_slot[0].reshape(-1)
    away = owner - gx
    window = 2 + away * jnp.where(away % 2 == 1, side_near, side_far)
    entry = (window * ROWS + slot // 4) * 2 + (slot % 4) // 2
    second = lax.iota(jnp.int32, owner.shape[0]) % 2
    index = entry + ((slot % 2) ^ second) * (5 * ROWS * 2)
    index = jnp.concatenate([index, jnp.full((TURNED,), gy % 2, jnp.int32)])
    weight = remap_weight[0].reshape(ROWS, COLS, 128)
    mixes = jnp.concatenate([smix, imix], axis=0)

    fields, land = section_state[0], land_mask[0]
    exported = export(fields, prev_import[0], land, smix, imix)
    for interval in range(ITERS):
        last = interval == ITERS - 1
        opposite = lax.ppermute(exported, "sec", [(0, 1), (1, 0)])
        near = pack(opposite, fields, index, config, mixes)
        state_c = exchanged(near, "gx", 1, 1)
        state_i = exchanged(near, "gx", 1, 0)
        export_c = exchanged(opposite, "gx", 2, 1)
        export_i = exchanged(opposite, "gx", 2, 0)
        if interval == 0:
            weight = stage(weight, state_c, state_i)
        forcing, to_chip, to_outer, received = remap(
            index, (export_c, state_c, opposite, state_i, export_i), weight, land, fields
        )
        outer = exchanged(to_outer, "gy", 1, 1)
        chip = exchanged(to_chip, "gy", 1, 0)
        out_c, out_i, outer, left, right = pack_forcing(config, forcing, outer, chip, state_c, state_i)
        near_c = exchanged(out_c, "gx", 1, 1)
        near_i = exchanged(out_i, "gx", 1, 0)
        far_c = exchanged(outer, "gx", 2, 1)
        far_i = exchanged(outer, "gx", 2, 0)
        own = (forcing, left, right)
        state = (state_c, fields, state_i)
        operands = (near_c, *own, near_i, *state)
        if last:
            received, *prepared = tracer_steps(last, config, operands + (received,))
        else:
            prepared = tracer_steps(last, config, operands)
        operands = (far_c, near_c, near_i, far_i) if last else (far_i, near_c, near_i, far_c)
        operands += tuple(prepared)
        if last:
            fields = wave_steps(last, config, (), operands)
        else:
            operands += (received, land)
            fields, exported = wave_steps(last, config, (mixes,), operands)
    return (fields[None], received[None])


def solution(mesh):
    in_specs = (
        P("sec", None, "gx", "gy"),
        P("sec", None, "gx", "gy"),
        P("sec", "gx", "gy"),
        P("sec", None, None),
        P("sec", None, None),
        P("sec", None),
        P("sec", None),
        P("sec", "gx", "gy", None),
        P("sec", "gx", "gy", None),
        P("sec", "gx", "gy", None, None),
    )
    out_specs = (P("sec", None, "gx", "gy"), P("sec", None, "gx", "gy"))
    return jax.shard_map(local, mesh=mesh, in_specs=in_specs, out_specs=out_specs, check_vma=False)
```
